256 devices in a mesh: gx: 32 (over x, z), gy: 8 (over y, core).
Axes of the slice: x: 4, y: 4, z: 8, core: 2. Of those that a mesh axis runs over, the one named last changes fastest.
Arguments:
- history: bfloat16 [1, 20, 128, 64, 512], P(None, None, 'gx', 'gy'), may hold values from -6 to 6
- w_point: float32 [20, 20], replicated, may hold values from -1.25 to 1.25
- offset: float32 [20], replicated, may hold values from -3 to 3
- spectral_weight: float32 [2, 20, 20, 128, 24, 24], P(None, None, None, 'gx', 'gy'), may hold values from -3 to 3
- cotangent: bfloat16 [1, 20, 128, 64, 512], P(None, None, 'gx', 'gy'), may hold values from -6 to 6
Outputs:
- activated: bfloat16 [1, 20, 128, 64, 512], P(None, None, 'gx', 'gy')
- grad_history: bfloat16 [1, 20, 128, 64, 512], P(None, None, 'gx', 'gy')
- grad_spectral: float32 [2, 20, 20, 128, 24, 24], P(None, None, None, 'gx', 'gy')
- grad_point: float32 [20, 20], replicated
- grad_offset: float32 [20], replicated
The draws below stay inside these ranges and needn't reach their ends.
All inputs are finite; a program needn't handle non-finite values.
Results may differ from the reference program's by a relative error of at most 0.0011.
Values sent between devices are 32-bit elements; how exact they have to be, the bound alone decides.
A program may use at most 128 MiB of HBM per device.

```python
import jax
import jax.numpy as jnp
from jax import lax

C = 20
MX = 24
MY = 24
MZ = 16
MT = 8
NZ = 64
NT = 8
B = 1
NX = 128
NY = 64


def levels(own_key, dims, pieces, low, high):
    level, own = 1.0, jax.random.fold_in(own_key, 6)
    for axis_at, blocks in pieces:
        heights = jnp.exp(jax.random.uniform(jax.random.fold_in(own, axis_at), (blocks,), jnp.float32, low / len(pieces), high / len(pieces)))
        level = level * jnp.repeat(heights, dims[axis_at] // blocks).reshape([-1 if axis == axis_at else 1 for axis in range(len(dims))])
    return level


def gaussian(rng, shape, spread, reach, pieces=(), kind=jnp.bfloat16):
    values = spread * jax.random.normal(rng, shape, jnp.float32)
    if pieces:
        values = values * levels(rng, shape, pieces, -0.22, 0.18)
    return jnp.clip(values, -reach, reach).astype(kind)


def setup_inputs(seed: int = 0) -> dict:
    streams_of = jax.random.split(jax.random.key(seed), 6)
    return {
        "history": gaussian(streams_of[0], (B, C, NX, NY, NZ * NT), 1.0, 6.0, ((2, 32), (3, 8))),
        "w_point": gaussian(streams_of[1], (C, C), C ** -0.5, 1.25, (), jnp.float32),
        "offset": gaussian(streams_of[2], (C,), 0.5, 3.0, (), jnp.float32),
        "spectral_weight": gaussian(streams_of[3], (2, C, C, MZ * MT, MX, MY), 0.5, 3.0, ((3, 32), (4, 8)), jnp.float32),
        "cotangent": gaussian(streams_of[4], (B, C, NX, NY, NZ * NT), 1.0, 6.0, ((2, 32), (3, 8))),
    }


gelu_coef = 0.7978845608028654
gelu_cubic = 0.044715


def gelu_parts(inputs):
    inner = gelu_coef * (inputs + gelu_cubic * inputs * inputs * inputs)
    smooth = jnp.tanh(inner)
    result = 0.5 * inputs * (1.0 + smooth)
    slope = 0.5 * (1.0 + smooth) + 0.5 * inputs * (1.0 - smooth * smooth) * gelu_coef * (1.0 + 3.0 * gelu_cubic * inputs * inputs)
    return result, slope


def kept_freqs(length, keep):
    half = keep // 2
    return jnp.concatenate([jnp.arange(half), length - half + jnp.arange(half)]).astype(jnp.int32)


def to_modes(block):
    grid = block.reshape(B, NX, NY, NZ, NT)
    spectrum = jnp.fft.fftn(grid, axes=(1, 2, 3, 4))
    spectrum = jnp.take(spectrum, kept_freqs(NX, MX), axis=1)
    spectrum = jnp.take(spectrum, kept_freqs(NY, MY), axis=2)
    spectrum = jnp.take(spectrum, kept_freqs(NZ, MZ), axis=3)
    spectrum = jnp.take(spectrum, kept_freqs(NT, MT), axis=4)
    spectrum = jnp.transpose(spectrum, (0, 3, 4, 1, 2))
    return spectrum.reshape(B, MZ * MT, MX, MY)


def from_modes(modes):
    spectrum = jnp.transpose(modes.reshape(B, MZ, MT, MX, MY), (0, 3, 4, 1, 2))
    x_freqs = kept_freqs(NX, MX)
    y_freqs = kept_freqs(NY, MY)
    z_freqs = kept_freqs(NZ, MZ)
    t_freqs = kept_freqs(NT, MT)
    full = jnp.zeros((B, NX, NY, NZ, NT), spectrum.dtype)
    full = full.at[:, x_freqs[:, None, None, None], y_freqs[None, :, None, None], z_freqs[None, None, :, None], t_freqs[None, None, None, :]].set(spectrum)
    grid = jnp.real(jnp.fft.ifftn(full, axes=(1, 2, 3, 4)))
    return grid.reshape(B, NX, NY, NZ * NT).astype(jnp.float32)


def channel_of(array, channel):
    return lax.dynamic_index_in_dim(array, channel, 1, keepdims=False).astype(jnp.float32)


def reference(history, w_point, offset, spectral_weight, cotangent):
    channels = jnp.arange(C)
    highest = lax.Precision.HIGHEST

    def analyse_input(channel):
        return to_modes(channel_of(history, channel))

    modes = lax.map(analyse_input, channels)
    weight_complex = lax.complex(spectral_weight[0], spectral_weight[1])
    mixed = jnp.einsum('oiqkj,ibqkj->obqkj', weight_complex, modes)

    def forward_channel(channel):
        weight_row = lax.dynamic_index_in_dim(w_point, channel, 0, keepdims=False)
        local = jnp.einsum('i,bixyq->bxyq', weight_row, history.astype(jnp.float32), precision=highest)
        offset_here = lax.dynamic_index_in_dim(offset, channel, 0, keepdims=False)
        mixed_here = lax.dynamic_index_in_dim(mixed, channel, 0, keepdims=False)
        pre_gelu = local + offset_here + from_modes(mixed_here)
        result, slope = gelu_parts(pre_gelu)
        grad_pre = channel_of(cotangent, channel) * slope
        point_row = jnp.einsum('bxyq,bixyq->i', grad_pre, history.astype(jnp.float32), precision=highest)
        return result.astype(jnp.bfloat16), grad_pre, to_modes(grad_pre), jnp.sum(grad_pre), point_row

    results, grads, grad_modes, offset_sums, point_sums = lax.map(forward_channel, channels)
    activated = jnp.moveaxis(results, 0, 1)
    back_modes = jnp.einsum('oiqkj,obqkj->ibqkj', jnp.conj(weight_complex), grad_modes)

    def backward_channel(channel):
        weight_column = lax.dynamic_index_in_dim(w_point, channel, 1, keepdims=False)
        local = jnp.einsum('o,obxyq->bxyq', weight_column, grads, precision=highest)
        back_here = lax.dynamic_index_in_dim(back_modes, channel, 0, keepdims=False)
        return (local + from_modes(back_here)).astype(jnp.bfloat16)

    grad_history = jnp.moveaxis(lax.map(backward_channel, channels), 0, 1)
    cells_all = float(NX * NY * NZ * NT)
    products = jnp.einsum('obqkj,ibqkj->oiqkj', jnp.conj(grad_modes), modes) / cells_all
    grad_spectral = jnp.stack([jnp.real(products), -jnp.imag(products)]).astype(jnp.float32)
    return activated, grad_history, grad_spectral, point_sums, offset_sums
```

```python
import functools

import jax
import jax.numpy as jnp
import ml_dtypes
import numpy as np
from jax import lax
from jax.experimental import pallas as pl
from jax.experimental.pallas import tpu as pltpu
from jax.sharding import PartitionSpec as P

MESH = pl.DeviceIdType.MESH
F32 = jnp.float32
BF16 = jnp.bfloat16
C = 20
NX, NY, NZ, NT = 128, 64, 64, 8
MX, MY, MZ, MT = 24, 24, 16, 8
GX, GY = 32, 8
XC, YC = NX // GX, NY // GY
KX = MX // GY
Q = MZ * MT // GX
ROWS = C * YC
CELLS = NX * NY * NZ * NT
XPOS, ZPOS = 4, 8
gelu_coef = 0.7978845608028654
gelu_cubic = 0.044715


def kept(length, keep):
    half = keep // 2
    return np.concatenate([np.arange(half), length - half + np.arange(half)])


def halves(table):
    table = np.asarray(table, np.float64)
    hi = table.astype(np.float32).astype(ml_dtypes.bfloat16)
    lo = (table - hi.astype(np.float64)).astype(np.float32).astype(ml_dtypes.bfloat16)
    return np.stack([hi, lo])


def depth_table():
    fz, ft = kept(NZ, MZ), kept(NT, MT)
    z, t = np.arange(NZ), np.arange(NT)
    turn = (fz[:, None, None, None] * z[None, None, :, None] % NZ) / NZ + (
        ft[None, :, None, None] * t[None, None, None, :] % NT
    ) / NT
    angle = 2 * np.pi * turn.reshape(GX, 1, Q, NZ * NT)
    return np.concatenate([np.cos(angle), -np.sin(angle)], axis=1).reshape(GX * 2 * Q, NZ * NT)


def x_table():
    fx = kept(NX, MX).reshape(GY, KX)
    x = np.arange(NX).reshape(GX, XC)
    angle = 2 * np.pi * (x[:, :, None, None] * fx[None, None] % NX) / NX
    cos, sin = np.cos(angle), np.sin(angle)
    out = np.zeros((XC, GX, 2, Q, GY, 2, 4, Q))
    for q in range(Q):
        part = out[:, :, :, q, :, :, :KX, q]
        part[:, :, 0, :, 0] = cos.transpose(1, 0, 2, 3)
        part[:, :, 1, :, 0] = sin.transpose(1, 0, 2, 3)
        part[:, :, 0, :, 1] = -sin.transpose(1, 0, 2, 3)
        part[:, :, 1, :, 1] = cos.transpose(1, 0, 2, 3)
    return out.reshape(XC, GX * 2 * Q, GY * 2 * 4 * Q)


def y_table():
    fy = kept(NY, MY)
    angle = 2 * np.pi * (np.arange(NY)[:, None] * fy[None] % NY) / NY
    cos, sin = np.cos(angle), np.sin(angle)
    out = np.zeros((2, NY, 2, 128))
    out[0, :, 0, :MY] = cos
    out[1, :, 0, :MY] = sin
    out[0, :, 1, :MY] = -sin
    out[1, :, 1, :MY] = cos
    return out.reshape(2 * NY, 256)


def split(value):
    hi = value.astype(BF16)
    return hi, (value - hi.astype(F32)).astype(BF16)


def dot(a, b, dims):
    return lax.dot_general(a, b, (dims, ((), ())), preferred_element_type=F32)


NN = ((1,), (0,))
NTD = ((1,), (1,))


def dot3(a, b, dims=NN):
    return dot(a[0], b[0], dims) + (dot(a[0], b[1], dims) + dot(a[1], b[0], dims))


def exact(a, b, dims=NN):
    return lax.dot_general(
        a, b, (dims, ((), ())), precision=lax.Precision.HIGHEST, preferred_element_type=F32
    )


def swap_groups(parts):
    parts = list(parts)
    group = lax.broadcasted_iota(jnp.int32, parts[0].shape, 1) // 8
    for s in (8, 4, 2, 1):
        low = lax.rem(group // s, 2) == 0
        for i in range(16):
            if i & s:
                continue
            a, b = parts[i], parts[i + s]
            parts[i] = jnp.where(low, a, pltpu.roll(b, 8 * s, 1))
            parts[i + s] = jnp.where(low, pltpu.roll(a, 128 - 8 * s, 1), b)
    return parts


def kernel(
    hist, cot, wpt, off, w_hbm, dtab, xa, xs, ya, ys,
    act, ghist, gs_hbm, gpoint, goff,
    w_v, wp, gs_v, vb, base, gpre, sendx, recvx, sendy, recvy, modes, grads, mixed, small, smalls,
    w_sem, gs_sem, sx_sem, rx_sem, sy_sem, ry_sem, ss_sem, rs_sem,
):
    d = lax.axis_index("gx")
    e = lax.axis_index("gy")

    w_copy = pltpu.make_async_copy(w_hbm, w_v, w_sem)
    w_copy.start()

    barrier = pltpu.get_barrier_semaphore()

    def greet_x(k, carry):
        pl.semaphore_signal(
            barrier, inc=1, device_id=(lax.rem(d + k, GX), e), device_id_type=MESH
        )
        return carry

    def greet_y(k, carry):
        pl.semaphore_signal(
            barrier, inc=1, device_id=(d, lax.rem(e + k, GY)), device_id_type=MESH
        )
        return carry

    lax.fori_loop(1, GX, greet_x, 0)
    lax.fori_loop(1, GY, greet_y, 0)

    def x_copy(p, peer, slot):
        return pltpu.make_async_remote_copy(
            src_ref=sendx.at[p, peer],
            dst_ref=recvx.at[p, slot],
            send_sem=sx_sem.at[p, peer],
            recv_sem=rx_sem.at[p, slot],
            device_id=(peer, e),
            device_id_type=MESH,
        )

    def y_copy(p, peer, slot):
        return pltpu.make_async_remote_copy(
            src_ref=sendy.at[p, peer],
            dst_ref=recvy.at[p, slot],
            send_sem=sy_sem.at[p, peer],
            recv_sem=ry_sem.at[p, slot],
            device_id=(d, peer),
            device_id_type=MESH,
        )

    def start_x(p):
        def go(k, carry):
            x_copy(p, lax.rem(d + k, GX), d).start()
            return carry

        lax.fori_loop(1, GX, go, 0)
        recvx[p, d] = sendx[p, d]

    def wait_x(p):
        def go(k, carry):
            peer = lax.rem(d + GX - k, GX)
            copy = x_copy(p, peer, peer)
            copy.wait_recv()
            copy.wait_send()
            return carry

        lax.fori_loop(1, GX, go, 0)

    def start_y(p):
        def go(k, carry):
            y_copy(p, lax.rem(e + k, GY), e).start()
            return carry

        lax.fori_loop(1, GY, go, 0)
        recvy[p, e] = sendy[p, e]

    def wait_y(p):
        def go(k, carry):
            peer = lax.rem(e + GY - k, GY)
            copy = y_copy(p, peer, peer)
            copy.wait_recv()
            copy.wait_send()
            return carry

        lax.fori_loop(1, GY, go, 0)

    def depth_analyse(p, get, terms):
        for t in range(XC + 1):
            total = None
            for tab, half in terms:
                if t < XC:
                    rows = get(t, half)[0:128]
                else:
                    rows = jnp.concatenate([get(x, half)[128:ROWS] for x in range(XC)], axis=0)
                term = dot(dtab[tab], rows, NTD)
                total = term if total is None else total + term
            sendx[p, :, :, t * 128 : (t + 1) * 128] = total.reshape(GX, 8, 128)

    def x_analyse(p):
        left = recvx[p, :, :, 512:640].reshape(256, 128)
        total = None
        for x in range(XC):
            tile = recvx[p, :, :, x * 128 : (x + 1) * 128].reshape(256, 128)
            tail = left if x == 0 else pltpu.roll(left, 128 - 32 * x, 1)
            term = dot3((xa[0, x], xa[1, x]), split(jnp.concatenate([tile, tail], axis=1)))
            total = term if total is None else total + term
        sendy[p] = total.reshape(GY, 32, 256)

    def y_analyse(p, out):
        rows = []
        for t, count in ((0, 16), (1, C - 16)):
            parts = [
                recvy[p, g % GY, 16 * (g // GY) : 16 * (g // GY) + 16, t * 128 : (t + 1) * 128]
                for g in range(16)
            ]
            rows += swap_groups(parts)[:count]
        out[...] = dot3(split(jnp.concatenate(rows, axis=0)), (ya[0], ya[1]))

    def y_synthesise(p):
        cols = dot3(split(mixed[...]), (ys[0], ys[1]))
        blank = jnp.zeros((16, 128), F32)
        for t, count in ((0, 16), (1, C - 16)):
            parts = [cols[(16 * t + c) * 16 : (16 * t + c + 1) * 16] for c in range(count)]
            parts = swap_groups(parts + [blank] * (16 - count))
            for g in range(16):
                sendy[
                    p, g % GY, 16 * (g // GY) : 16 * (g // GY) + 16, t * 128 : (t + 1) * 128
                ] = parts[g]

    def x_synthesise(py, px):
        cols = split(recvy[py].reshape(256, 256))
        left = None
        for x in range(XC):
            out = dot3((xs[0, x], xs[1, x]), cols)
            sendx[px, :, :, x * 128 : (x + 1) * 128] = out[:, :128].reshape(GX, 8, 128)
            tail = out[:, 128:]
            left = tail if x == 0 else left + pltpu.roll(tail, 32 * x, 1)
        sendx[px, :, :, 512:640] = left.reshape(GX, 8, 128)

    def depth_synthesise(p, x, left):
        tile = recvx[p, :, :, x * 128 : (x + 1) * 128].reshape(256, 128).T
        cols = jnp.concatenate([tile, left[32 * x : 32 * x + 32]], axis=0)
        return dot3(split(cols), (dtab[0], dtab[1])) * (1.0 / CELLS)

    def left_of(p):
        return recvx[p, :, :, 512:640].reshape(256, 128).T

    for x in range(XC):
        vb[x] = hist[:, x].astype(F32).reshape(ROWS, 512).astype(BF16)
    depth_analyse(0, lambda x, half: vb[x], ((0, 0), (1, 0)))

    pl.semaphore_wait(barrier, GX + GY - 2)
    start_x(0)

    w_copy.wait()

    def pack(o, carry):
        for r in range(2):
            for i in range(C):
                for k in range(KX):
                    wp[r, o, i, 4 * k : 4 * k + 4, 0:MY] = w_v[r, o, i, k]
        return carry

    lax.fori_loop(0, C, pack, 0)

    spread = (
        lax.broadcasted_iota(jnp.int32, (ROWS, C), 0) // YC
        == lax.broadcasted_iota(jnp.int32, (ROWS, C), 1)
    ).astype(F32)
    same_y = lax.rem(lax.broadcasted_iota(jnp.int32, (ROWS, ROWS), 0), YC) == lax.rem(
        lax.broadcasted_iota(jnp.int32, (ROWS, ROWS), 1), YC
    )
    wide = exact(exact(spread, wpt[...]), spread, NTD)
    point = split(jnp.where(same_y, wide, 0.0))
    wide_t = exact(exact(spread, wpt[...], ((1,), (1,))), spread, NTD)
    point_t = split(jnp.where(same_y, wide_t, 0.0))
    bias = jnp.sum(spread * off[...], axis=1, keepdims=True)
    for x in range(XC):
        base[x] = dot(point[0], vb[x], NN) + dot(point[1], vb[x], NN) + bias

    wait_x(0)
    x_analyse(0)
    start_y(0)
    wait_y(0)
    y_analyse(0, modes)

    valid = (lax.broadcasted_iota(jnp.int32, (16, 128), 0) < 4 * KX) & (
        lax.broadcasted_iota(jnp.int32, (16, 128), 1) < MY
    )

    def mix(o, carry):
        real = jnp.zeros((16, 128), F32)
        imag = jnp.zeros((16, 128), F32)
        for i in range(C):
            wr, wi = wp[0, o, i], wp[1, o, i]
            mr, mi = modes[16 * i : 16 * i + 16, 0:128], modes[16 * i : 16 * i + 16, 128:256]
            real += wr * mr - wi * mi
            imag += wr * mi + wi * mr
        at = pl.ds(pl.multiple_of(o * 16, 16), 16)
        mixed[at, 0:128] = jnp.where(valid, real, 0.0)
        mixed[at, 128:256] = jnp.where(valid, imag, 0.0)
        return carry

    lax.fori_loop(0, C, mix, 0)
    y_synthesise(1)
    start_y(1)
    wait_y(1)
    x_synthesise(1, 1)
    start_x(1)
    wait_x(1)

    left = left_of(1)
    row_sum = jnp.zeros((ROWS, 1), F32)
    for x in range(XC):
        pre = depth_synthesise(1, x, left) + base[x]
        inner = gelu_coef * (pre + gelu_cubic * pre * pre * pre)
        smooth = jnp.tanh(inner)
        slope = 0.5 * (1.0 + smooth) + 0.5 * pre * (1.0 - smooth * smooth) * gelu_coef * (
            1.0 + 3.0 * gelu_cubic * pre * pre
        )
        act[:, x] = (0.5 * pre * (1.0 + smooth)).reshape(C, YC, 512).astype(BF16)
        grad = cot[:, x].astype(F32).reshape(ROWS, 512) * slope
        row_sum += jnp.sum(grad, axis=1, keepdims=True)
        hi, lo = split(grad)
        gpre[0, x] = hi
        gpre[1, x] = lo
    depth_analyse(2, lambda x, half: gpre[half, x], ((0, 0), (0, 1), (1, 0)))
    start_x(2)

    cross = jnp.zeros((ROWS, ROWS), F32)
    for x in range(XC):
        g = (gpre[0, x], gpre[1, x])
        base[x] = dot3(point_t, g)
        cross += dot(g[0], vb[x], NTD) + dot(g[1], vb[x], NTD)
    gather = (
        lax.broadcasted_iota(jnp.int32, (24, ROWS), 1) // YC
        == lax.broadcasted_iota(jnp.int32, (24, ROWS), 0)
    ).astype(F32)
    place = (
        lax.broadcasted_iota(jnp.int32, (ROWS, 128), 0) // YC
        == lax.broadcasted_iota(jnp.int32, (ROWS, 128), 1)
    ).astype(F32)
    lane = lax.broadcasted_iota(jnp.int32, (ROWS, 128), 1)
    both = exact(jnp.where(same_y, cross, 0.0), place) + jnp.where(lane == C, row_sum, 0.0)
    small[0] = exact(gather, both)

    def small_copy(s, k, peer, slot):
        return pltpu.make_async_remote_copy(
            src_ref=small.at[s],
            dst_ref=smalls.at[s, slot],
            send_sem=ss_sem.at[s, k],
            recv_sem=rs_sem.at[s, slot],
            device_id=peer,
            device_id_type=MESH,
        )

    xpos, zpos = d // ZPOS, lax.rem(d, ZPOS)
    steps = (
        (GY, e, lambda i: (d, i)),
        (XPOS, xpos, lambda i: (i * ZPOS + zpos, e)),
        (ZPOS, zpos, lambda i: (xpos * ZPOS + i, e)),
    )

    def start_small(s):
        count, me, peer_of = steps[s]
        for k in range(1, count):
            small_copy(s, k, peer_of(lax.rem(me + k, count)), me).start()
        smalls[s, me] = small[s]

    def finish_small(s):
        count, me, peer_of = steps[s]
        for k in range(1, count):
            other = lax.rem(me + count - k, count)
            copy = small_copy(s, k, peer_of(other), other)
            copy.wait_recv()
            copy.wait_send()
        total = smalls[s, 0]
        for k in range(1, count):
            total = total + smalls[s, k]
        return total

    start_small(0)
    wait_x(2)
    x_analyse(2)
    start_y(2)
    small[1] = finish_small(0)
    start_small(1)
    wait_y(2)
    y_analyse(2, grads)

    def mix_back(j, carry):
        real = jnp.zeros((16, 128), F32)
        imag = jnp.zeros((16, 128), F32)
        for o in range(C):
            wr, wi = wp[0, o, j], wp[1, o, j]
            gr, gi = grads[16 * o : 16 * o + 16, 0:128], grads[16 * o : 16 * o + 16, 128:256]
            real += wr * gr + wi * gi
            imag += wr * gi - wi * gr
        at = pl.ds(pl.multiple_of(j * 16, 16), 16)
        mixed[at, 0:128] = jnp.where(valid, real, 0.0)
        mixed[at, 128:256] = jnp.where(valid, imag, 0.0)
        return carry

    lax.fori_loop(0, C, mix_back, 0)
    y_synthesise(3)
    start_y(3)
    small[2] = finish_small(1)
    start_small(2)
    wait_y(3)
    x_synthesise(3, 3)
    start_x(3)

    def pair(o, carry):
        at = pl.ds(pl.multiple_of(o * 16, 16), 16)
        gr = grads[at, 0:128] * (1.0 / CELLS)
        gi = grads[at, 128:256] * (1.0 / CELLS)
        for j in range(C):
            mr, mi = modes[16 * j : 16 * j + 16, 0:128], modes[16 * j : 16 * j + 16, 128:256]
            real = gr * mr + gi * mi
            imag = gi * mr - gr * mi
            for k in range(KX):
                gs_v[0, o, j, k] = real[4 * k : 4 * k + 4, 0:MY]
                gs_v[1, o, j, k] = imag[4 * k : 4 * k + 4, 0:MY]
        return carry

    lax.fori_loop(0, C, pair, 0)
    gs_copy = pltpu.make_async_copy(gs_v, gs_hbm, gs_sem)
    gs_copy.start()

    total = finish_small(2)
    gpoint[...] = total[0:C, 0:C]
    column = total[0:C, C : C + 1]
    diagonal = lax.broadcasted_iota(jnp.int32, (C, C), 0) == lax.broadcasted_iota(
        jnp.int32, (C, C), 1
    )
    goff[...] = jnp.sum(jnp.where(diagonal, column, 0.0), axis=0, keepdims=True)

    wait_x(3)
    left = left_of(3)
    for x in range(XC):
        total = depth_synthesise(3, x, left) + base[x]
        ghist[:, x] = total.reshape(C, YC, 512).astype(BF16)
    gs_copy.wait()


def per_device(history, w_point, offset, spectral_weight, cotangent):
    depth = jnp.asarray(halves(depth_table()))
    xt = x_table()
    x_forward = jnp.asarray(halves(xt.transpose(0, 2, 1)))
    x_backward = jnp.asarray(halves(xt))
    yt = y_table()
    y_forward = jnp.asarray(halves(yt))
    y_backward = jnp.asarray(halves(yt.T))
    weight = jnp.transpose(spectral_weight, (0, 1, 2, 4, 3, 5))
    vmem = pl.BlockSpec(memory_space=pltpu.VMEM)
    hbm = pl.BlockSpec(memory_space=pl.ANY)
    block = (C, XC, YC, NZ * NT)
    act, ghist, gs, gpoint, goff = pl.pallas_call(
        kernel,
        out_shape=(
            jax.ShapeDtypeStruct(block, BF16),
            jax.ShapeDtypeStruct(block, BF16),
            jax.ShapeDtypeStruct((2, C, C, KX, Q, MY), F32),
            jax.ShapeDtypeStruct((C, C), F32),
            jax.ShapeDtypeStruct((1, C), F32),
        ),
        in_specs=[vmem] * 4 + [hbm] + [vmem] * 5,
        out_specs=(vmem, vmem, hbm, vmem, vmem),
        scratch_shapes=[
            pltpu.VMEM((2, C, C, KX, Q, MY), F32),
            pltpu.VMEM((2, C, C, 16, 128), F32),
            pltpu.VMEM((2, C, C, KX, Q, MY), F32),
            pltpu.VMEM((XC, ROWS, 512), BF16),
            pltpu.VMEM((XC, ROWS, 512), F32),
            pltpu.VMEM((2, XC, ROWS, 512), BF16),
            pltpu.VMEM((4, GX, 8, 640), F32),
            pltpu.VMEM((4, GX, 8, 640), F32),
            pltpu.VMEM((4, GY, 32, 256), F32),
            pltpu.VMEM((4, GY, 32, 256), F32),
            pltpu.VMEM((C * 16, 256), F32),
            pltpu.VMEM((C * 16, 256), F32),
            pltpu.VMEM((C * 16, 256), F32),
            pltpu.VMEM((3, 24, 128), F32),
            pltpu.VMEM((3, 8, 24, 128), F32),
            pltpu.SemaphoreType.DMA,
            pltpu.SemaphoreType.DMA,
            pltpu.SemaphoreType.DMA((4, GX)),
            pltpu.SemaphoreType.DMA((4, GX)),
            pltpu.SemaphoreType.DMA((4, GY)),
            pltpu.SemaphoreType.DMA((4, GY)),
            pltpu.SemaphoreType.DMA((3, 8)),
            pltpu.SemaphoreType.DMA((3, 8)),
        ],
        compiler_params=pltpu.CompilerParams(
            collective_id=0, has_side_effects=True, vmem_limit_bytes=58 * 1024 * 1024
        ),
    )(
        history[0], cotangent[0], w_point, offset.reshape(1, C), weight,
        depth, x_forward, x_backward, y_forward, y_backward,
    )
    grad_spectral = jnp.transpose(gs, (0, 1, 2, 4, 3, 5))
    return act[None], ghist[None], grad_spectral, gpoint, goff.reshape(C)


def solution(mesh):
    grid = P(None, None, "gx", "gy", None)
    modes = P(None, None, None, "gx", "gy", None)
    return jax.shard_map(
        per_device,
        mesh=mesh,
        in_specs=(grid, P(), P(), modes, grid),
        out_specs=(grid, grid, modes, P(), P()),
        check_vma=False,
    )
```

```python
import functools

import jax
import jax.numpy as jnp
import ml_dtypes
import numpy as np
from jax import lax
from jax.experimental import pallas as pl
from jax.experimental.pallas import tpu as pltpu
from jax.sharding import PartitionSpec as P

MESH = pl.DeviceIdType.MESH
F32 = jnp.float32
BF16 = jnp.bfloat16
C = 20
NX, NY, NZ, NT = 128, 64, 64, 8
MX, MY, MZ, MT = 24, 24, 16, 8
GX, GY = 32, 8
XC, YC = NX // GX, NY // GY
KX = MX // GY
Q = MZ * MT // GX
ROWS = C * YC
CELLS = NX * NY * NZ * NT
XPOS, ZPOS = 4, 8
EXTRA, STRIDE = 4, 10
gelu_coef = 0.7978845608028654
gelu_cubic = 0.044715


def kept(length, keep):
    half = keep // 2
    return np.concatenate([np.arange(half), length - half + np.arange(half)])


def halves(table):
    table = np.asarray(table, np.float64)
    hi = table.astype(np.float32).astype(ml_dtypes.bfloat16)
    lo = (table - hi.astype(np.float64)).astype(np.float32).astype(ml_dtypes.bfloat16)
    return np.stack([hi, lo])


def handled(h):
    p, s = h // 2, h % 2
    if p == 0:
        return [(NZ - 8, t) for t in ((2, 3) if s == 0 else (6, 7))]
    if p == 8:
        return [(NZ - 8, t) for t in ((0, 1) if s == 0 else (4, 5))]
    if p < 8:
        return [(p, t) for t in ((0, 3) if s == 0 else (4, 7))]
    return [(16 - p, t) for t in ((5, 6) if s == 0 else (1, 2))]


def depth_table():
    z, t = np.arange(NZ)[:, None], np.arange(NT)[None]

    def wave(kz, kt):
        return 2 * np.pi * ((z * kz % NZ) / NZ + (t * kt % NT) / NT).reshape(-1)

    rows = []
    for h in range(GX):
        angles = [wave(*mode) for mode in handled(h)]
        rows += [np.cos(a) for a in angles] + [-np.sin(a) for a in angles]
    rows += [np.cos(wave(0, 0)), np.cos(wave(0, 4))]
    for j in range(1, EXTRA):
        rows += [np.cos(wave(0, j)), -np.sin(wave(0, j))]
    return np.stack(rows + [np.zeros(NZ * NT)] * 8)


def x_tables():
    fx = kept(NX, MX).reshape(GY, KX)
    x = np.arange(NX).reshape(GX, XC).T
    angle = 2 * np.pi * (fx[:, :, None, None] * x[None, None] % NX) / NX
    cos, sin = np.cos(angle), np.sin(angle)
    main = np.zeros((GY, 2, 16, XC, GX, 2, 2))
    extra = np.zeros((2, GY, 2, 16, XC, GX, 2))
    direct = ((cos, sin), (-sin, cos))
    conj = ((cos, -sin), (-sin, -cos))
    for out in range(2):
        for k in range(KX):
            row = 6 * out + 2 * k
            for into in range(2):
                for m in range(2):
                    main[:, 0, row + m, :, :, into, m] = direct[out][into][:, k]
                    main[:, 1, row + m, :, :, into, m] = conj[out][into][:, k]
                extra[1, :, 0, row, :, :, into] = direct[out][into][:, k]
                extra[1, :, 1, row, :, :, into] = conj[out][into][:, k]
            extra[0, :, 0, row, :, :, 0] = direct[out][0][:, k]
            extra[0, :, 1, row, :, :, 1] = direct[out][0][:, k]

    def spread_rows(full):
        out = np.zeros((4,) + full.shape[:2] + (4,) + full.shape[3:])
        for g in range(4):
            out[g, :, :, :3] = full[:, :, g:12:4]
        return out

    def both(full):
        tail = spread_rows(full)
        columns = full[0, 0, 0].size
        rows = tail.transpose(0, 2, 1, *range(3, tail.ndim))
        return (
            full.reshape(256, columns),
            tail.reshape(256, columns),
            full.swapaxes(0, 1).reshape(2, GY * 16, columns),
            rows.reshape(4, 2, GY * 4, columns),
        )

    am, al, sm, sl = both(main)
    sm = np.concatenate([sm[0], sm[1], sm[1]]).T
    sl = np.concatenate([sl[:, :1], sl[:, 1:], sl[:, 1:]], axis=1).reshape(384, -1).T
    ex = [both(extra[kind]) for kind in range(2)]
    em, el = np.stack([v[0] for v in ex]), np.stack([v[1] for v in ex])
    esm = np.stack([v[2].reshape(256, 256).T for v in ex])
    esl = np.stack([v[3].reshape(256, 256).T for v in ex])
    return np.stack([am, al]), np.stack([sm, sl]), np.stack([em, el, esm, esl], axis=1)


def slot_tables():
    maps = (
        {(0, 0): 0, (0, 1): 3, (1, 0): 1, (1, 1): 2},
        {(0, 0): 3, (0, 1): 2, (1, 0): 0, (2, 1): 1},
        {(0, 0): 3, (0, 1): 2, (1, 1): 1, (2, 0): 0},
        {(0, 0): 0, (0, 1): 1, (1, 0): 2, (1, 1): 3},
        {(0, 0): 0, (1, 0): 1, (2, 0): 2, (3, 0): 3},
        {(0, 0): 0, (1, 0): 3, (2, 0): 2, (3, 0): 1},
    )
    out = np.zeros((len(maps), 64, 160))
    for kind, table in enumerate(maps):
        for (slot, m), q in table.items():
            for ri in range(2):
                for k in range(KX):
                    r = 6 * ri + 2 * k + m
                    at = 16 * ri + 4 * k + q
                    out[kind, 16 * slot + r, at] = 1
                    out[kind, 16 * slot + 12 + r // 4, 32 + 32 * (r % 4) + at] = 1
    return out


def y_table():
    fy = kept(NY, MY)
    angle = 2 * np.pi * (np.arange(NY)[:, None] * fy[None] % NY) / NY
    cos, sin = np.cos(angle), np.sin(angle)
    out = np.zeros((2, NY, 2, 128))
    out[0, :, 0, :MY] = cos
    out[1, :, 0, :MY] = sin
    out[0, :, 1, :MY] = -sin
    out[1, :, 1, :MY] = cos
    return out.reshape(2 * NY, 256)


def split(value):
    hi = value.astype(BF16)
    return hi, (value - hi.astype(F32)).astype(BF16)


def dot(a, b, dims):
    return lax.dot_general(a, b, (dims, ((), ())), preferred_element_type=F32)


NN = ((1,), (0,))
NTD = ((1,), (1,))


def dot3(a, b, dims=NN):
    return dot(a[0], b[0], dims) + (dot(a[0], b[1], dims) + dot(a[1], b[0], dims))


def exact(a, b, dims=NN):
    return lax.dot_general(
        a, b, (dims, ((), ())), precision=lax.Precision.HIGHEST, preferred_element_type=F32
    )


def swap_groups(parts):
    parts = list(parts)
    group = lax.broadcasted_iota(jnp.int32, parts[0].shape, 1) // 8
    for s in (8, 4, 2, 1):
        low = lax.rem(group // s, 2) == 0
        for i in range(16):
            if i & s:
                continue
            a, b = parts[i], parts[i + s]
            parts[i] = jnp.where(low, a, pltpu.roll(b, 8 * s, 1))
            parts[i + s] = jnp.where(low, pltpu.roll(a, 128 - 8 * s, 1), b)
    return parts


def dot2(a, b):
    return dot(a, b[0], NN) + dot(a, b[1], NN)


def kernel(
    hist, cot, wpt, off, w_hbm, dtab_h, xa_h, xs_h, xe_h, ya_h, ys_h, u_h, ut_h,
    fields, sums,
    dtab, xa, xs, xe, ya, ys, u, ut, w_v, wp, vb, base, gpre, mixed,
    sendx, recvx, sende, recve, sendr, recvr, sendy, recvy, backs, backr, exy, small, smalls,
    load_sem, sx_sem, rx_sem, se_sem, re_sem, sr_sem, rr_sem, sy_sem, ry_sem, sb_sem, rb_sem, ss_sem, rs_sem,
):
    d = lax.axis_index("gx")
    e = lax.axis_index("gy")
    modes, grads = sums.at[0:320], sums.at[320:640]
    half, side = d // 2, lax.rem(d, 2)
    is_a = (d >= 2) & (d < 16)
    is_b = d >= 18
    is_mid = (d >= 16) & (d < 18)
    is_low = d < 2
    special = lax.rem(d, STRIDE) == 0
    which = d // STRIDE
    kind = jnp.where(is_low, 4 + side, jnp.where(is_mid, 3, jnp.where(is_a, 0, 1 + side)))
    kind_e = jnp.where(d == 0, 0, 1)
    pair = GX - 2 * half
    mirror = GX + 1 - d

    loads = [
        pltpu.make_async_copy(src, dst, load_sem.at[i])
        for i, (src, dst) in enumerate((
            (dtab_h, dtab), (w_hbm, w_v), (xa_h, xa), (xs_h, xs), (ya_h, ya), (ys_h, ys),
            (u_h.at[kind], u), (ut_h.at[kind], ut),
        ))
    ]
    extra_load = pltpu.make_async_copy(xe_h.at[:, kind_e], xe, load_sem.at[len(loads)])
    for load in loads:
        load.start()

    @pl.when(special)
    def _():
        extra_load.start()

    recvy[...] = jnp.zeros_like(recvy)
    backr[...] = jnp.zeros_like(backr)

    barrier = pltpu.get_barrier_semaphore()

    def signal(x, y):
        pl.semaphore_signal(barrier, inc=1, device_id=(x, y), device_id_type=MESH)

    def over(count, body, first=0):
        def go(k, carry):
            body(k)
            return carry

        lax.fori_loop(first, count, go, 0)

    over(GX, lambda k: signal((d + k) & (GX - 1), e), 1)
    over(GY, lambda k: signal(d, (e + k) & (GY - 1)), 1)
    def remote(src, dst, send, recv, x, y):
        return pltpu.make_async_remote_copy(
            src_ref=src, dst_ref=dst, send_sem=send, recv_sem=recv,
            device_id=(x, y), device_id_type=MESH,
        )

    def x_copy(p, peer, slot):
        return remote(
            sendx.at[p, peer], recvx.at[p, slot], sx_sem.at[p, peer], rx_sem.at[p, slot], peer, e
        )

    def start_x(p):
        over(GX, lambda k: x_copy(p, (d + k) & (GX - 1), d).start(), 1)
        recvx[p, d] = sendx[p, d]

    def wait_x(p):
        def go(k):
            peer = (d + GX - k) & (GX - 1)
            copy = x_copy(p, peer, peer)
            copy.wait_recv()
            copy.wait_send()

        over(GX, go, 1)

    def e_copy(f, j, slot):
        return remote(
            sende.at[f, j], recve.at[f, slot], se_sem.at[f, j], re_sem.at[f, slot], j * STRIDE, e
        )

    def start_e(f):
        def go(j):
            @pl.when(d != j * STRIDE)
            def _():
                e_copy(f, j, d).start()

        over(EXTRA, go)

        @pl.when(special)
        def _():
            recve[f, d] = sende[f, which]

    def wait_e_sent(f):
        def go(j):
            @pl.when(d != j * STRIDE)
            def _():
                e_copy(f, j, d).wait_send()

        over(EXTRA, go)

    def wait_e(f):
        def go(k):
            peer = (d + GX - k) & (GX - 1)
            remote(
                sende.at[f, 0], recve.at[f, peer], se_sem.at[f, 0], re_sem.at[f, peer], peer, e
            ).wait_recv()

        over(GX, go, 1)

    def r_copy(f, peer, j):
        return remote(
            sendr.at[f, peer], recvr.at[f, j], sr_sem.at[f, peer], rr_sem.at[f, j], peer, e
        )

    def start_r(f):
        over(GX, lambda k: r_copy(f, (d + k) & (GX - 1), which).start(), 1)
        recvr[f, which] = sendr[f, d]

    def wait_r(f):
        def go(j):
            @pl.when(d != j * STRIDE)
            def _():
                r_copy(f, 0, j).wait_recv()

        over(EXTRA, go)

        @pl.when(special)
        def _():
            over(GX, lambda k: r_copy(f, (d + k) & (GX - 1), which).wait_send(), 1)

    others = jnp.where(is_a, 2, jnp.where(is_mid, 0, 1))
    own_part = jnp.where(is_b, 1, 0)
    other_part = jnp.where(is_a, 1, 0)
    other_slot = jnp.where(is_a, 1 + side, 1)

    def other_at(t):
        return jnp.where(is_a, pair + t, jnp.where(is_low, d + 16, mirror))

    def y_copy(f, y, part, slot, x, sem):
        return remote(
            sendy.at[f, y, part], recvy.at[f, slot, e], sy_sem.at[f, sem, y], ry_sem.at[f, slot, e], x, y
        )

    def ex_copy(f, y, part):
        return remote(
            exy.at[f, y, part], recvy.at[f, which, e], sy_sem.at[f, 3 + part, y],
            ry_sem.at[f, which, e], part, y,
        )

    def each_y(f, act_on):
        def own(k):
            y = (e + k) & (GY - 1)
            act_on(y_copy(f, y, own_part, 0, d, 0))

        @pl.when(d >= 2)
        def _():
            over(GY, own, 1)

        def other(k):
            y = (e + k) & (GY - 1)
            over(
                others,
                lambda t: act_on(y_copy(f, y, other_part, other_slot, other_at(t), 1 + t)),
            )

        over(GY, other)

    def each_ex(f, act_on):
        def go(k):
            y = (e + k) & (GY - 1)

            @pl.when((d != 0) | (k != 0))
            def _():
                act_on(ex_copy(f, y, 0))

            act_on(ex_copy(f, y, 1))

        over(GY, go)

    def start_y(f):
        each_y(f, lambda copy: copy.start())

        @pl.when(d >= 2)
        def _():
            recvy[f, 0, e] = sendy[f, e, own_part]

    def start_ex(f):
        each_ex(f, lambda copy: copy.start())

        @pl.when(d == 0)
        def _():
            recvy[f, 0, e] = exy[f, e, 0]

    def wait_y(f):
        def arrived(slot, y):
            remote(
                sendy.at[f, 0, 0], recvy.at[f, slot, y], sy_sem.at[f, 0, 0], ry_sem.at[f, slot, y], d, y
            ).wait_recv()

        @pl.when(d >= 1)
        def _():
            over(GY, lambda k: arrived(0, (e + GY - k) & (GY - 1)), 1)

        @pl.when(d == 1)
        def _():
            arrived(0, e)

        @pl.when(d == 0)
        def _():
            over(GY, lambda k: arrived(0, (e + GY - k) & (GY - 1)), 1)

        slots = jnp.where(is_low, 4, jnp.where(is_b, 3, 2))

        def rest(k):
            y = (e + GY - k) & (GY - 1)
            over(slots, lambda slot: arrived(slot, y), 1)

        over(GY, rest)
        each_y(f, lambda copy: copy.wait_send())

        @pl.when(special)
        def _():
            each_ex(f, lambda copy: copy.wait_send())

    def b_copy(f, slot, y, x, into):
        return remote(
            backs.at[f, slot, y], backr.at[f, into, e], sb_sem.at[f, slot, y], rb_sem.at[f, into, e], x, y
        )

    def each_b(f, act_on):
        def own(k):
            y = (e + k) & (GY - 1)
            act_on(b_copy(f, 0, y, d, jnp.where(is_b, 1, 0)))

        @pl.when(d >= 2)
        def _():
            over(GY, own, 1)

        def other(k):
            y = (e + k) & (GY - 1)

            @pl.when(is_a | is_mid)
            def _():
                act_on(b_copy(f, 1, y, jnp.where(is_a, mirror, d - 16), 0))

            @pl.when(is_b)
            def _():
                over(2, lambda t: act_on(b_copy(f, 1 + t, y, pair + t, 1 + side)))

            @pl.when(is_low)
            def _():
                def slot(j):
                    @pl.when((d != 0) | (j != 0) | (k != 0))
                    def _():
                        act_on(b_copy(f, j, y, j * STRIDE, 3 + side))

                over(EXTRA, slot)

        over(GY, other)

    def start_b(f):
        each_b(f, lambda copy: copy.start())

        @pl.when(d >= 2)
        def _():
            backr[f, jnp.where(is_b, 1, 0), e] = backs[f, 0, e]

        @pl.when(d == 0)
        def _():
            backr[f, 3, e] = backs[f, 0, e]

    def wait_b(f):
        def arrived(into, y):
            remote(
                backs.at[f, 0, 0], backr.at[f, into, y], sb_sem.at[f, 0, 0], rb_sem.at[f, into, y], d, y
            ).wait_recv()

        def own(k):
            arrived(jnp.where(is_b, 1, 0), (e + GY - k) & (GY - 1))

        @pl.when(d >= 2)
        def _():
            over(GY, own, 1)

        def rest(k):
            y = (e + GY - k) & (GY - 1)

            @pl.when(is_a)
            def _():
                over(3, lambda into: arrived(into, y), 1)

            @pl.when(is_b | is_low)
            def _():
                arrived(0, y)

        over(GY, rest)
        each_b(f, lambda copy: copy.wait_send())

    def wait_b_extra(f):
        def go(k):
            y = (e + GY - k) & (GY - 1)

            @pl.when((d != 0) | (k != 0))
            def _():
                remote(
                    backs.at[f, 0, 0], backr.at[f, 3, y], sb_sem.at[f, 0, 0], rb_sem.at[f, 3, y], d, y
                ).wait_recv()

            remote(
                backs.at[f, 0, 0], backr.at[f, 4, y], sb_sem.at[f, 0, 0], rb_sem.at[f, 4, y], d, y
            ).wait_recv()

        over(GY, go)

    lane128 = lax.broadcasted_iota(jnp.int32, (1, 128), 1)

    def depth_analyse(p, f, get, terms):
        for t in range(XC + 1):
            total = None
            for tab, part in terms:
                if t < XC:
                    rows = get(t, part)[0:128]
                else:
                    rows = jnp.concatenate([get(x, part)[128:ROWS] for x in range(XC)], axis=0)
                term = dot(dtab[tab], rows, NTD)
                total = term if total is None else total + term
            sendx[p, :, t] = total[0:128].reshape(GX, 4, 128)
            sende[f, :, t] = total[128:136].reshape(EXTRA, 2, 128)

    def x_analyse(tiles, tables, out):
        left = tiles[XC]
        count = left.shape[0]
        per = 256 // count
        main, tail = None, None
        for b in range(XC // per):
            xs_here = range(b * per, (b + 1) * per)
            at = slice(b * 256, (b + 1) * 256)
            cols = split(jnp.concatenate([tiles[x] for x in xs_here], axis=0))
            term = dot3((tables[0, 0, :, at], tables[1, 0, :, at]), cols)
            main = term if main is None else main + term
            cols = split(jnp.concatenate(
                [left if x == 0 else pltpu.roll(left, 128 - 32 * x, 1) for x in xs_here], axis=0
            ))
            term = dot3((tables[0, 1, :, at], tables[1, 1, :, at]), cols)
            tail = term if tail is None else tail + term
        out[...] = main.reshape(GY, 2, 16, 128)
        tail = jnp.where(lane128 < 32, tail, 0.0)
        packed = tail[0:64]
        for g in range(1, 4):
            packed = packed + pltpu.roll(tail[64 * g : 64 * g + 64], 32 * g, 1)
        out[:, :, 12:16, :] = packed.reshape(GY, 2, 4, 128)

    def analyse_main(p, f):
        x_analyse([recvx[p, :, t].reshape(128, 128) for t in range(XC + 1)], xa, sendy.at[f])

    def analyse_extra(f):
        x_analyse(
            [recve[f, :, t].reshape(64, 128) for t in range(XC + 1)], xe.at[:, 0:2], exy.at[f]
        )

    def y_analyse(f, out):
        cols = split(jnp.concatenate([recvy[f, :, y].reshape(64, 128) for y in range(GY)], axis=1))
        merged = dot2(ut[...], cols)
        rows = []
        parts = [
            merged[16 * (g // GY) : 16 * (g // GY) + 16, 128 * (g % GY) : 128 * (g % GY) + 128]
            for g in range(16)
        ]
        rows += swap_groups(parts)
        parts = []
        for g in range(16):
            at = 32 + 16 * (g // GY)
            lanes = slice(128 * (g % GY), 128 * (g % GY) + 128)
            total = merged[at : at + 16, lanes]
            for n in range(1, 4):
                total = total + pltpu.roll(merged[at + 32 * n : at + 32 * n + 16, lanes], 128 - 32 * n, 1)
            parts.append(total)
        rows += swap_groups([jnp.where(lane128 < 32, part, 0.0) for part in parts])[: C - 16]
        out[...] = dot3(split(jnp.concatenate(rows, axis=0)), (ya[0], ya[1]))

    def y_synthesise(f):
        cols = dot3(split(mixed[...]), (ys[0], ys[1]))
        blank = jnp.zeros((16, 128), F32)
        main = swap_groups([cols[16 * c : 16 * c + 16] for c in range(16)])
        tail = swap_groups(
            [cols[16 * c : 16 * c + 16] for c in range(16, C)] + [blank] * (32 - C)
        )
        stack = []
        for y in range(GY):
            rows = [main[y], main[GY + y]]
            for n in range(4):
                for g in (y, GY + y):
                    rows.append(tail[g] if n == 0 else pltpu.roll(tail[g], 32 * n, 1))
            stack.append(jnp.concatenate(rows, axis=0))
        out = dot2(u[...], split(jnp.concatenate(stack, axis=1)))
        for y in range(GY):
            backs[f, :, y] = out[:, 128 * y : 128 * y + 128].reshape(4, 16, 128)

    def x_synthesise(slots, tables, put):
        count = slots.shape[0] * GY
        rows = slots[...]
        main_cols = split(rows.reshape(count * 16, 128))
        tail = rows[:, :, 12:16, :].reshape(count * 4, 128)
        tail_cols = split(jnp.concatenate(
            [tail] + [pltpu.roll(tail, 128 - 32 * g, 1) for g in range(1, 4)], axis=0
        ))
        main = dot3((tables[0, 0], tables[1, 0]), main_cols)
        tail = dot3((tables[0, 1], tables[1, 1]), tail_cols)
        tail = jnp.where(lane128 < 32, tail, 0.0)
        per = main.shape[0] // XC
        left = None
        for x in range(XC):
            at = slice(per * x, per * x + per)
            put(x, main[at])
            part = tail[at]
            left = part if x == 0 else left + pltpu.roll(part, 32 * x, 1)
        put(XC, left)

    def synthesise_main(f, p):
        def put(t, rows):
            sendx[p, :, t] = rows.reshape(GX, 4, 128)

        x_synthesise(backr.at[f, 0:3], xs, put)

    def synthesise_extra(f):
        def put(t, rows):
            sendr[f, :, t] = rows.reshape(GX, 2, 128)

        x_synthesise(backr.at[f, 3:5], xe.at[:, 2:4], put)

    def depth_rows(p, f, t):
        tile = recvx[p, :, t].reshape(128, 128)
        extra = recvr[f, :, t].reshape(8, 128)
        rest = jnp.zeros((120, 128), F32)
        low = jnp.concatenate([extra, rest], axis=0).T
        return jnp.concatenate([tile.T, low[:, 0:16]], axis=1)

    def depth_synthesise(p, f, x, left):
        cols = jnp.concatenate([depth_rows(p, f, x), left[32 * x : 32 * x + 32]], axis=0)
        return dot3(split(cols), (dtab[0], dtab[1])) * (1.0 / CELLS)

    def send_main_then_extra(p, f):
        @pl.when(special)
        def _():
            wait_e(f)
            analyse_extra(f)
            start_ex(f)

        wait_x(p)
        analyse_main(p, f)
        start_y(f)

    def cells_back(f, p):
        @pl.when(special)
        def _():
            wait_b_extra(f)
            synthesise_extra(f)
            start_r(f)

        wait_b(f)
        synthesise_main(f, p)
        start_x(p)

    for x in range(XC):
        vb[x] = hist[:, x].astype(F32).reshape(ROWS, 512).astype(BF16)
    loads[0].wait()
    depth_analyse(0, 0, lambda x, part: vb[x], ((0, 0), (1, 0)))

    pl.semaphore_wait(barrier, GX + GY - 2)
    start_e(0)
    start_x(0)

    for load in loads[1:]:
        load.wait()

    @pl.when(special)
    def _():
        extra_load.wait()

    def pack(o):
        for r in range(2):
            for i in range(C):
                for k in range(KX):
                    wp[r, o, i, 4 * k : 4 * k + 4, 0:MY] = w_v[r, o, i, k]

    over(C, pack)

    spread = (
        lax.broadcasted_iota(jnp.int32, (ROWS, C), 0) // YC
        == lax.broadcasted_iota(jnp.int32, (ROWS, C), 1)
    ).astype(F32)
    same_y = lax.rem(lax.broadcasted_iota(jnp.int32, (ROWS, ROWS), 0), YC) == lax.rem(
        lax.broadcasted_iota(jnp.int32, (ROWS, ROWS), 1), YC
    )
    wide = exact(exact(spread, wpt[...]), spread, NTD)
    point = split(jnp.where(same_y, wide, 0.0))
    wide_t = exact(exact(spread, wpt[...], ((1,), (1,))), spread, NTD)
    point_t = split(jnp.where(same_y, wide_t, 0.0))
    bias = jnp.sum(spread * off[...], axis=1, keepdims=True)
    for x in range(XC):
        base[x] = dot(point[0], vb[x], NN) + dot(point[1], vb[x], NN) + bias

    send_main_then_extra(0, 0)
    wait_y(0)
    y_analyse(0, modes)

    valid = (lax.broadcasted_iota(jnp.int32, (16, 128), 0) < 4 * KX) & (
        lax.broadcasted_iota(jnp.int32, (16, 128), 1) < MY
    )

    def mix(o):
        real = jnp.zeros((16, 128), F32)
        imag = jnp.zeros((16, 128), F32)
        for i in range(C):
            wr, wi = wp[0, o, i], wp[1, o, i]
            mr, mi = modes[16 * i : 16 * i + 16, 0:128], modes[16 * i : 16 * i + 16, 128:256]
            real += wr * mr - wi * mi
            imag += wr * mi + wi * mr
        at = pl.ds(pl.multiple_of(o * 16, 16), 16)
        mixed[at, 0:128] = jnp.where(valid, real, 0.0)
        mixed[at, 128:256] = jnp.where(valid, imag, 0.0)

    over(C, mix)
    y_synthesise(0)
    start_b(0)
    cells_back(0, 1)
    wait_x(1)
    wait_r(0)
    wait_e_sent(0)

    left = depth_rows(1, 0, XC)
    row_sum = jnp.zeros((ROWS, 1), F32)
    for x in range(XC):
        pre = depth_synthesise(1, 0, x, left) + base[x]
        inner = gelu_coef * (pre + gelu_cubic * pre * pre * pre)
        smooth = jnp.tanh(inner)
        slope = 0.5 * (1.0 + smooth) + 0.5 * pre * (1.0 - smooth * smooth) * gelu_coef * (
            1.0 + 3.0 * gelu_cubic * pre * pre
        )
        fields[0, :, x] = (0.5 * pre * (1.0 + smooth)).reshape(C, YC, 512).astype(BF16)
        grad = cot[:, x].astype(F32).reshape(ROWS, 512) * slope
        row_sum += jnp.sum(grad, axis=1, keepdims=True)
        hi, lo = split(grad)
        gpre[0, x] = hi
        gpre[1, x] = lo
    depth_analyse(2, 1, lambda x, part: gpre[part, x], ((0, 0), (0, 1), (1, 0)))
    start_e(1)
    start_x(2)

    cross = jnp.zeros((ROWS, ROWS), F32)
    for x in range(XC):
        g = (gpre[0, x], gpre[1, x])
        base[x] = dot3(point_t, g)
        cross += dot(g[0], vb[x], NTD) + dot(g[1], vb[x], NTD)
    gather = (
        lax.broadcasted_iota(jnp.int32, (24, ROWS), 1) // YC
        == lax.broadcasted_iota(jnp.int32, (24, ROWS), 0)
    ).astype(F32)
    place = (
        lax.broadcasted_iota(jnp.int32, (ROWS, 128), 0) // YC
        == lax.broadcasted_iota(jnp.int32, (ROWS, 128), 1)
    ).astype(F32)
    lane = lax.broadcasted_iota(jnp.int32, (ROWS, 128), 1)
    both = exact(jnp.where(same_y, cross, 0.0), place) + jnp.where(lane == C, row_sum, 0.0)
    small[0] = exact(gather, both)

    def small_copy(s, k, peer, slot):
        return remote(small.at[s], smalls.at[s, slot], ss_sem.at[s, k], rs_sem.at[s, slot], *peer)

    xpos, zpos = d // ZPOS, lax.rem(d, ZPOS)
    steps = (
        (GY, e, lambda i: (d, i)),
        (XPOS, xpos, lambda i: (i * ZPOS + zpos, e)),
        (ZPOS, zpos, lambda i: (xpos * ZPOS + i, e)),
    )

    def start_small(s):
        count, me, peer_of = steps[s]
        for k in range(1, count):
            small_copy(s, k, peer_of(lax.rem(me + k, count)), me).start()
        smalls[s, me] = small[s]

    def finish_small(s):
        count, me, peer_of = steps[s]
        for k in range(1, count):
            other = lax.rem(me + count - k, count)
            copy = small_copy(s, k, peer_of(other), other)
            copy.wait_recv()
            copy.wait_send()
        total = smalls[s, 0]
        for k in range(1, count):
            total = total + smalls[s, k]
        return total

    start_small(0)
    send_main_then_extra(2, 1)
    small[1] = finish_small(0)
    start_small(1)
    wait_y(1)
    y_analyse(1, grads)

    def mix_back(j):
        real = jnp.zeros((16, 128), F32)
        imag = jnp.zeros((16, 128), F32)
        for o in range(C):
            wr, wi = wp[0, o, j], wp[1, o, j]
            gr, gi = grads[16 * o : 16 * o + 16, 0:128], grads[16 * o : 16 * o + 16, 128:256]
            real += wr * gr + wi * gi
            imag += wr * gi - wi * gr
        at = pl.ds(pl.multiple_of(j * 16, 16), 16)
        mixed[at, 0:128] = jnp.where(valid, real, 0.0)
        mixed[at, 128:256] = jnp.where(valid, imag, 0.0)

    over(C, mix_back)
    y_synthesise(1)
    start_b(1)
    small[2] = finish_small(1)
    start_small(2)
    cells_back(1, 3)

    total = finish_small(2)
    sums[640:664, 0:128] = total
    sums[640:664, 128:256] = jnp.zeros_like(total)

    wait_x(3)
    wait_r(1)
    wait_e_sent(1)
    left = depth_rows(3, 1, XC)
    for x in range(XC):
        total = depth_synthesise(3, 1, x, left) + base[x]
        fields[1, :, x] = total.reshape(C, YC, 512).astype(BF16)


GROUPS = 5


def finish(fields, sums, act, ghist, gs, gpoint, goff, gs_v, io_sem, gs_sem):
    modes, grads = sums.at[0:320], sums.at[320:640]
    copies = [
        pltpu.make_async_copy(fields.at[0], act, io_sem.at[0]),
        pltpu.make_async_copy(fields.at[1], ghist, io_sem.at[1]),
    ]
    for copy in copies:
        copy.start()
    gpoint[...] = sums[640 : 640 + C, 0:C]
    column = sums[640 : 640 + C, C : C + 1]
    diagonal = lax.broadcasted_iota(jnp.int32, (C, C), 0) == lax.broadcasted_iota(
        jnp.int32, (C, C), 1
    )
    goff[...] = jnp.sum(jnp.where(diagonal, column, 0.0), axis=0, keepdims=True)

    def row(o, carry):
        at = pl.ds(pl.multiple_of(o * 16, 16), 16)
        gr = grads[at, 0:128] * (1.0 / CELLS)
        gi = grads[at, 128:256] * (1.0 / CELLS)
        for j in range(C):
            mr, mi = modes[16 * j : 16 * j + 16, 0:128], modes[16 * j : 16 * j + 16, 128:256]
            real = gr * mr + gi * mi
            imag = gi * mr - gr * mi
            for k in range(KX):
                gs_v[0, o, j, k] = real[4 * k : 4 * k + 4, 0:MY]
                gs_v[1, o, j, k] = imag[4 * k : 4 * k + 4, 0:MY]
        return carry

    size = C // GROUPS
    for b in range(GROUPS):
        lax.fori_loop(b * size, (b + 1) * size, row, 0)
        for r in range(2):
            at = pl.ds(b * size, size)
            copy = pltpu.make_async_copy(gs_v.at[r, at], gs.at[r, at], gs_sem.at[r, b])
            copy.start()
            copies.append(copy)
    for copy in copies:
        copy.wait()


def per_device(history, w_point, offset, spectral_weight, cotangent):
    def two(table):
        return jnp.asarray(halves(table))

    xa, xs, xe = x_tables()
    yt = y_table()
    slots = slot_tables()
    weight = jnp.transpose(spectral_weight, (0, 1, 2, 4, 3, 5))
    vmem = pl.BlockSpec(memory_space=pltpu.VMEM)
    hbm = pl.BlockSpec(memory_space=pl.ANY)
    block = jax.ShapeDtypeStruct((C, XC, YC, NZ * NT), BF16)
    square = jax.ShapeDtypeStruct((C, C), F32)
    line = jax.ShapeDtypeStruct((1, C), F32)
    dma = pltpu.SemaphoreType.DMA
    fields, sums = pl.pallas_call(
        kernel,
        out_shape=(jax.ShapeDtypeStruct((2,) + block.shape, BF16), jax.ShapeDtypeStruct((664, 256), F32)),
        in_specs=[vmem] * 4 + [hbm] * 9,
        out_specs=(vmem,) * 2,
        scratch_shapes=[
            pltpu.VMEM((2, 144, 512), BF16),
            pltpu.VMEM((2, 2, 256, 512), BF16),
            pltpu.VMEM((2, 2, 512, 384), BF16),
            pltpu.VMEM((2, 4, 256, 256), BF16),
            pltpu.VMEM((2, 128, 256), BF16),
            pltpu.VMEM((2, 256, 128), BF16),
            pltpu.VMEM((64, 160), BF16),
            pltpu.VMEM((160, 64), BF16),
            pltpu.VMEM((2, C, C, KX, Q, MY), F32),
            pltpu.VMEM((2, C, C, 16, 128), F32),
            pltpu.VMEM((XC, ROWS, 512), BF16),
            pltpu.VMEM((XC, ROWS, 512), F32),
            pltpu.VMEM((2, XC, ROWS, 512), BF16),
            pltpu.VMEM((C * 16, 256), F32),
            pltpu.VMEM((4, GX, XC + 1, 4, 128), F32),
            pltpu.VMEM((4, GX, XC + 1, 4, 128), F32),
            pltpu.VMEM((2, EXTRA, XC + 1, 2, 128), F32),
            pltpu.VMEM((2, GX, XC + 1, 2, 128), F32),
            pltpu.VMEM((2, GX, XC + 1, 2, 128), F32),
            pltpu.VMEM((2, EXTRA, XC + 1, 2, 128), F32),
            pltpu.VMEM((2, GY, 2, 16, 128), F32),
            pltpu.VMEM((2, 4, GY, 16, 128), F32),
            pltpu.VMEM((2, 4, GY, 16, 128), F32),
            pltpu.VMEM((2, 5, GY, 16, 128), F32),
            pltpu.VMEM((2, GY, 2, 16, 128), F32),
            pltpu.VMEM((3, 24, 128), F32),
            pltpu.VMEM((3, 8, 24, 128), F32),
            dma((9,)),
            dma((4, GX)),
            dma((4, GX)),
            dma((2, EXTRA)),
            dma((2, GX)),
            dma((2, GX)),
            dma((2, EXTRA)),
            dma((2, 5, GY)),
            dma((2, 4, GY)),
            dma((2, 4, GY)),
            dma((2, 5, GY)),
            dma((3, 8)),
            dma((3, 8)),
        ],
        compiler_params=pltpu.CompilerParams(
            collective_id=0, has_side_effects=True, vmem_limit_bytes=58 * 1024 * 1024
        ),
    )(
        history[0], cotangent[0], w_point, offset.reshape(1, C), weight,
        two(depth_table()), two(xa), two(xs), two(xe), two(yt), two(yt.T),
        jnp.asarray(slots.astype(ml_dtypes.bfloat16)),
        jnp.asarray(slots.transpose(0, 2, 1).astype(ml_dtypes.bfloat16)),
    )
    act, ghist, gs, gpoint, goff = pl.pallas_call(
        finish,
        out_shape=(
            block, block, jax.ShapeDtypeStruct((2, C, C, KX, Q, MY), F32), square, line,
        ),
        in_specs=[hbm, vmem],
        out_specs=(hbm,) * 3 + (vmem,) * 2,
        scratch_shapes=[pltpu.VMEM((2, C, C, KX, Q, MY), F32), dma((2,)), dma((2, GROUPS))],
        compiler_params=pltpu.CompilerParams(vmem_limit_bytes=16 * 1024 * 1024),
    )(fields, sums)
    grad_spectral = jnp.transpose(gs, (0, 1, 2, 4, 3, 5))
    return act[None], ghist[None], grad_spectral, gpoint, goff.reshape(C)


def solution(mesh):
    grid = P(None, None, "gx", "gy", None)
    modes = P(None, None, None, "gx", "gy", None)
    return jax.shard_map(
        per_device,
        mesh=mesh,
        in_specs=(grid, P(), P(), modes, grid),
        out_specs=(grid, grid, modes, P(), P()),
        check_vma=False,
    )
```

```python
import math

import jax
import jax.numpy as jnp
import ml_dtypes
import numpy as np
from jax import lax
from jax.experimental import pallas as pl
from jax.experimental.pallas import tpu as pltpu
from jax.sharding import PartitionSpec as P

MESH = pl.DeviceIdType.MESH
F32 = jnp.float32
BF16 = jnp.bfloat16
C = 20
NX, NY, NZ, NT = 128, 64, 64, 8
MX, MY, MZ, MT = 24, 24, 16, 8
GX, GY = 32, 8
XC, YC = NX // GX, NY // GY
KX = MX // GY
Q = MZ * MT // GX
ROWS = C * YC
CELLS = NX * NY * NZ * NT
XPOS, ZPOS = 4, 8
EXTRA, STRIDE = 4, 10
gelu_coef = 0.7978845608028654
gelu_cubic = 0.044715


def kept(length, keep):
    half = keep // 2
    return np.concatenate([np.arange(half), length - half + np.arange(half)])


def halves(table):
    table = np.asarray(table, np.float64)
    hi = table.astype(np.float32).astype(ml_dtypes.bfloat16)
    lo = (table - hi.astype(np.float64)).astype(np.float32).astype(ml_dtypes.bfloat16)
    return np.stack([hi, lo])


def handled(h):
    p, s = h // 2, h % 2
    if p == 0:
        return [(NZ - 8, t) for t in ((2, 3) if s == 0 else (6, 7))]
    if p == 8:
        return [(NZ - 8, t) for t in ((0, 1) if s == 0 else (4, 5))]
    if p < 8:
        return [(p, t) for t in ((0, 3) if s == 0 else (4, 7))]
    return [(16 - p, t) for t in ((5, 6) if s == 0 else (1, 2))]


def depth_table():
    z, t = np.arange(NZ)[:, None], np.arange(NT)[None]

    def wave(kz, kt):
        return 2 * np.pi * ((z * kz % NZ) / NZ + (t * kt % NT) / NT).reshape(-1)

    rows = []
    for h in range(GX):
        angles = [wave(*mode) for mode in handled(h)]
        rows += [np.cos(a) for a in angles] + [-np.sin(a) for a in angles]
    rows += [np.cos(wave(0, 0)), np.cos(wave(0, 4))]
    for j in range(1, EXTRA):
        rows += [np.cos(wave(0, j)), -np.sin(wave(0, j))]
    return np.stack(rows + [np.zeros(NZ * NT)] * 8)


def x_tables():
    fx = kept(NX, MX).reshape(GY, KX)
    x = np.arange(NX).reshape(GX, XC).T
    angle = 2 * np.pi * (fx[:, :, None, None] * x[None, None] % NX) / NX
    cos, sin = np.cos(angle), np.sin(angle)
    main = np.zeros((GY, 2, 2, 8, XC, GX, 2, 2))
    extra = np.zeros((2, GY, 2, 8, XC, GX, 2))
    direct = ((cos, sin), (-sin, cos))
    conj = ((cos, -sin), (-sin, -cos))
    for out in range(2):
        for k in range(KX):
            row = KX * out + k
            for into in range(2):
                for m in range(2):
                    main[:, 0, m, row, :, :, into, m] = direct[out][into][:, k]
                    main[:, 1, m, row, :, :, into, m] = conj[out][into][:, k]
                extra[1, :, 0, row, :, :, into] = direct[out][into][:, k]
                extra[1, :, 1, row, :, :, into] = conj[out][into][:, k]
            extra[0, :, 0, row, :, :, 0] = direct[out][0][:, k]
            extra[0, :, 1, row, :, :, 1] = direct[out][0][:, k]

    def tables(full, columns):
        blocks = full.size // (GY * 8 * columns)
        full = full.reshape(GY, blocks, 8, columns)
        tail = np.zeros((4, GY, blocks, 2, columns))
        for g in range(4):
            rows = full[:, :, g:6:4]
            tail[g, :, :, : rows.shape[2]] = rows
        count = GY * blocks * 8
        forward = np.stack([full.reshape(count, columns), tail.reshape(count, columns)])
        backward = np.stack([
            full.swapaxes(0, 1).reshape(count, columns).T,
            tail.swapaxes(1, 2).reshape(count, columns).T,
        ])
        return forward, backward

    forward, backward = tables(main, XC * GX * 4)
    extras = [tables(extra[kind], XC * GX * 2) for kind in range(2)]
    return (
        forward, backward, np.stack([v[0] for v in extras]), np.stack([v[1] for v in extras])
    )


def slot_table():
    out = np.zeros((Q, 8, 160))
    for q in range(Q):
        for ri in range(2):
            for k in range(KX):
                r = KX * ri + k
                at = 16 * ri + 4 * k + q
                out[q, r, at] = 1
                out[q, 6 + r // 4, 32 + 32 * (r % 4) + at] = 1
    return out.reshape(Q * 8, 160)


def y_table():
    fy = kept(NY, MY)
    angle = 2 * np.pi * (np.arange(NY)[:, None] * fy[None] % NY) / NY
    cos, sin = np.cos(angle), np.sin(angle)
    out = np.zeros((2, NY, 2, 128))
    out[0, :, 0, :MY] = cos
    out[1, :, 0, :MY] = sin
    out[0, :, 1, :MY] = -sin
    out[1, :, 1, :MY] = cos
    return out.reshape(2 * NY, 256)


def split(value):
    hi = value.astype(BF16)
    return hi, (value - hi.astype(F32)).astype(BF16)


def dot(a, b, dims):
    return lax.dot_general(a, b, (dims, ((), ())), preferred_element_type=F32)


NN = ((1,), (0,))
NTD = ((1,), (1,))


def dot3(a, b, dims=NN):
    return dot(a[0], b[0], dims) + (dot(a[0], b[1], dims) + dot(a[1], b[0], dims))


def exact(a, b, dims=NN):
    return lax.dot_general(
        a, b, (dims, ((), ())), precision=lax.Precision.HIGHEST, preferred_element_type=F32
    )


def swap_groups(parts):
    parts = list(parts)
    group = lax.broadcasted_iota(jnp.int32, parts[0].shape, 1) // 8
    for s in (8, 4, 2, 1):
        low = lax.rem(group // s, 2) == 0
        for i in range(16):
            if i & s:
                continue
            a, b = parts[i], parts[i + s]
            parts[i] = jnp.where(low, a, pltpu.roll(b, 8 * s, 1))
            parts[i + s] = jnp.where(low, pltpu.roll(a, 128 - 8 * s, 1), b)
    return parts


def dot2(a, b):
    return dot(a, b[0], NN) + dot(a, b[1], NN)


def kernel(
    hist, cot, wpt, off, w_hbm, dtab_h, xa_h, xs_h, xea_h, xes_h, ya_h, ys_h, u_h, ut_h,
    fields, sums,
    dtab, xa, xs, xea, xes, ya, ys, u, ut, w_v, wp, vb, base, gpre, mixed,
    sendx, recvx, sende, recve, sendr, recvr, sendy, recvy, backs, backr, exy, backx, small, smalls,
    load_sem, sx_sem, rx_sem, se_sem, re_sem, sr_sem, rr_sem, sy_sem, ry_sem, sb_sem, rb_sem, ss_sem, rs_sem,
):
    d = lax.axis_index("gx")
    e = lax.axis_index("gy")
    modes, grads = sums.at[0:320], sums.at[320:640]
    half, side = d // 2, lax.rem(d, 2)
    is_a = (d >= 2) & (d < 16)
    is_b = d >= 18
    is_mid = (d >= 16) & (d < 18)
    is_low = d < 2
    special = lax.rem(d, STRIDE) == 0
    which = d // STRIDE
    kind_e = jnp.where(d == 0, 0, 1)
    pair = GX - 2 * half
    mirror = GX + 1 - d

    loads = [
        pltpu.make_async_copy(src, dst, load_sem.at[i])
        for i, (src, dst) in enumerate((
            (dtab_h, dtab), (w_hbm, w_v), (xa_h, xa), (xs_h, xs), (ya_h, ya), (ys_h, ys),
            (u_h, u), (ut_h, ut),
        ))
    ]
    extra_loads = [
        pltpu.make_async_copy(src.at[:, kind_e], dst, load_sem.at[len(loads) + i])
        for i, (src, dst) in enumerate(((xea_h, xea), (xes_h, xes)))
    ]
    for load in loads:
        load.start()

    @pl.when(special)
    def _():
        for load in extra_loads:
            load.start()


    @pl.when(is_low | is_mid)
    def _():
        backr[:, 1] = jnp.zeros_like(backr[:, 1])

    barrier = pltpu.get_barrier_semaphore()

    def signal(x, y):
        pl.semaphore_signal(barrier, inc=1, device_id=(x, y), device_id_type=MESH)

    def over(count, body, first=0):
        def go(k, carry):
            body(k)
            return carry

        lax.fori_loop(first, count, go, 0)

    over(GX, lambda k: signal((d + k) & (GX - 1), e), 1)
    over(GY, lambda k: signal(d, (e + k) & (GY - 1)), 1)
    def remote(src, dst, send, recv, x, y):
        return pltpu.make_async_remote_copy(
            src_ref=src, dst_ref=dst, send_sem=send, recv_sem=recv,
            device_id=(x, y), device_id_type=MESH,
        )

    def x_copy(p, peer, slot):
        return remote(
            sendx.at[p, peer], recvx.at[p, slot], sx_sem.at[p, peer], rx_sem.at[p, slot], peer, e
        )

    def start_x(p):
        over(GX, lambda k: x_copy(p, (d + k) & (GX - 1), d).start(), 1)
        recvx[p, d] = sendx[p, d]

    def wait_x(p):
        def go(k):
            peer = (d + GX - k) & (GX - 1)
            copy = x_copy(p, peer, peer)
            copy.wait_recv()
            copy.wait_send()

        over(GX, go, 1)

    def e_copy(f, j, slot):
        return remote(
            sende.at[f, j], recve.at[f, slot], se_sem.at[f, j], re_sem.at[f, slot], j * STRIDE, e
        )

    def start_e(f):
        def go(j):
            @pl.when(d != j * STRIDE)
            def _():
                e_copy(f, j, d).start()

        over(EXTRA, go)

        @pl.when(special)
        def _():
            recve[f, d] = sende[f, which]

    def wait_e_sent(f):
        def go(j):
            @pl.when(d != j * STRIDE)
            def _():
                e_copy(f, j, d).wait_send()

        over(EXTRA, go)

    def wait_e(f):
        def go(k):
            peer = (d + GX - k) & (GX - 1)
            remote(
                sende.at[f, 0], recve.at[f, peer], se_sem.at[f, 0], re_sem.at[f, peer], peer, e
            ).wait_recv()

        over(GX, go, 1)

    def r_copy(f, peer, j):
        return remote(
            sendr.at[f, peer], recvr.at[f, j], sr_sem.at[f, peer], rr_sem.at[f, j], peer, e
        )

    def start_r(f):
        over(GX, lambda k: r_copy(f, (d + k) & (GX - 1), which).start(), 1)
        recvr[f, which] = sendr[f, d]

    def wait_r(f):
        def go(j):
            @pl.when(d != j * STRIDE)
            def _():
                r_copy(f, 0, j).wait_recv()

        over(EXTRA, go)

        @pl.when(special)
        def _():
            over(GX, lambda k: r_copy(f, (d + k) & (GX - 1), which).wait_send(), 1)

    def owner_of(part, m):
        if part == 0:
            x = jnp.where(is_a | is_mid, d, jnp.where(is_low, d + 16, mirror))
            slot = jnp.where(is_a, 3 * m, jnp.where(is_b, 1 + m, jnp.where(is_mid, m, 2 + m)))
        else:
            x = jnp.where(is_a, pair + (side + m) % 2, d)
            slot = jnp.where(is_a, m, 3 - m)
        return x, slot

    def each_y(f, act_on):
        def block(part, m, y, k):
            x, slot = owner_of(part, m)

            @pl.when((x != d) | (k != 0))
            def _():
                act_on(remote(
                    sendy.at[f, y, part, m], recvy.at[f, e, slot], sy_sem.at[f, 2 * part + m, y],
                    ry_sem.at[f, slot, e], x, y,
                ))

        def go(k):
            y = (e + k) & (GY - 1)
            for m in range(2):
                block(0, m, y, k)

            @pl.when(is_a | is_b)
            def _():
                for m in range(2):
                    block(1, m, y, k)

        over(GY, go)

    def each_ex(f, act_on):
        def go(k):
            y = (e + k) & (GY - 1)
            for part in range(2):
                slot = which if part == 0 else (4 - which) & 3

                def act_here():
                    act_on(remote(
                        exy.at[f, y, part], recvy.at[f, e, slot], sy_sem.at[f, 4 + part, y],
                        ry_sem.at[f, slot, e], part, y,
                    ))

                if part == 0:
                    pl.when((d != 0) | (k != 0))(act_here)
                else:
                    act_here()

        over(GY, go)

    def start_y(f):
        each_y(f, lambda copy: copy.start())
        for part in range(2):
            for m in range(2):
                x, slot = owner_of(part, m)

                @pl.when((x == d) & ((part == 0) | is_b))
                def _():
                    recvy[f, e, slot] = sendy[f, e, part, m]

    def start_ex(f):
        each_ex(f, lambda copy: copy.start())

        @pl.when(d == 0)
        def _():
            recvy[f, e, 0] = exy[f, e, 0]

    def wait_y(f):
        def go(k):
            y = (e + GY - k) & (GY - 1)
            for slot in range(4):
                own = jnp.where(
                    is_a, slot in (0, 3), jnp.where(is_b, slot >= 2, jnp.where(is_mid, slot < 2, slot == 0))
                ) & (d != 1)

                @pl.when((k != 0) | ~own)
                def _():
                    remote(
                        sendy.at[f, 0, 0, 0], recvy.at[f, y, slot], sy_sem.at[f, 0, 0],
                        ry_sem.at[f, slot, y], d, y,
                    ).wait_recv()

        over(GY, go)
        each_y(f, lambda copy: copy.wait_send())

        @pl.when(special)
        def _():
            each_ex(f, lambda copy: copy.wait_send())

    def maker_of(slot):
        if slot in (1, 2):
            x = mirror
            part, m = 0, slot - 1
        else:
            x = d
            part, m = 0, slot // 3
        if slot < 2:
            xb, mb = pair + (side + slot) % 2, slot
        else:
            xb, mb = d, 3 - slot
        xm, mm = (d, slot) if slot < 2 else (d - 16, slot - 2)
        x = jnp.where(is_b, xb, jnp.where(is_mid, xm, x))
        part = jnp.where(is_b, 1, part)
        m = jnp.where(is_b, mb, jnp.where(is_mid, mm, m))
        return x, part, m

    def each_b(f, act_on):
        def go(k):
            y = (e + k) & (GY - 1)

            @pl.when(d >= 2)
            def _():
                for slot in range(4):
                    x, part, m = maker_of(slot)

                    @pl.when((x != d) | (k != 0))
                    def _():
                        act_on(remote(
                            backs.at[f, y, slot], backr.at[f, part, m, e], sb_sem.at[f, slot, y],
                            rb_sem.at[f, 2 * part + m, e], x, y,
                        ))

            @pl.when(is_low)
            def _():
                for slot in range(4):
                    j = jnp.where(d == 0, slot, (4 - slot) & 3)

                    def act_here():
                        act_on(remote(
                            backs.at[f, y, slot], backx.at[f, side, e], sb_sem.at[f, slot, y],
                            rb_sem.at[f, 4 + side, e], j * STRIDE, y,
                        ))

                    if slot == 0:
                        pl.when((d != 0) | (k != 0))(act_here)
                    else:
                        act_here()

        over(GY, go)

    def start_b(f):
        each_b(f, lambda copy: copy.start())

        @pl.when(d >= 2)
        def _():
            for slot in range(4):
                x, part, m = maker_of(slot)

                @pl.when(x == d)
                def _():
                    backr[f, part, m, e] = backs[f, e, slot]

        @pl.when(d == 0)
        def _():
            backx[f, 0, e] = backs[f, e, 0]

    def wait_b(f):
        def go(k):
            y = (e + GY - k) & (GY - 1)

            def arrived(part, m):
                remote(
                    backs.at[f, 0, 0], backr.at[f, part, m, y], sb_sem.at[f, 0, 0],
                    rb_sem.at[f, 2 * part + m, y], d, y,
                ).wait_recv()

            for m in range(2):
                @pl.when((k != 0) | is_b | is_low)
                def _():
                    arrived(0, m)

                @pl.when(is_a | (is_b & (k != 0)))
                def _():
                    arrived(1, m)

        over(GY, go)
        each_b(f, lambda copy: copy.wait_send())

    def wait_b_extra(f):
        def go(k):
            y = (e + GY - k) & (GY - 1)
            for part in range(2):
                def arrived():
                    remote(
                        backs.at[f, 0, 0], backx.at[f, part, y], sb_sem.at[f, 0, 0],
                        rb_sem.at[f, 4 + part, y], d, y,
                    ).wait_recv()

                if part == 0:
                    pl.when((d != 0) | (k != 0))(arrived)
                else:
                    arrived()

        over(GY, go)

    lane128 = lax.broadcasted_iota(jnp.int32, (1, 128), 1)

    def depth_analyse(p, f, get, terms):
        for t in range(XC + 1):
            total = None
            for tab, part in terms:
                if t < XC:
                    rows = get(t, part)[0:128]
                else:
                    rows = jnp.concatenate([get(x, part)[128:ROWS] for x in range(XC)], axis=0)
                term = dot(dtab[tab], rows, NTD)
                total = term if total is None else total + term
            sendx[p, :, t] = total[0:128].reshape(GX, 4, 128)
            sende[f, :, t] = total[128:136].reshape(EXTRA, 2, 128)

    def x_analyse(tiles, tables, out):
        left = tiles[XC]
        count = left.shape[0]
        per = 256 // count
        main, tail = None, None
        for b in range(XC // per):
            xs_here = range(b * per, (b + 1) * per)
            at = slice(b * 256, (b + 1) * 256)
            cols = split(jnp.concatenate([tiles[x] for x in xs_here], axis=0))
            term = dot3((tables[0, 0, :, at], tables[1, 0, :, at]), cols)
            main = term if main is None else main + term
            cols = split(jnp.concatenate(
                [left if x == 0 else pltpu.roll(left, 128 - 32 * x, 1) for x in xs_here], axis=0
            ))
            term = dot3((tables[0, 1, :, at], tables[1, 1, :, at]), cols)
            tail = term if tail is None else tail + term
        blocks = out.shape[:-2]
        size = tail.shape[0] // 4
        out[...] = main.reshape(blocks + (8, 128))
        tail = jnp.where(lane128 < 32, tail, 0.0)
        packed = tail[0:size]
        for g in range(1, 4):
            packed = packed + pltpu.roll(tail[size * g : size * g + size], 32 * g, 1)
        out[..., 6:8, :] = packed.reshape(blocks + (2, 128))

    def analyse_main(p, f):
        x_analyse([recvx[p, :, t].reshape(128, 128) for t in range(XC + 1)], xa, sendy.at[f])

    def analyse_extra(f):
        x_analyse(
            [recve[f, :, t].reshape(64, 128) for t in range(XC + 1)], xea, exy.at[f]
        )

    def y_analyse(f, out):
        cols = split(jnp.concatenate([recvy[f, y].reshape(32, 128) for y in range(GY)], axis=1))
        merged = dot2(ut[...], cols)
        rows = []
        parts = [
            merged[16 * (g // GY) : 16 * (g // GY) + 16, 128 * (g % GY) : 128 * (g % GY) + 128]
            for g in range(16)
        ]
        rows += swap_groups(parts)
        parts = []
        for g in range(16):
            at = 32 + 16 * (g // GY)
            lanes = slice(128 * (g % GY), 128 * (g % GY) + 128)
            total = merged[at : at + 16, lanes]
            for n in range(1, 4):
                total = total + pltpu.roll(merged[at + 32 * n : at + 32 * n + 16, lanes], 128 - 32 * n, 1)
            parts.append(total)
        rows += swap_groups([jnp.where(lane128 < 32, part, 0.0) for part in parts])[: C - 16]
        out[...] = dot3(split(jnp.concatenate(rows, axis=0)), (ya[0], ya[1]))

    def y_synthesise(f):
        cols = dot3(split(mixed[...]), (ys[0], ys[1]))
        blank = jnp.zeros((16, 128), F32)
        main = swap_groups([cols[16 * c : 16 * c + 16] for c in range(16)])
        tail = swap_groups(
            [cols[16 * c : 16 * c + 16] for c in range(16, C)] + [blank] * (32 - C)
        )
        stack = []
        for y in range(GY):
            rows = [main[y], main[GY + y]]
            for n in range(4):
                for g in (y, GY + y):
                    rows.append(tail[g] if n == 0 else pltpu.roll(tail[g], 32 * n, 1))
            stack.append(jnp.concatenate(rows, axis=0))
        out = dot2(u[...], split(jnp.concatenate(stack, axis=1)))
        for y in range(GY):
            backs[f, y] = out[:, 128 * y : 128 * y + 128].reshape(4, 8, 128)

    def x_synthesise(slots, tables, put):
        rows = slots[...]
        count = math.prod(rows.shape[:-2])
        main_cols = split(rows.reshape(count * 8, 128))
        tail = rows[..., 6:8, :].reshape(count * 2, 128)
        tail_cols = split(jnp.concatenate(
            [tail] + [pltpu.roll(tail, 128 - 32 * g, 1) for g in range(1, 4)], axis=0
        ))
        main = dot3((tables[0, 0], tables[1, 0]), main_cols)
        tail = dot3((tables[0, 1], tables[1, 1]), tail_cols)
        tail = jnp.where(lane128 < 32, tail, 0.0)
        per = main.shape[0] // XC
        left = None
        for x in range(XC):
            at = slice(per * x, per * x + per)
            put(x, main[at])
            part = tail[at]
            left = part if x == 0 else left + pltpu.roll(part, 32 * x, 1)
        put(XC, left)

    def synthesise_main(f, p):
        def put(t, rows):
            sendx[p, :, t] = rows.reshape(GX, 4, 128)

        x_synthesise(backr.at[f], xs, put)

    def synthesise_extra(f):
        def put(t, rows):
            sendr[f, :, t] = rows.reshape(GX, 2, 128)

        x_synthesise(backx.at[f], xes, put)

    def depth_rows(p, f, t):
        tile = recvx[p, :, t].reshape(128, 128)
        extra = recvr[f, :, t].reshape(8, 128)
        rest = jnp.zeros((120, 128), F32)
        low = jnp.concatenate([extra, rest], axis=0).T
        return jnp.concatenate([tile.T, low[:, 0:16]], axis=1)

    def depth_synthesise(p, f, x, left):
        cols = jnp.concatenate([depth_rows(p, f, x), left[32 * x : 32 * x + 32]], axis=0)
        return dot3(split(cols), (dtab[0], dtab[1])) * (1.0 / CELLS)

    def send_main_then_extra(p, f):
        @pl.when(special)
        def _():
            wait_e(f)
            analyse_extra(f)
            start_ex(f)

        wait_x(p)
        analyse_main(p, f)
        start_y(f)

    def cells_back(f, p):
        @pl.when(special)
        def _():
            wait_b_extra(f)
            synthesise_extra(f)
            start_r(f)

        wait_b(f)
        synthesise_main(f, p)
        start_x(p)

    for x in range(XC):
        vb[x] = hist[:, x].astype(F32).reshape(ROWS, 512).astype(BF16)
    loads[0].wait()
    depth_analyse(0, 0, lambda x, part: vb[x], ((0, 0), (1, 0)))

    pl.semaphore_wait(barrier, GX + GY - 2)
    start_e(0)
    start_x(0)

    for load in loads[1:]:
        load.wait()

    @pl.when(special)
    def _():
        for load in extra_loads:
            load.wait()

    def pack(o):
        for r in range(2):
            for i in range(C):
                for k in range(KX):
                    wp[r, o, i, 4 * k : 4 * k + 4, 0:MY] = w_v[r, o, i, k]

    over(C, pack)

    spread = (
        lax.broadcasted_iota(jnp.int32, (ROWS, C), 0) // YC
        == lax.broadcasted_iota(jnp.int32, (ROWS, C), 1)
    ).astype(F32)
    same_y = lax.rem(lax.broadcasted_iota(jnp.int32, (ROWS, ROWS), 0), YC) == lax.rem(
        lax.broadcasted_iota(jnp.int32, (ROWS, ROWS), 1), YC
    )
    wide = exact(exact(spread, wpt[...]), spread, NTD)
    point = split(jnp.where(same_y, wide, 0.0))
    wide_t = exact(exact(spread, wpt[...], ((1,), (1,))), spread, NTD)
    point_t = split(jnp.where(same_y, wide_t, 0.0))
    bias = jnp.sum(spread * off[...], axis=1, keepdims=True)
    for x in range(XC):
        base[x] = dot(point[0], vb[x], NN) + dot(point[1], vb[x], NN) + bias

    send_main_then_extra(0, 0)
    wait_y(0)
    y_analyse(0, modes)

    valid = (lax.broadcasted_iota(jnp.int32, (16, 128), 0) < 4 * KX) & (
        lax.broadcasted_iota(jnp.int32, (16, 128), 1) < MY
    )

    def mix(o):
        real = jnp.zeros((16, 128), F32)
        imag = jnp.zeros((16, 128), F32)
        for i in range(C):
            wr, wi = wp[0, o, i], wp[1, o, i]
            mr, mi = modes[16 * i : 16 * i + 16, 0:128], modes[16 * i : 16 * i + 16, 128:256]
            real += wr * mr - wi * mi
            imag += wr * mi + wi * mr
        at = pl.ds(pl.multiple_of(o * 16, 16), 16)
        mixed[at, 0:128] = jnp.where(valid, real, 0.0)
        mixed[at, 128:256] = jnp.where(valid, imag, 0.0)

    over(C, mix)
    y_synthesise(0)
    start_b(0)
    cells_back(0, 1)
    wait_x(1)
    wait_r(0)
    wait_e_sent(0)

    left = depth_rows(1, 0, XC)
    row_sum = jnp.zeros((ROWS, 1), F32)
    for x in range(XC):
        pre = depth_synthesise(1, 0, x, left) + base[x]
        inner = gelu_coef * (pre + gelu_cubic * pre * pre * pre)
        smooth = jnp.tanh(inner)
        slope = 0.5 * (1.0 + smooth) + 0.5 * pre * (1.0 - smooth * smooth) * gelu_coef * (
            1.0 + 3.0 * gelu_cubic * pre * pre
        )
        fields[0, :, x] = (0.5 * pre * (1.0 + smooth)).reshape(C, YC, 512).astype(BF16)
        grad = cot[:, x].astype(F32).reshape(ROWS, 512) * slope
        row_sum += jnp.sum(grad, axis=1, keepdims=True)
        hi, lo = split(grad)
        gpre[0, x] = hi
        gpre[1, x] = lo
    depth_analyse(2, 1, lambda x, part: gpre[part, x], ((0, 0), (0, 1), (1, 0)))
    start_e(1)
    start_x(2)

    cross = jnp.zeros((ROWS, ROWS), F32)
    for x in range(XC):
        g = (gpre[0, x], gpre[1, x])
        base[x] = dot3(point_t, g)
        cross += dot(g[0], vb[x], NTD) + dot(g[1], vb[x], NTD)
    gather = (
        lax.broadcasted_iota(jnp.int32, (24, ROWS), 1) // YC
        == lax.broadcasted_iota(jnp.int32, (24, ROWS), 0)
    ).astype(F32)
    place = (
        lax.broadcasted_iota(jnp.int32, (ROWS, 128), 0) // YC
        == lax.broadcasted_iota(jnp.int32, (ROWS, 128), 1)
    ).astype(F32)
    lane = lax.broadcasted_iota(jnp.int32, (ROWS, 128), 1)
    both = exact(jnp.where(same_y, cross, 0.0), place) + jnp.where(lane == C, row_sum, 0.0)
    small[0] = exact(gather, both)

    def small_copy(s, k, peer, slot):
        return remote(small.at[s], smalls.at[s, slot], ss_sem.at[s, k], rs_sem.at[s, slot], *peer)

    xpos, zpos = d // ZPOS, lax.rem(d, ZPOS)
    steps = (
        (GY, e, lambda i: (d, i)),
        (XPOS, xpos, lambda i: (i * ZPOS + zpos, e)),
        (ZPOS, zpos, lambda i: (xpos * ZPOS + i, e)),
    )

    def start_small(s):
        count, me, peer_of = steps[s]
        for k in range(1, count):
            small_copy(s, k, peer_of(lax.rem(me + k, count)), me).start()
        smalls[s, me] = small[s]

    def finish_small(s):
        count, me, peer_of = steps[s]
        for k in range(1, count):
            other = lax.rem(me + count - k, count)
            copy = small_copy(s, k, peer_of(other), other)
            copy.wait_recv()
            copy.wait_send()
        total = smalls[s, 0]
        for k in range(1, count):
            total = total + smalls[s, k]
        return total

    start_small(0)
    send_main_then_extra(2, 1)
    small[1] = finish_small(0)
    start_small(1)
    wait_y(1)
    y_analyse(1, grads)

    def mix_back(j):
        real = jnp.zeros((16, 128), F32)
        imag = jnp.zeros((16, 128), F32)
        for o in range(C):
            wr, wi = wp[0, o, j], wp[1, o, j]
            gr, gi = grads[16 * o : 16 * o + 16, 0:128], grads[16 * o : 16 * o + 16, 128:256]
            real += wr * gr + wi * gi
            imag += wr * gi - wi * gr
        at = pl.ds(pl.multiple_of(j * 16, 16), 16)
        mixed[at, 0:128] = jnp.where(valid, real, 0.0)
        mixed[at, 128:256] = jnp.where(valid, imag, 0.0)

    over(C, mix_back)
    y_synthesise(1)
    start_b(1)
    small[2] = finish_small(1)
    start_small(2)
    cells_back(1, 3)

    total = finish_small(2)
    sums[640:664, 0:128] = total
    sums[640:664, 128:256] = jnp.zeros_like(total)

    wait_x(3)
    wait_r(1)
    wait_e_sent(1)
    left = depth_rows(3, 1, XC)
    for x in range(XC):
        total = depth_synthesise(3, 1, x, left) + base[x]
        fields[1, :, x] = total.reshape(C, YC, 512).astype(BF16)


GROUPS = 5


def finish(fields, sums, act, ghist, gs, gpoint, goff, gs_v, io_sem, gs_sem):
    modes, grads = sums.at[0:320], sums.at[320:640]
    copies = [
        pltpu.make_async_copy(fields.at[0], act, io_sem.at[0]),
        pltpu.make_async_copy(fields.at[1], ghist, io_sem.at[1]),
    ]
    for copy in copies:
        copy.start()
    gpoint[...] = sums[640 : 640 + C, 0:C]
    column = sums[640 : 640 + C, C : C + 1]
    diagonal = lax.broadcasted_iota(jnp.int32, (C, C), 0) == lax.broadcasted_iota(
        jnp.int32, (C, C), 1
    )
    goff[...] = jnp.sum(jnp.where(diagonal, column, 0.0), axis=0, keepdims=True)

    def row(o, carry):
        at = pl.ds(pl.multiple_of(o * 16, 16), 16)
        gr = grads[at, 0:128] * (1.0 / CELLS)
        gi = grads[at, 128:256] * (1.0 / CELLS)
        for j in range(C):
            mr, mi = modes[16 * j : 16 * j + 16, 0:128], modes[16 * j : 16 * j + 16, 128:256]
            real = gr * mr + gi * mi
            imag = gi * mr - gr * mi
            for k in range(KX):
                gs_v[0, o, j, k] = real[4 * k : 4 * k + 4, 0:MY]
                gs_v[1, o, j, k] = imag[4 * k : 4 * k + 4, 0:MY]
        return carry

    size = C // GROUPS
    for b in range(GROUPS):
        lax.fori_loop(b * size, (b + 1) * size, row, 0)
        for r in range(2):
            at = pl.ds(b * size, size)
            copy = pltpu.make_async_copy(gs_v.at[r, at], gs.at[r, at], gs_sem.at[r, b])
            copy.start()
            copies.append(copy)
    for copy in copies:
        copy.wait()


def per_device(history, w_point, offset, spectral_weight, cotangent):
    def two(table):
        return jnp.asarray(halves(table))

    xa, xs, xea, xes = x_tables()
    yt = y_table()
    slots = slot_table()
    weight = jnp.transpose(spectral_weight, (0, 1, 2, 4, 3, 5))
    vmem = pl.BlockSpec(memory_space=pltpu.VMEM)
    hbm = pl.BlockSpec(memory_space=pl.ANY)
    block = jax.ShapeDtypeStruct((C, XC, YC, NZ * NT), BF16)
    square = jax.ShapeDtypeStruct((C, C), F32)
    line = jax.ShapeDtypeStruct((1, C), F32)
    dma = pltpu.SemaphoreType.DMA
    fields, sums = pl.pallas_call(
        kernel,
        out_shape=(jax.ShapeDtypeStruct((2,) + block.shape, BF16), jax.ShapeDtypeStruct((664, 256), F32)),
        in_specs=[vmem] * 4 + [hbm] * 10,
        out_specs=(vmem,) * 2,
        scratch_shapes=[
            pltpu.VMEM((2, 144, 512), BF16),
            pltpu.VMEM((2, 2, 256, 512), BF16),
            pltpu.VMEM((2, 2, 512, 256), BF16),
            pltpu.VMEM((2, 2, 128, 256), BF16),
            pltpu.VMEM((2, 2, 256, 128), BF16),
            pltpu.VMEM((2, 128, 256), BF16),
            pltpu.VMEM((2, 256, 128), BF16),
            pltpu.VMEM((32, 160), BF16),
            pltpu.VMEM((160, 32), BF16),
            pltpu.VMEM((2, C, C, KX, Q, MY), F32),
            pltpu.VMEM((2, C, C, 16, 128), F32),
            pltpu.VMEM((XC, ROWS, 512), BF16),
            pltpu.VMEM((XC, ROWS, 512), F32),
            pltpu.VMEM((2, XC, ROWS, 512), BF16),
            pltpu.VMEM((C * 16, 256), F32),
            pltpu.VMEM((4, GX, XC + 1, 4, 128), F32),
            pltpu.VMEM((4, GX, XC + 1, 4, 128), F32),
            pltpu.VMEM((2, EXTRA, XC + 1, 2, 128), F32),
            pltpu.VMEM((2, GX, XC + 1, 2, 128), F32),
            pltpu.VMEM((2, GX, XC + 1, 2, 128), F32),
            pltpu.VMEM((2, EXTRA, XC + 1, 2, 128), F32),
            pltpu.VMEM((2, GY, 2, 2, 8, 128), F32),
            pltpu.VMEM((2, GY, Q, 8, 128), F32),
            pltpu.VMEM((2, GY, Q, 8, 128), F32),
            pltpu.VMEM((2, 2, 2, GY, 8, 128), F32),
            pltpu.VMEM((2, GY, 2, 8, 128), F32),
            pltpu.VMEM((2, 2, GY, 8, 128), F32),
            pltpu.VMEM((3, 24, 128), F32),
            pltpu.VMEM((3, 8, 24, 128), F32),
            dma((10,)),
            dma((4, GX)),
            dma((4, GX)),
            dma((2, EXTRA)),
            dma((2, GX)),
            dma((2, GX)),
            dma((2, EXTRA)),
            dma((2, 6, GY)),
            dma((2, 4, GY)),
            dma((2, 4, GY)),
            dma((2, 6, GY)),
            dma((3, 8)),
            dma((3, 8)),
        ],
        compiler_params=pltpu.CompilerParams(
            collective_id=0, has_side_effects=True, vmem_limit_bytes=58 * 1024 * 1024
        ),
    )(
        history[0], cotangent[0], w_point, offset.reshape(1, C), weight,
        two(depth_table()), two(xa), two(xs), two(xea), two(xes), two(yt), two(yt.T),
        jnp.asarray(slots.astype(ml_dtypes.bfloat16)),
        jnp.asarray(slots.T.astype(ml_dtypes.bfloat16)),
    )
    act, ghist, gs, gpoint, goff = pl.pallas_call(
        finish,
        out_shape=(
            block, block, jax.ShapeDtypeStruct((2, C, C, KX, Q, MY), F32), square, line,
        ),
        in_specs=[hbm, vmem],
        out_specs=(hbm,) * 3 + (vmem,) * 2,
        scratch_shapes=[pltpu.VMEM((2, C, C, KX, Q, MY), F32), dma((2,)), dma((2, GROUPS))],
        compiler_params=pltpu.CompilerParams(vmem_limit_bytes=16 * 1024 * 1024),
    )(fields, sums)
    grad_spectral = jnp.transpose(gs, (0, 1, 2, 4, 3, 5))
    return act[None], ghist[None], grad_spectral, gpoint, goff.reshape(C)


def solution(mesh):
    grid = P(None, None, "gx", "gy", None)
    modes = P(None, None, None, "gx", "gy", None)
    return jax.shard_map(
        per_device,
        mesh=mesh,
        in_specs=(grid, P(), P(), modes, grid),
        out_specs=(grid, grid, modes, P(), P()),
        check_vma=False,
    )
```

```python
import math

import jax
import jax.numpy as jnp
import ml_dtypes
import numpy as np
from jax import lax
from jax.experimental import pallas as pl
from jax.experimental.pallas import tpu as pltpu
from jax.sharding import PartitionSpec as P

MESH = pl.DeviceIdType.MESH
F32 = jnp.float32
BF16 = jnp.bfloat16
C = 20
NX, NY, NZ, NT = 128, 64, 64, 8
MX, MY, MZ, MT = 24, 24, 16, 8
GX, GY = 32, 8
XC, YC = NX // GX, NY // GY
KX = MX // GY
Q = MZ * MT // GX
ROWS = C * YC
CELLS = NX * NY * NZ * NT
XPOS, ZPOS = 4, 8
EXTRA, STRIDE = 4, 10
gelu_coef = 0.7978845608028654
gelu_cubic = 0.044715


def kept(length, keep):
    half = keep // 2
    return np.concatenate([np.arange(half), length - half + np.arange(half)])


def halves(table):
    table = np.asarray(table, np.float64)
    hi = table.astype(np.float32).astype(ml_dtypes.bfloat16)
    lo = (table - hi.astype(np.float64)).astype(np.float32).astype(ml_dtypes.bfloat16)
    return np.stack([hi, lo])


def handled(h):
    p, s = h // 2, h % 2
    if p == 0:
        return [(NZ - 8, t) for t in ((2, 3) if s == 0 else (6, 7))]
    if p == 8:
        return [(NZ - 8, t) for t in ((0, 1) if s == 0 else (4, 5))]
    if p < 8:
        return [(p, t) for t in ((0, 3) if s == 0 else (4, 7))]
    return [(16 - p, t) for t in ((5, 6) if s == 0 else (1, 2))]


def depth_table():
    z, t = np.arange(NZ)[:, None], np.arange(NT)[None]

    def wave(kz, kt):
        return 2 * np.pi * ((z * kz % NZ) / NZ + (t * kt % NT) / NT).reshape(-1)

    rows = []
    for h in range(GX):
        angles = [wave(*mode) for mode in handled(h)]
        rows += [np.cos(a) for a in angles] + [-np.sin(a) for a in angles]
    rows += [np.cos(wave(0, 0)), np.cos(wave(0, 4))]
    for j in range(1, EXTRA):
        rows += [np.cos(wave(0, j)), -np.sin(wave(0, j))]
    return np.stack(rows + [np.zeros(NZ * NT)] * 8)


def x_tables():
    fx = kept(NX, MX).reshape(GY, KX)
    x = np.arange(NX).reshape(GX, XC).T
    angle = 2 * np.pi * (fx[:, :, None, None] * x[None, None] % NX) / NX
    cos, sin = np.cos(angle), np.sin(angle)
    main = np.zeros((GY, 2, 2, 8, XC, GX, 2, 2))
    extra = np.zeros((2, GY, 2, 8, XC, GX, 2))
    direct = ((cos, sin), (-sin, cos))
    conj = ((cos, -sin), (-sin, -cos))
    for out in range(2):
        for k in range(KX):
            row = KX * out + k
            for into in range(2):
                for m in range(2):
                    main[:, 0, m, row, :, :, into, m] = direct[out][into][:, k]
                    main[:, 1, m, row, :, :, into, m] = conj[out][into][:, k]
                extra[1, :, 0, row, :, :, into] = direct[out][into][:, k]
                extra[1, :, 1, row, :, :, into] = conj[out][into][:, k]
            extra[0, :, 0, row, :, :, 0] = direct[out][0][:, k]
            extra[0, :, 1, row, :, :, 1] = direct[out][0][:, k]

    def tables(full, columns):
        blocks = full.size // (GY * 8 * columns)
        full = full.reshape(GY, blocks, 8, columns)
        tail = np.zeros((4, GY, blocks, 2, columns))
        for g in range(4):
            rows = full[:, :, g:6:4]
            tail[g, :, :, : rows.shape[2]] = rows
        count = GY * blocks * 8
        forward = np.stack([full.reshape(count, columns), tail.reshape(count, columns)])
        backward = np.stack([
            full.swapaxes(0, 1).reshape(count, columns).T,
            tail.swapaxes(1, 2).reshape(count, columns).T,
        ])
        return forward, backward

    forward, backward = tables(main, XC * GX * 4)
    extras = [tables(extra[kind], XC * GX * 2) for kind in range(2)]
    return (
        forward, backward, np.stack([v[0] for v in extras]), np.stack([v[1] for v in extras])
    )


def slot_table():
    out = np.zeros((Q, 8, 160))
    for q in range(Q):
        for ri in range(2):
            for k in range(KX):
                r = KX * ri + k
                at = 16 * ri + 4 * k + q
                out[q, r, at] = 1
                out[q, 6 + r // 4, 32 + 32 * (r % 4) + at] = 1
    return out.reshape(Q * 8, 160)


def y_tables():
    fy = kept(NY, MY)
    angle = 2 * np.pi * (np.arange(NY)[:, None] * fy[None] % NY) / NY
    cos, sin = np.cos(angle), np.sin(angle)
    out = np.zeros((4, 2, NY, 2, 4, 32))
    for g in range(4):
        out[g, 0, :, 0, g, :MY] = cos
        out[g, 1, :, 0, g, :MY] = sin
        out[g, 0, :, 1, g, :MY] = -sin
        out[g, 1, :, 1, g, :MY] = cos
    return out.reshape(8 * NY, 256), out.sum(axis=0).reshape(2 * NY, 256)


def split(value):
    hi = value.astype(BF16)
    return hi, (value - hi.astype(F32)).astype(BF16)


def dot(a, b, dims):
    return lax.dot_general(a, b, (dims, ((), ())), preferred_element_type=F32)


NN = ((1,), (0,))
NTD = ((1,), (1,))


def dot3(a, b, dims=NN):
    return dot(a[0], b[0], dims) + (dot(a[0], b[1], dims) + dot(a[1], b[0], dims))


def exact(a, b, dims=NN):
    return lax.dot_general(
        a, b, (dims, ((), ())), precision=lax.Precision.HIGHEST, preferred_element_type=F32
    )


def swap_groups(parts):
    parts = list(parts)
    group = lax.broadcasted_iota(jnp.int32, parts[0].shape, 1) // 8
    for s in (8, 4, 2, 1):
        low = lax.rem(group // s, 2) == 0
        for i in range(16):
            if i & s:
                continue
            a, b = parts[i], parts[i + s]
            if b is None:
                if a is not None:
                    parts[i] = jnp.where(low, a, 0.0)
                    parts[i + s] = jnp.where(low, pltpu.roll(a, 128 - 8 * s, 1), 0.0)
                continue
            parts[i] = jnp.where(low, a, pltpu.roll(b, 8 * s, 1))
            parts[i + s] = jnp.where(low, pltpu.roll(a, 128 - 8 * s, 1), b)
    return parts


def dot2(a, b):
    return dot(a, b[0], NN) + dot(a, b[1], NN)


def kernel(
    hist, cot, wpt, off, w_hbm, dtab_h, xa_h, xs_h, xea_h, xes_h, ya_h, yar_h, ys_h, ysr_h, u_h, ut_h,
    fields, sums,
    dtab, xa, xs, xea, xes, ya, yar, ys, ysr, u, ut, w_v, wp, vb, base, gpre, mixed,
    sendx, recvx, sende, recve, sendr, recvr, sendy, recvy, backs, backr, exy, backx, small, smalls,
    load_sem, sx_sem, rx_sem, se_sem, re_sem, sr_sem, rr_sem, sy_sem, ry_sem, sb_sem, rb_sem, ss_sem, rs_sem,
):
    d = lax.axis_index("gx")
    e = lax.axis_index("gy")
    modes, grads = sums.at[0:80], sums.at[80:400]
    half, side = d // 2, lax.rem(d, 2)
    is_a = (d >= 2) & (d < 16)
    is_b = d >= 18
    is_mid = (d >= 16) & (d < 18)
    is_low = d < 2
    special = lax.rem(d, STRIDE) == 0
    which = d // STRIDE
    kind_e = jnp.where(d == 0, 0, 1)
    pair = GX - 2 * half
    mirror = GX + 1 - d

    loads = [
        pltpu.make_async_copy(src, dst, load_sem.at[i])
        for i, (src, dst) in enumerate((
            (dtab_h, dtab), (w_hbm, w_v), (xa_h, xa), (xs_h, xs), (ya_h, ya), (yar_h, yar), (ys_h, ys), (ysr_h, ysr),
            (u_h, u), (ut_h, ut),
        ))
    ]
    extra_loads = [
        pltpu.make_async_copy(src.at[:, kind_e], dst, load_sem.at[len(loads) + i])
        for i, (src, dst) in enumerate(((xea_h, xea), (xes_h, xes)))
    ]
    for load in loads:
        load.start()

    @pl.when(special)
    def _():
        for load in extra_loads:
            load.start()


    @pl.when(is_low | is_mid)
    def _():
        backr[:, 1] = jnp.zeros_like(backr[:, 1])

    barrier = pltpu.get_barrier_semaphore()

    def signal(x, y):
        pl.semaphore_signal(barrier, inc=1, device_id=(x, y), device_id_type=MESH)

    def over(count, body, first=0):
        def go(k, carry):
            body(k)
            return carry

        lax.fori_loop(first, count, go, 0)

    over(GX, lambda k: signal((d + k) & (GX - 1), e), 1)
    over(GY, lambda k: signal(d, (e + k) & (GY - 1)), 1)
    def remote(src, dst, send, recv, x, y):
        return pltpu.make_async_remote_copy(
            src_ref=src, dst_ref=dst, send_sem=send, recv_sem=recv,
            device_id=(x, y), device_id_type=MESH,
        )

    def x_copy(p, peer, slot):
        return remote(
            sendx.at[p, peer], recvx.at[p, slot], sx_sem.at[p, peer], rx_sem.at[p, slot], peer, e
        )

    def start_x(p):
        over(GX, lambda k: x_copy(p, (d + k) & (GX - 1), d).start(), 1)
        recvx[p, d] = sendx[p, d]

    def wait_x(p):
        def go(k):
            peer = (d + GX - k) & (GX - 1)
            copy = x_copy(p, peer, peer)
            copy.wait_recv()
            copy.wait_send()

        over(GX, go, 1)

    def e_copy(f, j, slot):
        return remote(
            sende.at[f, j], recve.at[f, slot], se_sem.at[f, j], re_sem.at[f, slot], j * STRIDE, e
        )

    def start_e(f):
        def go(j):
            @pl.when(d != j * STRIDE)
            def _():
                e_copy(f, j, d).start()

        over(EXTRA, go)

        @pl.when(special)
        def _():
            recve[f, d] = sende[f, which]

    def wait_e_sent(f):
        def go(j):
            @pl.when(d != j * STRIDE)
            def _():
                e_copy(f, j, d).wait_send()

        over(EXTRA, go)

    def wait_e(f):
        def go(k):
            peer = (d + GX - k) & (GX - 1)
            remote(
                sende.at[f, 0], recve.at[f, peer], se_sem.at[f, 0], re_sem.at[f, peer], peer, e
            ).wait_recv()

        over(GX, go, 1)

    def r_copy(f, peer, j):
        return remote(
            sendr.at[f, peer], recvr.at[f, j], sr_sem.at[f, peer], rr_sem.at[f, j], peer, e
        )

    def start_r(f):
        over(GX, lambda k: r_copy(f, (d + k) & (GX - 1), which).start(), 1)
        recvr[f, which] = sendr[f, d]

    def wait_r(f):
        def go(j):
            @pl.when(d != j * STRIDE)
            def _():
                r_copy(f, 0, j).wait_recv()

        over(EXTRA, go)

        @pl.when(special)
        def _():
            over(GX, lambda k: r_copy(f, (d + k) & (GX - 1), which).wait_send(), 1)

    def owner_of(part, m):
        if part == 0:
            x = jnp.where(is_a | is_mid, d, jnp.where(is_low, d + 16, mirror))
            slot = jnp.where(is_a, 3 * m, jnp.where(is_b, 1 + m, jnp.where(is_mid, m, 2 + m)))
        else:
            x = jnp.where(is_a, pair + (side + m) % 2, d)
            slot = jnp.where(is_a, m, 3 - m)
        return x, slot

    def each_y(f, act_on):
        def block(part, m, y, k):
            x, slot = owner_of(part, m)

            @pl.when((x != d) | (k != 0))
            def _():
                act_on(remote(
                    sendy.at[f, y, part, m], recvy.at[f, e, slot], sy_sem.at[f, 2 * part + m, y],
                    ry_sem.at[f, slot, e], x, y,
                ))

        def go(k):
            y = (e + k) & (GY - 1)
            for m in range(2):
                block(0, m, y, k)

            @pl.when(is_a | is_b)
            def _():
                for m in range(2):
                    block(1, m, y, k)

        over(GY, go)

    def each_ex(f, act_on):
        def go(k):
            y = (e + k) & (GY - 1)
            for part in range(2):
                slot = which if part == 0 else (4 - which) & 3

                def act_here():
                    act_on(remote(
                        exy.at[f, y, part], recvy.at[f, e, slot], sy_sem.at[f, 4 + part, y],
                        ry_sem.at[f, slot, e], part, y,
                    ))

                if part == 0:
                    pl.when((d != 0) | (k != 0))(act_here)
                else:
                    act_here()

        over(GY, go)

    def start_y(f):
        each_y(f, lambda copy: copy.start())
        for part in range(2):
            for m in range(2):
                x, slot = owner_of(part, m)

                @pl.when((x == d) & ((part == 0) | is_b))
                def _():
                    recvy[f, e, slot] = sendy[f, e, part, m]

    def start_ex(f):
        each_ex(f, lambda copy: copy.start())

        @pl.when(d == 0)
        def _():
            recvy[f, e, 0] = exy[f, e, 0]

    def wait_y(f):
        def go(k):
            y = (e + GY - k) & (GY - 1)
            for slot in range(4):
                own = jnp.where(
                    is_a, slot in (0, 3), jnp.where(is_b, slot >= 2, jnp.where(is_mid, slot < 2, slot == 0))
                ) & (d != 1)

                @pl.when((k != 0) | ~own)
                def _():
                    remote(
                        sendy.at[f, 0, 0, 0], recvy.at[f, y, slot], sy_sem.at[f, 0, 0],
                        ry_sem.at[f, slot, y], d, y,
                    ).wait_recv()

        over(GY, go)
        each_y(f, lambda copy: copy.wait_send())

        @pl.when(special)
        def _():
            each_ex(f, lambda copy: copy.wait_send())

    def maker_of(slot):
        if slot in (1, 2):
            x = mirror
            part, m = 0, slot - 1
        else:
            x = d
            part, m = 0, slot // 3
        if slot < 2:
            xb, mb = pair + (side + slot) % 2, slot
        else:
            xb, mb = d, 3 - slot
        xm, mm = (d, slot) if slot < 2 else (d - 16, slot - 2)
        x = jnp.where(is_b, xb, jnp.where(is_mid, xm, x))
        part = jnp.where(is_b, 1, part)
        m = jnp.where(is_b, mb, jnp.where(is_mid, mm, m))
        return x, part, m

    def each_b(f, act_on):
        def go(k):
            y = (e + k) & (GY - 1)

            @pl.when(d >= 2)
            def _():
                for slot in range(4):
                    x, part, m = maker_of(slot)

                    @pl.when((x != d) | (k != 0))
                    def _():
                        act_on(remote(
                            backs.at[f, y, slot], backr.at[f, part, m, e], sb_sem.at[f, slot, y],
                            rb_sem.at[f, 2 * part + m, e], x, y,
                        ))

            @pl.when(is_low)
            def _():
                for slot in range(4):
                    j = jnp.where(d == 0, slot, (4 - slot) & 3)

                    def act_here():
                        act_on(remote(
                            backs.at[f, y, slot], backx.at[f, side, e], sb_sem.at[f, slot, y],
                            rb_sem.at[f, 4 + side, e], j * STRIDE, y,
                        ))

                    if slot == 0:
                        pl.when((d != 0) | (k != 0))(act_here)
                    else:
                        act_here()

        over(GY, go)

    def start_b(f):
        each_b(f, lambda copy: copy.start())

        @pl.when(d >= 2)
        def _():
            for slot in range(4):
                x, part, m = maker_of(slot)

                @pl.when(x == d)
                def _():
                    backr[f, part, m, e] = backs[f, e, slot]

        @pl.when(d == 0)
        def _():
            backx[f, 0, e] = backs[f, e, 0]

    def wait_b(f):
        def go(k):
            y = (e + GY - k) & (GY - 1)

            def arrived(part, m):
                remote(
                    backs.at[f, 0, 0], backr.at[f, part, m, y], sb_sem.at[f, 0, 0],
                    rb_sem.at[f, 2 * part + m, y], d, y,
                ).wait_recv()

            for m in range(2):
                @pl.when((k != 0) | is_b | is_low)
                def _():
                    arrived(0, m)

                @pl.when(is_a | (is_b & (k != 0)))
                def _():
                    arrived(1, m)

        over(GY, go)
        each_b(f, lambda copy: copy.wait_send())

    def wait_b_extra(f):
        def go(k):
            y = (e + GY - k) & (GY - 1)
            for part in range(2):
                def arrived():
                    remote(
                        backs.at[f, 0, 0], backx.at[f, part, y], sb_sem.at[f, 0, 0],
                        rb_sem.at[f, 4 + part, y], d, y,
                    ).wait_recv()

                if part == 0:
                    pl.when((d != 0) | (k != 0))(arrived)
                else:
                    arrived()

        over(GY, go)

    lane128 = lax.broadcasted_iota(jnp.int32, (1, 128), 1)

    def depth_analyse(p, f, get, terms):
        for t in range(XC + 1):
            total = None
            for tab, part in terms:
                if t < XC:
                    rows = get(t, part)[0:128]
                else:
                    rows = jnp.concatenate([get(x, part)[128:ROWS] for x in range(XC)], axis=0)
                term = dot(dtab[tab], rows, NTD)
                total = term if total is None else total + term
            sendx[p, :, t] = total[0:128].reshape(GX, 4, 128)
            sende[f, :, t] = total[128:136].reshape(EXTRA, 2, 128)

    def x_analyse(tiles, tables, out):
        left = tiles[XC]
        count = left.shape[0]
        per = 256 // count
        main, tail = None, None
        for b in range(XC // per):
            xs_here = range(b * per, (b + 1) * per)
            at = slice(b * 256, (b + 1) * 256)
            cols = split(jnp.concatenate([tiles[x] for x in xs_here], axis=0))
            term = dot3((tables[0, 0, :, at], tables[1, 0, :, at]), cols)
            main = term if main is None else main + term
            cols = split(jnp.concatenate(
                [left if x == 0 else pltpu.roll(left, 128 - 32 * x, 1) for x in xs_here], axis=0
            ))
            term = dot3((tables[0, 1, :, at], tables[1, 1, :, at]), cols)
            tail = term if tail is None else tail + term
        blocks = out.shape[:-2]
        size = tail.shape[0] // 4
        out[...] = main.reshape(blocks + (8, 128))
        tail = jnp.where(lane128 < 32, tail, 0.0)
        packed = tail[0:size]
        for g in range(1, 4):
            packed = packed + pltpu.roll(tail[size * g : size * g + size], 32 * g, 1)
        out[..., 6:8, :] = packed.reshape(blocks + (2, 128))

    def analyse_main(p, f):
        x_analyse([recvx[p, :, t].reshape(128, 128) for t in range(XC + 1)], xa, sendy.at[f])

    def analyse_extra(f):
        x_analyse(
            [recve[f, :, t].reshape(64, 128) for t in range(XC + 1)], xea, exy.at[f]
        )

    def y_cells(f):
        cols = split(jnp.concatenate([recvy[f, y].reshape(32, 128) for y in range(GY)], axis=1))
        merged = dot2(ut[...], cols)
        rows = []
        parts = [
            merged[16 * (g // GY) : 16 * (g // GY) + 16, 128 * (g % GY) : 128 * (g % GY) + 128]
            for g in range(16)
        ]
        rows += swap_groups(parts)
        parts = []
        for g in range(16):
            at = 32 + 16 * (g // GY)
            lanes = slice(128 * (g % GY), 128 * (g % GY) + 128)
            total = merged[at : at + 16, lanes]
            for n in range(1, 4):
                total = total + pltpu.roll(merged[at + 32 * n : at + 32 * n + 16, lanes], 128 - 32 * n, 1)
            parts.append(total)
        rows += swap_groups([jnp.where(lane128 < 32, part, 0.0) for part in parts])[: C - 16]
        return rows

    def y_synthesise(f, cols):
        main = swap_groups(cols[:16])
        tail = swap_groups(cols[16:] + [None] * (32 - C))
        stack = []
        for y in range(GY):
            rows = [main[y], main[GY + y]]
            for n in range(4):
                for g in (y, GY + y):
                    rows.append(tail[g] if n == 0 else pltpu.roll(tail[g], 32 * n, 1))
            stack.append(jnp.concatenate(rows, axis=0))
        out = dot2(u[...], split(jnp.concatenate(stack, axis=1)))
        for y in range(GY):
            backs[f, y] = out[:, 128 * y : 128 * y + 128].reshape(4, 8, 128)

    def x_synthesise(slots, tables, put):
        rows = slots[...]
        count = math.prod(rows.shape[:-2])
        main_cols = split(rows.reshape(count * 8, 128))
        tail = rows[..., 6:8, :].reshape(count * 2, 128)
        tail_cols = split(jnp.concatenate(
            [tail] + [pltpu.roll(tail, 128 - 32 * g, 1) for g in range(1, 4)], axis=0
        ))
        main = dot3((tables[0, 0], tables[1, 0]), main_cols)
        tail = dot3((tables[0, 1], tables[1, 1]), tail_cols)
        tail = jnp.where(lane128 < 32, tail, 0.0)
        per = main.shape[0] // XC
        left = None
        for x in range(XC):
            at = slice(per * x, per * x + per)
            put(x, main[at])
            part = tail[at]
            left = part if x == 0 else left + pltpu.roll(part, 32 * x, 1)
        put(XC, left)

    def synthesise_main(f, p):
        def put(t, rows):
            sendx[p, :, t] = rows.reshape(GX, 4, 128)

        x_synthesise(backr.at[f], xs, put)

    def synthesise_extra(f):
        def put(t, rows):
            sendr[f, :, t] = rows.reshape(GX, 2, 128)

        x_synthesise(backx.at[f], xes, put)

    def depth_rows(p, f, t):
        tile = recvx[p, :, t].reshape(128, 128)
        extra = recvr[f, :, t].reshape(8, 128)
        rest = jnp.zeros((120, 128), F32)
        low = jnp.concatenate([extra, rest], axis=0).T
        return jnp.concatenate([tile.T, low[:, 0:16]], axis=1)

    def depth_synthesise(p, f, x, left):
        cols = jnp.concatenate([depth_rows(p, f, x), left[32 * x : 32 * x + 32]], axis=0)
        return dot3(split(cols), (dtab[0], dtab[1])) * (1.0 / CELLS)

    def send_main_then_extra(p, f):
        @pl.when(special)
        def _():
            wait_e(f)
            analyse_extra(f)
            start_ex(f)

        wait_x(p)
        analyse_main(p, f)
        start_y(f)

    def cells_back(f, p):
        @pl.when(special)
        def _():
            wait_b_extra(f)
            synthesise_extra(f)
            start_r(f)

        wait_b(f)
        synthesise_main(f, p)
        start_x(p)

    for x in range(XC):
        vb[x] = hist[:, x].astype(F32).reshape(ROWS, 512).astype(BF16)
    loads[0].wait()
    depth_analyse(0, 0, lambda x, part: vb[x], ((0, 0), (1, 0)))

    pl.semaphore_wait(barrier, GX + GY - 2)
    start_e(0)
    start_x(0)

    for load in loads[1:]:
        load.wait()

    @pl.when(special)
    def _():
        for load in extra_loads:
            load.wait()

    wp[...] = jnp.zeros_like(wp)

    def pack(o):
        for r in range(2):
            for i in range(C):
                lanes = slice(32 * (i % 4), 32 * (i % 4) + MY)
                for k in range(KX):
                    wp[r, o, i // 4, 4 * k : 4 * k + 4, lanes] = w_v[r, o, i, k]

    over(C, pack)

    spread = (
        lax.broadcasted_iota(jnp.int32, (ROWS, C), 0) // YC
        == lax.broadcasted_iota(jnp.int32, (ROWS, C), 1)
    ).astype(F32)
    same_y = lax.rem(lax.broadcasted_iota(jnp.int32, (ROWS, ROWS), 0), YC) == lax.rem(
        lax.broadcasted_iota(jnp.int32, (ROWS, ROWS), 1), YC
    )
    wide = exact(exact(spread, wpt[...]), spread, NTD)
    point = split(jnp.where(same_y, wide, 0.0))
    wide_t = exact(exact(spread, wpt[...], ((1,), (1,))), spread, NTD)
    point_t = split(jnp.where(same_y, wide_t, 0.0))
    bias = jnp.sum(spread * off[...], axis=1, keepdims=True)
    for x in range(XC):
        base[x] = dot(point[0], vb[x], NN) + dot(point[1], vb[x], NN) + bias

    send_main_then_extra(0, 0)
    wait_y(0)
    cells = y_cells(0)
    cells = jnp.concatenate(
        [jnp.concatenate(cells[i : i + 4], axis=1) for i in range(0, C, 4)], axis=0
    )
    modes[...] = dot3(split(cells), (ya[0], ya[1]))

    def mix(o):
        real = jnp.zeros((16, 128), F32)
        imag = jnp.zeros((16, 128), F32)
        for i in range(C // 4):
            wr, wi = wp[0, o, i], wp[1, o, i]
            mr, mi = modes[16 * i : 16 * i + 16, 0:128], modes[16 * i : 16 * i + 16, 128:256]
            real += wr * mr - wi * mi
            imag += wr * mi + wi * mr
        at = pl.ds(pl.multiple_of(o * 16, 16), 16)
        mixed[at, 0:128] = real
        mixed[at, 128:256] = imag

    over(C, mix)
    cols = dot3(split(mixed[...]), (ysr[0], ysr[1]))
    y_synthesise(0, [cols[16 * c : 16 * c + 16] for c in range(C)])
    start_b(0)
    cells_back(0, 1)
    wait_x(1)
    wait_r(0)
    wait_e_sent(0)

    left = depth_rows(1, 0, XC)
    row_sum = jnp.zeros((ROWS, 1), F32)
    for x in range(XC):
        pre = depth_synthesise(1, 0, x, left) + base[x]
        inner = gelu_coef * (pre + gelu_cubic * pre * pre * pre)
        smooth = jnp.tanh(inner)
        slope = 0.5 * (1.0 + smooth) + 0.5 * pre * (1.0 - smooth * smooth) * gelu_coef * (
            1.0 + 3.0 * gelu_cubic * pre * pre
        )
        fields[0, :, x] = (0.5 * pre * (1.0 + smooth)).reshape(C, YC, 512).astype(BF16)
        grad = cot[:, x].astype(F32).reshape(ROWS, 512) * slope
        row_sum += jnp.sum(grad, axis=1, keepdims=True)
        hi, lo = split(grad)
        gpre[0, x] = hi
        gpre[1, x] = lo
    depth_analyse(2, 1, lambda x, part: gpre[part, x], ((0, 0), (0, 1), (1, 0)))
    start_e(1)
    start_x(2)

    cross = jnp.zeros((ROWS, ROWS), F32)
    for x in range(XC):
        g = (gpre[0, x], gpre[1, x])
        base[x] = dot3(point_t, g)
        cross += dot(g[0], vb[x], NTD) + dot(g[1], vb[x], NTD)
    gather = (
        lax.broadcasted_iota(jnp.int32, (24, ROWS), 1) // YC
        == lax.broadcasted_iota(jnp.int32, (24, ROWS), 0)
    ).astype(F32)
    place = (
        lax.broadcasted_iota(jnp.int32, (ROWS, 128), 0) // YC
        == lax.broadcasted_iota(jnp.int32, (ROWS, 128), 1)
    ).astype(F32)
    lane = lax.broadcasted_iota(jnp.int32, (ROWS, 128), 1)
    both = exact(jnp.where(same_y, cross, 0.0), place) + jnp.where(lane == C, row_sum, 0.0)
    small[0] = exact(gather, both)

    def small_copy(s, k, peer, slot):
        return remote(small.at[s], smalls.at[s, slot], ss_sem.at[s, k], rs_sem.at[s, slot], *peer)

    xpos, zpos = d // ZPOS, lax.rem(d, ZPOS)
    steps = (
        (GY, e, lambda i: (d, i)),
        (XPOS, xpos, lambda i: (i * ZPOS + zpos, e)),
        (ZPOS, zpos, lambda i: (xpos * ZPOS + i, e)),
    )

    def start_small(s):
        count, me, peer_of = steps[s]
        for k in range(1, count):
            small_copy(s, k, peer_of(lax.rem(me + k, count)), me).start()
        smalls[s, me] = small[s]

    def finish_small(s):
        count, me, peer_of = steps[s]
        for k in range(1, count):
            other = lax.rem(me + count - k, count)
            copy = small_copy(s, k, peer_of(other), other)
            copy.wait_recv()
            copy.wait_send()
        total = smalls[s, 0]
        for k in range(1, count):
            total = total + smalls[s, k]
        return total

    start_small(0)
    send_main_then_extra(2, 1)
    small[1] = finish_small(0)
    start_small(1)
    wait_y(1)
    grads[...] = dot3(split(jnp.concatenate(y_cells(1), axis=0)), (yar[0], yar[1]))

    def mix_back(j):
        real = jnp.zeros((16, 128), F32)
        imag = jnp.zeros((16, 128), F32)
        for o in range(C):
            wr, wi = wp[0, o, j], wp[1, o, j]
            gr, gi = grads[16 * o : 16 * o + 16, 0:128], grads[16 * o : 16 * o + 16, 128:256]
            real += wr * gr + wi * gi
            imag += wr * gi - wi * gr
        at = pl.ds(pl.multiple_of(j * 16, 16), 16)
        mixed[at, 0:128] = real
        mixed[at, 128:256] = imag

    over(C // 4, mix_back)
    cols = dot3(split(mixed[0:80]), (ys[0], ys[1]))
    y_synthesise(1, [
        cols[16 * (c // 4) : 16 * (c // 4) + 16, 128 * (c % 4) : 128 * (c % 4) + 128] for c in range(C)
    ])
    start_b(1)
    small[2] = finish_small(1)
    start_small(2)
    cells_back(1, 3)

    total = finish_small(2)
    sums[400:424, 0:128] = total
    sums[400:424, 128:256] = jnp.zeros_like(total)

    wait_x(3)
    wait_r(1)
    wait_e_sent(1)
    left = depth_rows(3, 1, XC)
    for x in range(XC):
        total = depth_synthesise(3, 1, x, left) + base[x]
        fields[1, :, x] = total.reshape(C, YC, 512).astype(BF16)


GROUPS = 5


def finish(fields, sums, act, ghist, gs, gpoint, goff, modes, gs_v, io_sem, gs_sem):
    grads = sums.at[80:400]
    copies = [
        pltpu.make_async_copy(fields.at[0], act, io_sem.at[0]),
        pltpu.make_async_copy(fields.at[1], ghist, io_sem.at[1]),
    ]
    for copy in copies:
        copy.start()
    gpoint[...] = sums[400 : 400 + C, 0:C]
    column = sums[400 : 400 + C, C : C + 1]
    diagonal = lax.broadcasted_iota(jnp.int32, (C, C), 0) == lax.broadcasted_iota(
        jnp.int32, (C, C), 1
    )
    goff[...] = jnp.sum(jnp.where(diagonal, column, 0.0), axis=0, keepdims=True)

    for j in range(C):
        for half in range(2):
            lanes = slice(128 * half, 128 * half + 128)
            tile = sums[16 * (j // 4) : 16 * (j // 4) + 16, lanes]
            modes[16 * j : 16 * j + 16, lanes] = tile if j % 4 == 0 else pltpu.roll(tile, 128 - 32 * (j % 4), 1)

    def row(o, carry):
        at = pl.ds(pl.multiple_of(o * 16, 16), 16)
        gr = grads[at, 0:128] * (1.0 / CELLS)
        gi = grads[at, 128:256] * (1.0 / CELLS)
        for j in range(C):
            mr, mi = modes[16 * j : 16 * j + 16, 0:128], modes[16 * j : 16 * j + 16, 128:256]
            real = gr * mr + gi * mi
            imag = gi * mr - gr * mi
            for k in range(KX):
                gs_v[0, o, j, k] = real[4 * k : 4 * k + 4, 0:MY]
                gs_v[1, o, j, k] = imag[4 * k : 4 * k + 4, 0:MY]
        return carry

    size = C // GROUPS
    for b in range(GROUPS):
        lax.fori_loop(b * size, (b + 1) * size, row, 0)
        for r in range(2):
            at = pl.ds(b * size, size)
            copy = pltpu.make_async_copy(gs_v.at[r, at], gs.at[r, at], gs_sem.at[r, b])
            copy.start()
            copies.append(copy)
    for copy in copies:
        copy.wait()


def per_device(history, w_point, offset, spectral_weight, cotangent):
    def two(table):
        return jnp.asarray(halves(table))

    xa, xs, xea, xes = x_tables()
    ya, yar = y_tables()
    slots = slot_table()
    weight = jnp.transpose(spectral_weight, (0, 1, 2, 4, 3, 5))
    vmem = pl.BlockSpec(memory_space=pltpu.VMEM)
    hbm = pl.BlockSpec(memory_space=pl.ANY)
    block = jax.ShapeDtypeStruct((C, XC, YC, NZ * NT), BF16)
    square = jax.ShapeDtypeStruct((C, C), F32)
    line = jax.ShapeDtypeStruct((1, C), F32)
    dma = pltpu.SemaphoreType.DMA
    fields, sums = pl.pallas_call(
        kernel,
        out_shape=(jax.ShapeDtypeStruct((2,) + block.shape, BF16), jax.ShapeDtypeStruct((424, 256), F32)),
        in_specs=[vmem] * 4 + [hbm] * 12,
        out_specs=(vmem,) * 2,
        scratch_shapes=[
            pltpu.VMEM((2, 144, 512), BF16),
            pltpu.VMEM((2, 2, 256, 512), BF16),
            pltpu.VMEM((2, 2, 512, 256), BF16),
            pltpu.VMEM((2, 2, 128, 256), BF16),
            pltpu.VMEM((2, 2, 256, 128), BF16),
            pltpu.VMEM((2, 512, 256), BF16),
            pltpu.VMEM((2, 128, 256), BF16),
            pltpu.VMEM((2, 256, 512), BF16),
            pltpu.VMEM((2, 256, 128), BF16),
            pltpu.VMEM((32, 160), BF16),
            pltpu.VMEM((160, 32), BF16),
            pltpu.VMEM((2, C, C, KX, Q, MY), F32),
            pltpu.VMEM((2, C, C // 4, 16, 128), F32),
            pltpu.VMEM((XC, ROWS, 512), BF16),
            pltpu.VMEM((XC, ROWS, 512), F32),
            pltpu.VMEM((2, XC, ROWS, 512), BF16),
            pltpu.VMEM((C * 16, 256), F32),
            pltpu.VMEM((4, GX, XC + 1, 4, 128), F32),
            pltpu.VMEM((4, GX, XC + 1, 4, 128), F32),
            pltpu.VMEM((2, EXTRA, XC + 1, 2, 128), F32),
            pltpu.VMEM((2, GX, XC + 1, 2, 128), F32),
            pltpu.VMEM((2, GX, XC + 1, 2, 128), F32),
            pltpu.VMEM((2, EXTRA, XC + 1, 2, 128), F32),
            pltpu.VMEM((2, GY, 2, 2, 8, 128), F32),
            pltpu.VMEM((2, GY, Q, 8, 128), F32),
            pltpu.VMEM((2, GY, Q, 8, 128), F32),
            pltpu.VMEM((2, 2, 2, GY, 8, 128), F32),
            pltpu.VMEM((2, GY, 2, 8, 128), F32),
            pltpu.VMEM((2, 2, GY, 8, 128), F32),
            pltpu.VMEM((3, 24, 128), F32),
            pltpu.VMEM((3, 8, 24, 128), F32),
            dma((12,)),
            dma((4, GX)),
            dma((4, GX)),
            dma((2, EXTRA)),
            dma((2, GX)),
            dma((2, GX)),
            dma((2, EXTRA)),
            dma((2, 6, GY)),
            dma((2, 4, GY)),
            dma((2, 4, GY)),
            dma((2, 6, GY)),
            dma((3, 8)),
            dma((3, 8)),
        ],
        compiler_params=pltpu.CompilerParams(
            collective_id=0, has_side_effects=True, vmem_limit_bytes=58 * 1024 * 1024
        ),
    )(
        history[0], cotangent[0], w_point, offset.reshape(1, C), weight,
        two(depth_table()), two(xa), two(xs), two(xea), two(xes), two(ya), two(yar), two(ya.T), two(yar.T),
        jnp.asarray(slots.astype(ml_dtypes.bfloat16)),
        jnp.asarray(slots.T.astype(ml_dtypes.bfloat16)),
    )
    act, ghist, gs, gpoint, goff = pl.pallas_call(
        finish,
        out_shape=(
            block, block, jax.ShapeDtypeStruct((2, C, C, KX, Q, MY), F32), square, line,
        ),
        in_specs=[vmem, vmem],
        out_specs=(hbm,) * 3 + (vmem,) * 2,
        scratch_shapes=[
            pltpu.VMEM((C * 16, 256), F32), pltpu.VMEM((2, C, C, KX, Q, MY), F32), dma((2,)), dma((2, GROUPS)),
        ],
        compiler_params=pltpu.CompilerParams(vmem_limit_bytes=60 * 1024 * 1024),
    )(fields, sums)
    grad_spectral = jnp.transpose(gs, (0, 1, 2, 4, 3, 5))
    return act[None], ghist[None], grad_spectral, gpoint, goff.reshape(C)


def solution(mesh):
    grid = P(None, None, "gx", "gy", None)
    modes = P(None, None, None, "gx", "gy", None)
    return jax.shard_map(
        per_device,
        mesh=mesh,
        in_specs=(grid, P(), P(), modes, grid),
        out_specs=(grid, grid, modes, P(), P()),
        check_vma=False,
    )
```

```python
import math

import jax
import jax.numpy as jnp
import ml_dtypes
import numpy as np
from jax import lax
from jax.experimental import pallas as pl
from jax.experimental.pallas import tpu as pltpu
from jax.sharding import PartitionSpec as P

MESH = pl.DeviceIdType.MESH
F32 = jnp.float32
BF16 = jnp.bfloat16
C = 20
NX, NY, NZ, NT = 128, 64, 64, 8
MX, MY, MZ, MT = 24, 24, 16, 8
GX, GY = 32, 8
XC, YC = NX // GX, NY // GY
KX = MX // GY
Q = MZ * MT // GX
ROWS = C * YC
CELLS = NX * NY * NZ * NT
XPOS, ZPOS = 4, 8
EXTRA, STRIDE = 4, 10
gelu_coef = 0.7978845608028654
gelu_cubic = 0.044715


def kept(length, keep):
    half = keep // 2
    return np.concatenate([np.arange(half), length - half + np.arange(half)])


def halves(table):
    table = np.asarray(table, np.float64)
    hi = table.astype(np.float32).astype(ml_dtypes.bfloat16)
    lo = (table - hi.astype(np.float64)).astype(np.float32).astype(ml_dtypes.bfloat16)
    return np.stack([hi, lo])


def handled(h):
    p, s = h // 2, h % 2
    if p == 0:
        return [(NZ - 8, t) for t in ((2, 3) if s == 0 else (6, 7))]
    if p == 8:
        return [(NZ - 8, t) for t in ((0, 1) if s == 0 else (4, 5))]
    if p < 8:
        return [(p, t) for t in ((0, 3) if s == 0 else (4, 7))]
    return [(16 - p, t) for t in ((5, 6) if s == 0 else (1, 2))]


def depth_table():
    z, t = np.arange(NZ)[:, None], np.arange(NT)[None]

    def wave(kz, kt):
        return 2 * np.pi * ((z * kz % NZ) / NZ + (t * kt % NT) / NT).reshape(-1)

    rows = []
    for h in range(GX):
        angles = [wave(*mode) for mode in handled(h)]
        rows += [np.cos(a) for a in angles] + [-np.sin(a) for a in angles]
    rows += [np.cos(wave(0, 0)), np.cos(wave(0, 4))]
    for j in range(1, EXTRA):
        rows += [np.cos(wave(0, j)), -np.sin(wave(0, j))]
    return np.stack(rows + [np.zeros(NZ * NT)] * 8)


def x_tables():
    fx = kept(NX, MX).reshape(GY, KX)
    x = np.arange(NX).reshape(GX, XC).T
    angle = 2 * np.pi * (fx[:, :, None, None] * x[None, None] % NX) / NX
    cos, sin = np.cos(angle), np.sin(angle)
    main = np.zeros((GY, 2, 2, 8, XC, GX, 2, 2))
    extra = np.zeros((2, GY, 2, 8, XC, GX, 2))
    direct = ((cos, sin), (-sin, cos))
    conj = ((cos, -sin), (-sin, -cos))
    for out in range(2):
        for k in range(KX):
            row = KX * out + k
            for into in range(2):
                for m in range(2):
                    main[:, 0, m, row, :, :, into, m] = direct[out][into][:, k]
                    main[:, 1, m, row, :, :, into, m] = conj[out][into][:, k]
                extra[1, :, 0, row, :, :, into] = direct[out][into][:, k]
                extra[1, :, 1, row, :, :, into] = conj[out][into][:, k]
            extra[0, :, 0, row, :, :, 0] = direct[out][0][:, k]
            extra[0, :, 1, row, :, :, 1] = direct[out][0][:, k]

    def tables(full, columns):
        blocks = full.size // (GY * 8 * columns)
        full = full.reshape(GY, blocks, 8, columns)
        tail = np.zeros((4, GY, blocks, 2, columns))
        for g in range(4):
            rows = full[:, :, g:6:4]
            tail[g, :, :, : rows.shape[2]] = rows
        count = GY * blocks * 8
        forward = np.stack([full.reshape(count, columns), tail.reshape(count, columns)])
        backward = np.stack([
            full.swapaxes(0, 1).reshape(count, columns).T,
            tail.swapaxes(1, 2).reshape(count, columns).T,
        ])
        return forward, backward

    forward, backward = tables(main, XC * GX * 4)
    extras = [tables(extra[kind], XC * GX * 2) for kind in range(2)]
    return (
        forward, backward, np.stack([v[0] for v in extras]), np.stack([v[1] for v in extras])
    )


def slot_table():
    out = np.zeros((Q, 8, 160))
    for q in range(Q):
        for ri in range(2):
            for k in range(KX):
                r = KX * ri + k
                at = 16 * ri + 4 * k + q
                out[q, r, at] = 1
                out[q, 6 + r // 4, 32 + 32 * (r % 4) + at] = 1
    return out.reshape(Q * 8, 160)


def y_tables():
    fy = kept(NY, MY)
    angle = 2 * np.pi * (np.arange(NY)[:, None] * fy[None] % NY) / NY
    cos, sin = np.cos(angle), np.sin(angle)
    out = np.zeros((4, 2, NY, 2, 4, 32))
    for g in range(4):
        out[g, 0, :, 0, g, :MY] = cos
        out[g, 1, :, 0, g, :MY] = sin
        out[g, 0, :, 1, g, :MY] = -sin
        out[g, 1, :, 1, g, :MY] = cos
    return out.reshape(8 * NY, 256), out.sum(axis=0).reshape(2 * NY, 256)


def split(value):
    hi = value.astype(BF16)
    return hi, (value - hi.astype(F32)).astype(BF16)


def dot(a, b, dims):
    return lax.dot_general(a, b, (dims, ((), ())), preferred_element_type=F32)


NN = ((1,), (0,))
NTD = ((1,), (1,))


def dot3(a, b, dims=NN):
    return dot(a[0], b[0], dims) + (dot(a[0], b[1], dims) + dot(a[1], b[0], dims))


def exact(a, b, dims=NN):
    return lax.dot_general(
        a, b, (dims, ((), ())), precision=lax.Precision.HIGHEST, preferred_element_type=F32
    )


def swap_groups(parts):
    parts = list(parts)
    group = lax.broadcasted_iota(jnp.int32, parts[0].shape, 1) // 8
    for s in (8, 4, 2, 1):
        low = lax.rem(group // s, 2) == 0
        for i in range(16):
            if i & s:
                continue
            a, b = parts[i], parts[i + s]
            if b is None:
                if a is not None:
                    parts[i] = jnp.where(low, a, 0.0)
                    parts[i + s] = jnp.where(low, pltpu.roll(a, 128 - 8 * s, 1), 0.0)
                continue
            parts[i] = jnp.where(low, a, pltpu.roll(b, 8 * s, 1))
            parts[i + s] = jnp.where(low, pltpu.roll(a, 128 - 8 * s, 1), b)
    return parts


def dot2(a, b):
    return dot(a, b[0], NN) + dot(a, b[1], NN)


def kernel(
    hist_h, cot_h, wpt, off, w_hbm, dtab_h, xa_h, xs_h, xea_h, xes_h, ya_h, yar_h, ys_h, ysr_h, u_h, ut_h,
    fields, sums,
    hist, cot, dtab, xa, xs, xea, xes, ya, yar, ys, ysr, u, ut, w_v, wp, vb, base, gpre, mixed,
    sendx, recvx, sende, recve, sendr, recvr, sendy, recvy, backs, backr, exy, backx, small, smalls,
    load_sem, sx_sem, rx_sem, se_sem, re_sem, sr_sem, rr_sem, sy_sem, ry_sem, sb_sem, rb_sem, ss_sem, rs_sem,
):
    d = lax.axis_index("gx")
    e = lax.axis_index("gy")
    modes, grads = sums.at[0:80], sums.at[80:400]
    half, side = d // 2, lax.rem(d, 2)
    is_a = (d >= 2) & (d < 16)
    is_b = d >= 18
    is_mid = (d >= 16) & (d < 18)
    is_low = d < 2
    special = lax.rem(d, STRIDE) == 0
    which = d // STRIDE
    kind_e = jnp.where(d == 0, 0, 1)
    pair = GX - 2 * half
    mirror = GX + 1 - d

    barrier = pltpu.get_barrier_semaphore()

    def signal(x, y):
        pl.semaphore_signal(barrier, inc=1, device_id=(x, y), device_id_type=MESH)

    def over(count, body, first=0):
        def go(k, carry):
            body(k)
            return carry

        lax.fori_loop(first, count, go, 0)

    over(GX, lambda k: signal((d + k) & (GX - 1), e), 1)
    over(GY, lambda k: signal(d, (e + k) & (GY - 1)), 1)

    loads = [
        pltpu.make_async_copy(src, dst, load_sem.at[i])
        for i, (src, dst) in enumerate((
            (hist_h, hist), (dtab_h, dtab), (cot_h, cot), (w_hbm, w_v), (xa_h, xa), (xs_h, xs), (ya_h, ya), (yar_h, yar), (ys_h, ys), (ysr_h, ysr),
            (u_h, u), (ut_h, ut),
        ))
    ]
    extra_loads = [
        pltpu.make_async_copy(src.at[:, kind_e], dst, load_sem.at[len(loads) + i])
        for i, (src, dst) in enumerate(((xea_h, xea), (xes_h, xes)))
    ]
    for load in loads:
        load.start()

    @pl.when(special)
    def _():
        for load in extra_loads:
            load.start()


    @pl.when(is_low | is_mid)
    def _():
        backr[:, 1] = jnp.zeros_like(backr[:, 1])

    def remote(src, dst, send, recv, x, y):
        return pltpu.make_async_remote_copy(
            src_ref=src, dst_ref=dst, send_sem=send, recv_sem=recv,
            device_id=(x, y), device_id_type=MESH,
        )

    def x_copy(p, peer, slot):
        return remote(
            sendx.at[p, peer], recvx.at[p, slot], sx_sem.at[p, peer], rx_sem.at[p, slot], peer, e
        )

    def start_x(p):
        over(GX, lambda k: x_copy(p, (d + k) & (GX - 1), d).start(), 1)
        recvx[p, d] = sendx[p, d]

    def wait_x(p):
        def go(k):
            peer = (d + GX - k) & (GX - 1)
            x_copy(p, peer, peer).wait_recv()

        over(GX, go, 1)

    def wait_x_sent(p):
        over(GX, lambda k: x_copy(p, (d + k) & (GX - 1), d).wait_send(), 1)

    def e_copy(f, j, slot):
        return remote(
            sende.at[f, j], recve.at[f, slot], se_sem.at[f, j], re_sem.at[f, slot], j * STRIDE, e
        )

    def start_e(f):
        def go(j):
            @pl.when(d != j * STRIDE)
            def _():
                e_copy(f, j, d).start()

        over(EXTRA, go)

        @pl.when(special)
        def _():
            recve[f, d] = sende[f, which]

    def wait_e_sent(f):
        def go(j):
            @pl.when(d != j * STRIDE)
            def _():
                e_copy(f, j, d).wait_send()

        over(EXTRA, go)

    def wait_e(f):
        def go(k):
            peer = (d + GX - k) & (GX - 1)
            remote(
                sende.at[f, 0], recve.at[f, peer], se_sem.at[f, 0], re_sem.at[f, peer], peer, e
            ).wait_recv()

        over(GX, go, 1)

    def r_copy(f, peer, j):
        return remote(
            sendr.at[f, peer], recvr.at[f, j], sr_sem.at[f, peer], rr_sem.at[f, j], peer, e
        )

    def start_r(f):
        over(GX, lambda k: r_copy(f, (d + k) & (GX - 1), which).start(), 1)
        recvr[f, which] = sendr[f, d]

    def wait_r(f):
        def go(j):
            @pl.when(d != j * STRIDE)
            def _():
                r_copy(f, 0, j).wait_recv()

        over(EXTRA, go)

        @pl.when(special)
        def _():
            over(GX, lambda k: r_copy(f, (d + k) & (GX - 1), which).wait_send(), 1)

    def owner_of(part, m):
        if part == 0:
            x = jnp.where(is_a | is_mid, d, jnp.where(is_low, d + 16, mirror))
            slot = jnp.where(is_a, 3 * m, jnp.where(is_b, 1 + m, jnp.where(is_mid, m, 2 + m)))
        else:
            x = jnp.where(is_a, pair + (side + m) % 2, d)
            slot = jnp.where(is_a, m, 3 - m)
        return x, slot

    def each_y(f, act_on):
        def block(part, m, y, k):
            x, slot = owner_of(part, m)

            @pl.when((x != d) | (k != 0))
            def _():
                act_on(remote(
                    sendy.at[f, y, part, m], recvy.at[f, e, slot], sy_sem.at[f, 2 * part + m, y],
                    ry_sem.at[f, slot, e], x, y,
                ))

        def go(k):
            y = (e + k) & (GY - 1)
            for m in range(2):
                block(0, m, y, k)

            @pl.when(is_a | is_b)
            def _():
                for m in range(2):
                    block(1, m, y, k)

        over(GY, go)

    def each_ex(f, act_on):
        def go(k):
            y = (e + k) & (GY - 1)
            for part in range(2):
                slot = which if part == 0 else (4 - which) & 3

                def act_here():
                    act_on(remote(
                        exy.at[f, y, part], recvy.at[f, e, slot], sy_sem.at[f, 4 + part, y],
                        ry_sem.at[f, slot, e], part, y,
                    ))

                if part == 0:
                    pl.when((d != 0) | (k != 0))(act_here)
                else:
                    act_here()

        over(GY, go)

    def start_y(f):
        each_y(f, lambda copy: copy.start())
        for part in range(2):
            for m in range(2):
                x, slot = owner_of(part, m)

                @pl.when((x == d) & ((part == 0) | is_b))
                def _():
                    recvy[f, e, slot] = sendy[f, e, part, m]

    def start_ex(f):
        each_ex(f, lambda copy: copy.start())

        @pl.when(d == 0)
        def _():
            recvy[f, e, 0] = exy[f, e, 0]

    def wait_y(f):
        def go(k):
            y = (e + GY - k) & (GY - 1)
            for slot in range(4):
                own = jnp.where(
                    is_a, slot in (0, 3), jnp.where(is_b, slot >= 2, jnp.where(is_mid, slot < 2, slot == 0))
                ) & (d != 1)

                @pl.when((k != 0) | ~own)
                def _():
                    remote(
                        sendy.at[f, 0, 0, 0], recvy.at[f, y, slot], sy_sem.at[f, 0, 0],
                        ry_sem.at[f, slot, y], d, y,
                    ).wait_recv()

        over(GY, go)

    def maker_of(slot):
        if slot in (1, 2):
            x = mirror
            part, m = 0, slot - 1
        else:
            x = d
            part, m = 0, slot // 3
        if slot < 2:
            xb, mb = pair + (side + slot) % 2, slot
        else:
            xb, mb = d, 3 - slot
        xm, mm = (d, slot) if slot < 2 else (d - 16, slot - 2)
        x = jnp.where(is_b, xb, jnp.where(is_mid, xm, x))
        part = jnp.where(is_b, 1, part)
        m = jnp.where(is_b, mb, jnp.where(is_mid, mm, m))
        return x, part, m

    def each_b(f, act_on):
        def go(k):
            y = (e + k) & (GY - 1)

            @pl.when(d >= 2)
            def _():
                for slot in range(4):
                    x, part, m = maker_of(slot)

                    @pl.when((x != d) | (k != 0))
                    def _():
                        act_on(remote(
                            backs.at[f, y, slot], backr.at[f, part, m, e], sb_sem.at[f, slot, y],
                            rb_sem.at[f, 2 * part + m, e], x, y,
                        ))

            @pl.when(is_low)
            def _():
                for slot in range(4):
                    j = jnp.where(d == 0, slot, (4 - slot) & 3)

                    def act_here():
                        act_on(remote(
                            backs.at[f, y, slot], backx.at[f, side, e], sb_sem.at[f, slot, y],
                            rb_sem.at[f, 4 + side, e], j * STRIDE, y,
                        ))

                    if slot == 0:
                        pl.when((d != 0) | (k != 0))(act_here)
                    else:
                        act_here()

        over(GY, go)

    def start_b(f):
        each_b(f, lambda copy: copy.start())

        @pl.when(d >= 2)
        def _():
            for slot in range(4):
                x, part, m = maker_of(slot)

                @pl.when(x == d)
                def _():
                    backr[f, part, m, e] = backs[f, e, slot]

        @pl.when(d == 0)
        def _():
            backx[f, 0, e] = backs[f, e, 0]

    def wait_b(f):
        def go(k):
            y = (e + GY - k) & (GY - 1)

            def arrived(part, m):
                remote(
                    backs.at[f, 0, 0], backr.at[f, part, m, y], sb_sem.at[f, 0, 0],
                    rb_sem.at[f, 2 * part + m, y], d, y,
                ).wait_recv()

            for m in range(2):
                @pl.when((k != 0) | is_b | is_low)
                def _():
                    arrived(0, m)

                @pl.when(is_a | (is_b & (k != 0)))
                def _():
                    arrived(1, m)

        over(GY, go)

    def wait_sent(f):
        each_y(f, lambda copy: copy.wait_send())
        each_b(f, lambda copy: copy.wait_send())

        @pl.when(special)
        def _():
            each_ex(f, lambda copy: copy.wait_send())

    def wait_b_extra(f):
        def go(k):
            y = (e + GY - k) & (GY - 1)
            for part in range(2):
                def arrived():
                    remote(
                        backs.at[f, 0, 0], backx.at[f, part, y], sb_sem.at[f, 0, 0],
                        rb_sem.at[f, 4 + part, y], d, y,
                    ).wait_recv()

                if part == 0:
                    pl.when((d != 0) | (k != 0))(arrived)
                else:
                    arrived()

        over(GY, go)

    lane128 = lax.broadcasted_iota(jnp.int32, (1, 128), 1)

    def depth_analyse(p, f, get, terms):
        for t in range(XC + 1):
            total = None
            for tab, part in terms:
                if t < XC:
                    rows = get(t, part)[0:128]
                else:
                    rows = jnp.concatenate([get(x, part)[128:ROWS] for x in range(XC)], axis=0)
                term = dot(dtab[tab], rows, NTD)
                total = term if total is None else total + term
            sendx[p, :, t] = total[0:128].reshape(GX, 4, 128)
            sende[f, :, t] = total[128:136].reshape(EXTRA, 2, 128)

    def x_analyse(tiles, tables, out):
        left = tiles[XC]
        count = left.shape[0]
        per = 256 // count
        main, tail = None, None
        for b in range(XC // per):
            xs_here = range(b * per, (b + 1) * per)
            at = slice(b * 256, (b + 1) * 256)
            cols = split(jnp.concatenate([tiles[x] for x in xs_here], axis=0))
            term = dot3((tables[0, 0, :, at], tables[1, 0, :, at]), cols)
            main = term if main is None else main + term
            cols = split(jnp.concatenate(
                [left if x == 0 else pltpu.roll(left, 128 - 32 * x, 1) for x in xs_here], axis=0
            ))
            term = dot3((tables[0, 1, :, at], tables[1, 1, :, at]), cols)
            tail = term if tail is None else tail + term
        blocks = out.shape[:-2]
        size = tail.shape[0] // 4
        out[...] = main.reshape(blocks + (8, 128))
        tail = jnp.where(lane128 < 32, tail, 0.0)
        packed = tail[0:size]
        for g in range(1, 4):
            packed = packed + pltpu.roll(tail[size * g : size * g + size], 32 * g, 1)
        out[..., 6:8, :] = packed.reshape(blocks + (2, 128))

    def analyse_main(p, f):
        x_analyse([recvx[p, :, t].reshape(128, 128) for t in range(XC + 1)], xa, sendy.at[f])

    def analyse_extra(f):
        x_analyse(
            [recve[f, :, t].reshape(64, 128) for t in range(XC + 1)], xea, exy.at[f]
        )

    def y_cells(f):
        cols = split(jnp.concatenate([recvy[f, y].reshape(32, 128) for y in range(GY)], axis=1))
        merged = dot2(ut[...], cols)
        rows = []
        parts = [
            merged[16 * (g // GY) : 16 * (g // GY) + 16, 128 * (g % GY) : 128 * (g % GY) + 128]
            for g in range(16)
        ]
        rows += swap_groups(parts)
        parts = []
        for g in range(16):
            at = 32 + 16 * (g // GY)
            lanes = slice(128 * (g % GY), 128 * (g % GY) + 128)
            total = merged[at : at + 16, lanes]
            for n in range(1, 4):
                total = total + pltpu.roll(merged[at + 32 * n : at + 32 * n + 16, lanes], 128 - 32 * n, 1)
            parts.append(total)
        rows += swap_groups([jnp.where(lane128 < 32, part, 0.0) for part in parts])[: C - 16]
        return rows

    def y_synthesise(f, cols):
        main = swap_groups(cols[:16])
        tail = swap_groups(cols[16:] + [None] * (32 - C))
        stack = []
        for y in range(GY):
            rows = [main[y], main[GY + y]]
            for n in range(4):
                for g in (y, GY + y):
                    rows.append(tail[g] if n == 0 else pltpu.roll(tail[g], 32 * n, 1))
            stack.append(jnp.concatenate(rows, axis=0))
        out = dot2(u[...], split(jnp.concatenate(stack, axis=1)))
        for y in range(GY):
            backs[f, y] = out[:, 128 * y : 128 * y + 128].reshape(4, 8, 128)

    def x_synthesise(slots, tables, put):
        rows = slots[...]
        count = math.prod(rows.shape[:-2])
        main_cols = split(rows.reshape(count * 8, 128))
        tail = rows[..., 6:8, :].reshape(count * 2, 128)
        tail_cols = split(jnp.concatenate(
            [tail] + [pltpu.roll(tail, 128 - 32 * g, 1) for g in range(1, 4)], axis=0
        ))
        main = dot3((tables[0, 0], tables[1, 0]), main_cols)
        tail = dot3((tables[0, 1], tables[1, 1]), tail_cols)
        tail = jnp.where(lane128 < 32, tail, 0.0)
        per = main.shape[0] // XC
        left = None
        for x in range(XC):
            at = slice(per * x, per * x + per)
            put(x, main[at])
            part = tail[at]
            left = part if x == 0 else left + pltpu.roll(part, 32 * x, 1)
        put(XC, left)

    def synthesise_main(f, p):
        def put(t, rows):
            sendx[p, :, t] = rows.reshape(GX, 4, 128)

        x_synthesise(backr.at[f], xs, put)

    def synthesise_extra(f):
        def put(t, rows):
            sendr[f, :, t] = rows.reshape(GX, 2, 128)

        x_synthesise(backx.at[f], xes, put)

    def depth_rows(p, f, t):
        tile = recvx[p, :, t].reshape(128, 128)
        extra = recvr[f, :, t].reshape(8, 128)
        rest = jnp.zeros((120, 128), F32)
        low = jnp.concatenate([extra, rest], axis=0).T
        return jnp.concatenate([tile.T, low[:, 0:16]], axis=1)

    def depth_synthesise(p, f, x, left):
        cols = jnp.concatenate([depth_rows(p, f, x), left[32 * x : 32 * x + 32]], axis=0)
        return dot3(split(cols), (dtab[0], dtab[1])) * (1.0 / CELLS)

    def send_main_then_extra(p, f):
        @pl.when(special)
        def _():
            wait_e(f)
            analyse_extra(f)
            start_ex(f)

        wait_x(p)
        analyse_main(p, f)
        start_y(f)

    def cells_back(f, p):
        @pl.when(special)
        def _():
            wait_b_extra(f)
            synthesise_extra(f)
            start_r(f)

        wait_b(f)
        synthesise_main(f, p)
        start_x(p)

    loads[0].wait()
    for x in range(XC):
        vb[x] = hist[:, x].astype(F32).reshape(ROWS, 512).astype(BF16)
    loads[1].wait()
    depth_analyse(0, 0, lambda x, part: vb[x], ((0, 0), (1, 0)))

    pl.semaphore_wait(barrier, GX + GY - 2)
    start_e(0)
    start_x(0)

    for load in loads[2:]:
        load.wait()

    @pl.when(special)
    def _():
        for load in extra_loads:
            load.wait()

    wp[...] = jnp.zeros_like(wp)

    def pack(o):
        for r in range(2):
            for i in range(C):
                lanes = slice(32 * (i % 4), 32 * (i % 4) + MY)
                for k in range(KX):
                    wp[r, o, i // 4, 4 * k : 4 * k + 4, lanes] = w_v[r, o, i, k]

    over(C, pack)

    spread = (
        lax.broadcasted_iota(jnp.int32, (ROWS, C), 0) // YC
        == lax.broadcasted_iota(jnp.int32, (ROWS, C), 1)
    ).astype(F32)
    same_y = lax.rem(lax.broadcasted_iota(jnp.int32, (ROWS, ROWS), 0), YC) == lax.rem(
        lax.broadcasted_iota(jnp.int32, (ROWS, ROWS), 1), YC
    )
    wide = exact(exact(spread, wpt[...]), spread, NTD)
    point = split(jnp.where(same_y, wide, 0.0))
    wide_t = exact(exact(spread, wpt[...], ((1,), (1,))), spread, NTD)
    point_t = split(jnp.where(same_y, wide_t, 0.0))
    bias = jnp.sum(spread * off[...], axis=1, keepdims=True)
    for x in range(XC):
        base[x] = dot(point[0], vb[x], NN) + dot(point[1], vb[x], NN) + bias

    send_main_then_extra(0, 0)
    wait_y(0)
    cells = y_cells(0)
    cells = jnp.concatenate(
        [jnp.concatenate(cells[i : i + 4], axis=1) for i in range(0, C, 4)], axis=0
    )
    modes[...] = dot3(split(cells), (ya[0], ya[1]))

    def mix(o):
        real = jnp.zeros((16, 128), F32)
        imag = jnp.zeros((16, 128), F32)
        for i in range(C // 4):
            wr, wi = wp[0, o, i], wp[1, o, i]
            mr, mi = modes[16 * i : 16 * i + 16, 0:128], modes[16 * i : 16 * i + 16, 128:256]
            real += wr * mr - wi * mi
            imag += wr * mi + wi * mr
        at = pl.ds(pl.multiple_of(o * 16, 16), 16)
        mixed[at, 0:128] = real
        mixed[at, 128:256] = imag

    over(C, mix)
    cols = dot3(split(mixed[...]), (ysr[0], ysr[1]))
    y_synthesise(0, [cols[16 * c : 16 * c + 16] for c in range(C)])
    start_b(0)
    cells_back(0, 1)
    wait_x(1)
    wait_r(0)

    left = depth_rows(1, 0, XC)
    row_sum = jnp.zeros((ROWS, 1), F32)
    for x in range(XC):
        pre = depth_synthesise(1, 0, x, left) + base[x]
        inner = gelu_coef * (pre + gelu_cubic * pre * pre * pre)
        smooth = jnp.tanh(inner)
        slope = 0.5 * (1.0 + smooth) + 0.5 * pre * (1.0 - smooth * smooth) * gelu_coef * (
            1.0 + 3.0 * gelu_cubic * pre * pre
        )
        fields[0, :, x] = (0.5 * pre * (1.0 + smooth)).reshape(C, YC, 512).astype(BF16)
        grad = cot[:, x].astype(F32).reshape(ROWS, 512) * slope
        row_sum += jnp.sum(grad, axis=1, keepdims=True)
        hi, lo = split(grad)
        gpre[0, x] = hi
        gpre[1, x] = lo
    depth_analyse(2, 1, lambda x, part: gpre[part, x], ((0, 0), (0, 1), (1, 0)))
    start_e(1)
    start_x(2)
    wait_sent(0)
    wait_x_sent(0)
    wait_x_sent(1)

    cross = jnp.zeros((ROWS, ROWS), F32)
    for x in range(XC):
        g = (gpre[0, x], gpre[1, x])
        base[x] = dot3(point_t, g)
        cross += dot(g[0], vb[x], NTD) + dot(g[1], vb[x], NTD)
    gather = (
        lax.broadcasted_iota(jnp.int32, (24, ROWS), 1) // YC
        == lax.broadcasted_iota(jnp.int32, (24, ROWS), 0)
    ).astype(F32)
    place = (
        lax.broadcasted_iota(jnp.int32, (ROWS, 128), 0) // YC
        == lax.broadcasted_iota(jnp.int32, (ROWS, 128), 1)
    ).astype(F32)
    lane = lax.broadcasted_iota(jnp.int32, (ROWS, 128), 1)
    both = exact(jnp.where(same_y, cross, 0.0), place) + jnp.where(lane == C, row_sum, 0.0)
    small[0] = exact(gather, both)

    def small_copy(s, k, peer, slot):
        return remote(small.at[s], smalls.at[s, slot], ss_sem.at[s, k], rs_sem.at[s, slot], *peer)

    xpos, zpos = d // ZPOS, lax.rem(d, ZPOS)
    steps = (
        (GY, e, lambda i: (d, i)),
        (XPOS, xpos, lambda i: (i * ZPOS + zpos, e)),
        (ZPOS, zpos, lambda i: (xpos * ZPOS + i, e)),
    )

    def start_small(s):
        count, me, peer_of = steps[s]
        for k in range(1, count):
            small_copy(s, k, peer_of(lax.rem(me + k, count)), me).start()
        smalls[s, me] = small[s]

    def finish_small(s):
        count, me, peer_of = steps[s]
        for k in range(1, count):
            other = lax.rem(me + count - k, count)
            copy = small_copy(s, k, peer_of(other), other)
            copy.wait_recv()
            copy.wait_send()
        total = smalls[s, 0]
        for k in range(1, count):
            total = total + smalls[s, k]
        return total

    start_small(0)
    send_main_then_extra(2, 1)
    small[1] = finish_small(0)
    start_small(1)
    wait_y(1)
    grads[...] = dot3(split(jnp.concatenate(y_cells(1), axis=0)), (yar[0], yar[1]))

    def mix_back(j):
        real = jnp.zeros((16, 128), F32)
        imag = jnp.zeros((16, 128), F32)
        for o in range(C):
            wr, wi = wp[0, o, j], wp[1, o, j]
            gr, gi = grads[16 * o : 16 * o + 16, 0:128], grads[16 * o : 16 * o + 16, 128:256]
            real += wr * gr + wi * gi
            imag += wr * gi - wi * gr
        at = pl.ds(pl.multiple_of(j * 16, 16), 16)
        mixed[at, 0:128] = real
        mixed[at, 128:256] = imag

    over(C // 4, mix_back)
    cols = dot3(split(mixed[0:80]), (ys[0], ys[1]))
    y_synthesise(1, [
        cols[16 * (c // 4) : 16 * (c // 4) + 16, 128 * (c % 4) : 128 * (c % 4) + 128] for c in range(C)
    ])
    start_b(1)
    small[2] = finish_small(1)
    start_small(2)
    cells_back(1, 3)

    total = finish_small(2)
    sums[400:424, 0:128] = total
    sums[400:424, 128:256] = jnp.zeros_like(total)

    wait_sent(1)
    wait_x_sent(2)
    wait_x(3)
    wait_r(1)
    left = depth_rows(3, 1, XC)
    for x in range(XC):
        total = depth_synthesise(3, 1, x, left) + base[x]
        fields[1, :, x] = total.reshape(C, YC, 512).astype(BF16)
    wait_x_sent(3)
    wait_e_sent(0)
    wait_e_sent(1)


GROUPS = 5


def finish(fields, sums, act, ghist, gs, gpoint, goff, modes, gs_v, io_sem, gs_sem):
    grads = sums.at[80:400]
    copies = [
        pltpu.make_async_copy(fields.at[0], act, io_sem.at[0]),
        pltpu.make_async_copy(fields.at[1], ghist, io_sem.at[1]),
    ]
    for copy in copies:
        copy.start()
    gpoint[...] = sums[400 : 400 + C, 0:C]
    column = sums[400 : 400 + C, C : C + 1]
    diagonal = lax.broadcasted_iota(jnp.int32, (C, C), 0) == lax.broadcasted_iota(
        jnp.int32, (C, C), 1
    )
    goff[...] = jnp.sum(jnp.where(diagonal, column, 0.0), axis=0, keepdims=True)

    for j in range(C):
        for half in range(2):
            lanes = slice(128 * half, 128 * half + 128)
            tile = sums[16 * (j // 4) : 16 * (j // 4) + 16, lanes]
            modes[16 * j : 16 * j + 16, lanes] = tile if j % 4 == 0 else pltpu.roll(tile, 128 - 32 * (j % 4), 1)

    def row(o, carry):
        at = pl.ds(pl.multiple_of(o * 16, 16), 16)
        gr = grads[at, 0:128] * (1.0 / CELLS)
        gi = grads[at, 128:256] * (1.0 / CELLS)
        for j in range(C):
            mr, mi = modes[16 * j : 16 * j + 16, 0:128], modes[16 * j : 16 * j + 16, 128:256]
            real = gr * mr + gi * mi
            imag = gi * mr - gr * mi
            for k in range(KX):
                gs_v[0, o, j, k] = real[4 * k : 4 * k + 4, 0:MY]
                gs_v[1, o, j, k] = imag[4 * k : 4 * k + 4, 0:MY]
        return carry

    size = C // GROUPS
    for b in range(GROUPS):
        lax.fori_loop(b * size, (b + 1) * size, row, 0)
        for r in range(2):
            at = pl.ds(b * size, size)
            copy = pltpu.make_async_copy(gs_v.at[r, at], gs.at[r, at], gs_sem.at[r, b])
            copy.start()
            copies.append(copy)
    for copy in copies:
        copy.wait()


def per_device(history, w_point, offset, spectral_weight, cotangent):
    def two(table):
        return jnp.asarray(halves(table))

    xa, xs, xea, xes = x_tables()
    ya, yar = y_tables()
    slots = slot_table()
    weight = jnp.transpose(spectral_weight, (0, 1, 2, 4, 3, 5))
    vmem = pl.BlockSpec(memory_space=pltpu.VMEM)
    hbm = pl.BlockSpec(memory_space=pl.ANY)
    block = jax.ShapeDtypeStruct((C, XC, YC, NZ * NT), BF16)
    square = jax.ShapeDtypeStruct((C, C), F32)
    line = jax.ShapeDtypeStruct((1, C), F32)
    dma = pltpu.SemaphoreType.DMA
    fields, sums = pl.pallas_call(
        kernel,
        out_shape=(jax.ShapeDtypeStruct((2,) + block.shape, BF16), jax.ShapeDtypeStruct((424, 256), F32)),
        in_specs=[hbm] * 2 + [vmem] * 2 + [hbm] * 12,
        out_specs=(vmem,) * 2,
        scratch_shapes=[
            pltpu.VMEM(block.shape, BF16),
            pltpu.VMEM(block.shape, BF16),
            pltpu.VMEM((2, 144, 512), BF16),
            pltpu.VMEM((2, 2, 256, 512), BF16),
            pltpu.VMEM((2, 2, 512, 256), BF16),
            pltpu.VMEM((2, 2, 128, 256), BF16),
            pltpu.VMEM((2, 2, 256, 128), BF16),
            pltpu.VMEM((2, 512, 256), BF16),
            pltpu.VMEM((2, 128, 256), BF16),
            pltpu.VMEM((2, 256, 512), BF16),
            pltpu.VMEM((2, 256, 128), BF16),
            pltpu.VMEM((32, 160), BF16),
            pltpu.VMEM((160, 32), BF16),
            pltpu.VMEM((2, C, C, KX, Q, MY), F32),
            pltpu.VMEM((2, C, C // 4, 16, 128), F32),
            pltpu.VMEM((XC, ROWS, 512), BF16),
            pltpu.VMEM((XC, ROWS, 512), F32),
            pltpu.VMEM((2, XC, ROWS, 512), BF16),
            pltpu.VMEM((C * 16, 256), F32),
            pltpu.VMEM((4, GX, XC + 1, 4, 128), F32),
            pltpu.VMEM((4, GX, XC + 1, 4, 128), F32),
            pltpu.VMEM((2, EXTRA, XC + 1, 2, 128), F32),
            pltpu.VMEM((2, GX, XC + 1, 2, 128), F32),
            pltpu.VMEM((2, GX, XC + 1, 2, 128), F32),
            pltpu.VMEM((2, EXTRA, XC + 1, 2, 128), F32),
            pltpu.VMEM((2, GY, 2, 2, 8, 128), F32),
            pltpu.VMEM((2, GY, Q, 8, 128), F32),
            pltpu.VMEM((2, GY, Q, 8, 128), F32),
            pltpu.VMEM((2, 2, 2, GY, 8, 128), F32),
            pltpu.VMEM((2, GY, 2, 8, 128), F32),
            pltpu.VMEM((2, 2, GY, 8, 128), F32),
            pltpu.VMEM((3, 24, 128), F32),
            pltpu.VMEM((3, 8, 24, 128), F32),
            dma((14,)),
            dma((4, GX)),
            dma((4, GX)),
            dma((2, EXTRA)),
            dma((2, GX)),
            dma((2, GX)),
            dma((2, EXTRA)),
            dma((2, 6, GY)),
            dma((2, 4, GY)),
            dma((2, 4, GY)),
            dma((2, 6, GY)),
            dma((3, 8)),
            dma((3, 8)),
        ],
        compiler_params=pltpu.CompilerParams(
            collective_id=0, has_side_effects=True, vmem_limit_bytes=58 * 1024 * 1024
        ),
    )(
        history[0], cotangent[0], w_point, offset.reshape(1, C), weight,
        two(depth_table()), two(xa), two(xs), two(xea), two(xes), two(ya), two(yar), two(ya.T), two(yar.T),
        jnp.asarray(slots.astype(ml_dtypes.bfloat16)),
        jnp.asarray(slots.T.astype(ml_dtypes.bfloat16)),
    )
    act, ghist, gs, gpoint, goff = pl.pallas_call(
        finish,
        out_shape=(
            block, block, jax.ShapeDtypeStruct((2, C, C, KX, Q, MY), F32), square, line,
        ),
        in_specs=[vmem, vmem],
        out_specs=(hbm,) * 3 + (vmem,) * 2,
        scratch_shapes=[
            pltpu.VMEM((C * 16, 256), F32), pltpu.VMEM((2, C, C, KX, Q, MY), F32), dma((2,)), dma((2, GROUPS)),
        ],
        compiler_params=pltpu.CompilerParams(vmem_limit_bytes=60 * 1024 * 1024),
    )(fields, sums)
    grad_spectral = jnp.transpose(gs, (0, 1, 2, 4, 3, 5))
    return act[None], ghist[None], grad_spectral, gpoint, goff.reshape(C)


def solution(mesh):
    grid = P(None, None, "gx", "gy", None)
    modes = P(None, None, None, "gx", "gy", None)
    return jax.shard_map(
        per_device,
        mesh=mesh,
        in_specs=(grid, P(), P(), modes, grid),
        out_specs=(grid, grid, modes, P(), P()),
        check_vma=False,
    )
```

```python
import math

import jax
import jax.numpy as jnp
import ml_dtypes
import numpy as np
from jax import lax
from jax.experimental import pallas as pl
from jax.experimental.pallas import tpu as pltpu
from jax.sharding import PartitionSpec as P

MESH = pl.DeviceIdType.MESH
F32 = jnp.float32
BF16 = jnp.bfloat16
C = 20
NX, NY, NZ, NT = 128, 64, 64, 8
MX, MY, MZ, MT = 24, 24, 16, 8
GX, GY = 32, 8
XC, YC = NX // GX, NY // GY
KX = MX // GY
Q = MZ * MT // GX
ROWS = C * YC
CELLS = NX * NY * NZ * NT
XPOS, ZPOS = 4, 8
EXTRA, STRIDE = 4, 10
gelu_coef = 0.7978845608028654
gelu_cubic = 0.044715


def kept(length, keep):
    half = keep // 2
    return np.concatenate([np.arange(half), length - half + np.arange(half)])


def halves(table):
    table = np.asarray(table, np.float64)
    hi = table.astype(np.float32).astype(ml_dtypes.bfloat16)
    lo = (table - hi.astype(np.float64)).astype(np.float32).astype(ml_dtypes.bfloat16)
    return np.stack([hi, lo])


def handled(h):
    p, s = h // 2, h % 2
    if p == 0:
        return [(NZ - 8, t) for t in ((2, 3) if s == 0 else (6, 7))]
    if p == 8:
        return [(NZ - 8, t) for t in ((0, 1) if s == 0 else (4, 5))]
    if p < 8:
        return [(p, t) for t in ((0, 3) if s == 0 else (4, 7))]
    return [(16 - p, t) for t in ((5, 6) if s == 0 else (1, 2))]


def depth_table():
    z, t = np.arange(NZ)[:, None], np.arange(NT)[None]

    def wave(kz, kt):
        return 2 * np.pi * ((z * kz % NZ) / NZ + (t * kt % NT) / NT).reshape(-1)

    rows = []
    for h in range(GX):
        angles = [wave(*mode) for mode in handled(h)]
        rows += [np.cos(a) for a in angles] + [-np.sin(a) for a in angles]
    rows += [np.cos(wave(0, 0)), np.cos(wave(0, 4))]
    for j in range(1, EXTRA):
        rows += [np.cos(wave(0, j)), -np.sin(wave(0, j))]
    return np.stack(rows + [np.zeros(NZ * NT)] * 8)


def x_tables():
    fx = kept(NX, MX).reshape(GY, KX)
    x = np.arange(NX).reshape(GX, XC).T
    angle = 2 * np.pi * (fx[:, :, None, None] * x[None, None] % NX) / NX
    cos, sin = np.cos(angle), np.sin(angle)
    main = np.zeros((GY, 2, 2, 8, XC, GX, 2, 2))
    extra = np.zeros((2, GY, 2, 8, XC, GX, 2))
    direct = ((cos, sin), (-sin, cos))
    conj = ((cos, -sin), (-sin, -cos))
    for out in range(2):
        for k in range(KX):
            row = KX * out + k
            for into in range(2):
                for m in range(2):
                    main[:, 0, m, row, :, :, into, m] = direct[out][into][:, k]
                    main[:, 1, m, row, :, :, into, m] = conj[out][into][:, k]
                extra[1, :, 0, row, :, :, into] = direct[out][into][:, k]
                extra[1, :, 1, row, :, :, into] = conj[out][into][:, k]
            extra[0, :, 0, row, :, :, 0] = direct[out][0][:, k]
            extra[0, :, 1, row, :, :, 1] = direct[out][0][:, k]

    def tables(full, columns):
        blocks = full.size // (GY * 8 * columns)
        full = full.reshape(GY, blocks, 8, columns)
        tail = np.zeros((4, GY, blocks, 2, columns))
        for g in range(4):
            rows = full[:, :, g:6:4]
            tail[g, :, :, : rows.shape[2]] = rows
        count = GY * blocks * 8
        forward = np.stack([full.reshape(count, columns), tail.reshape(count, columns)])
        backward = np.stack([
            full.swapaxes(0, 1).reshape(count, columns).T,
            tail.swapaxes(1, 2).reshape(count, columns).T,
        ])
        return forward, backward

    forward, backward = tables(main, XC * GX * 4)
    extras = [tables(extra[kind], XC * GX * 2) for kind in range(2)]
    return (
        forward, backward, np.stack([v[0] for v in extras]), np.stack([v[1] for v in extras])
    )


def slot_table():
    out = np.zeros((Q, 8, 160))
    for q in range(Q):
        for ri in range(2):
            for k in range(KX):
                r = KX * ri + k
                at = 16 * ri + 4 * k + q
                out[q, r, at] = 1
                out[q, 6 + r // 4, 32 + 32 * (r % 4) + at] = 1
    return out.reshape(Q * 8, 160)


def y_tables():
    fy = kept(NY, MY)
    angle = 2 * np.pi * (np.arange(NY)[:, None] * fy[None] % NY) / NY
    cos, sin = np.cos(angle), np.sin(angle)
    out = np.zeros((4, 2, NY, 2, 4, 32))
    for g in range(4):
        out[g, 0, :, 0, g, :MY] = cos
        out[g, 1, :, 0, g, :MY] = sin
        out[g, 0, :, 1, g, :MY] = -sin
        out[g, 1, :, 1, g, :MY] = cos
    return out.reshape(8 * NY, 256), out.sum(axis=0).reshape(2 * NY, 256)


def split(value):
    hi = value.astype(BF16)
    return hi, (value - hi.astype(F32)).astype(BF16)


def dot(a, b, dims):
    return lax.dot_general(a, b, (dims, ((), ())), preferred_element_type=F32)


NN = ((1,), (0,))
NTD = ((1,), (1,))


def dot3(a, b, dims=NN):
    return dot(a[0], b[0], dims) + (dot(a[0], b[1], dims) + dot(a[1], b[0], dims))


def exact(a, b, dims=NN):
    return lax.dot_general(
        a, b, (dims, ((), ())), precision=lax.Precision.HIGHEST, preferred_element_type=F32
    )


def swap_groups(parts):
    parts = list(parts)
    group = lax.broadcasted_iota(jnp.int32, parts[0].shape, 1) // 8
    for s in (8, 4, 2, 1):
        low = lax.rem(group // s, 2) == 0
        for i in range(16):
            if i & s:
                continue
            a, b = parts[i], parts[i + s]
            if b is None:
                if a is not None:
                    parts[i] = jnp.where(low, a, 0.0)
                    parts[i + s] = jnp.where(low, pltpu.roll(a, 128 - 8 * s, 1), 0.0)
                continue
            parts[i] = jnp.where(low, a, pltpu.roll(b, 8 * s, 1))
            parts[i + s] = jnp.where(low, pltpu.roll(a, 128 - 8 * s, 1), b)
    return parts


def dot2(a, b):
    return dot(a, b[0], NN) + dot(a, b[1], NN)


def kernel(
    hist_h, cot_h, wpt, off, w_hbm, dtab_h, xa_h, xs_h, xea_h, xes_h, ya_h, yar_h, ys_h, ysr_h, u_h, ut_h,
    fields, sums,
    hist, cot, dtab, xa, xs, xea, xes, ya, yar, ys, ysr, u, ut, w_v, wp, vb, base, gpre, mixed,
    sendx, recvx, sende, recve, sendr, recvr, sendy, recvy, backs, backr, exy, backx, small, smalls,
    load_sem, sx_sem, rx_sem, se_sem, re_sem, sr_sem, rr_sem, sy_sem, ry_sem, sb_sem, rb_sem, ss_sem, rs_sem,
):
    d = lax.axis_index("gx")
    e = lax.axis_index("gy")
    modes, grads = sums.at[0:80], sums.at[80:400]
    half, side = d // 2, lax.rem(d, 2)
    is_a = (d >= 2) & (d < 16)
    is_b = d >= 18
    is_mid = (d >= 16) & (d < 18)
    is_low = d < 2
    special = lax.rem(d, STRIDE) == 0
    which = d // STRIDE
    kind_e = jnp.where(d == 0, 0, 1)
    pair = GX - 2 * half
    mirror = GX + 1 - d

    barrier = pltpu.get_barrier_semaphore()

    def signal(x, y):
        pl.semaphore_signal(barrier, inc=1, device_id=(x, y), device_id_type=MESH)

    def over(count, body, first=0):
        def go(k, carry):
            body(k)
            return carry

        lax.fori_loop(first, count, go, 0)

    over(GX, lambda k: signal((d + k) & (GX - 1), e), 1)
    over(GY, lambda k: signal(d, (e + k) & (GY - 1)), 1)

    loads = [
        pltpu.make_async_copy(src, dst, load_sem.at[i])
        for i, (src, dst) in enumerate((
            (hist_h, hist), (dtab_h, dtab), (cot_h, cot), (w_hbm, w_v), (xa_h, xa), (xs_h, xs), (ya_h, ya), (yar_h, yar), (ys_h, ys), (ysr_h, ysr),
            (u_h, u), (ut_h, ut),
        ))
    ]
    extra_loads = [
        pltpu.make_async_copy(src.at[:, kind_e], dst, load_sem.at[len(loads) + i])
        for i, (src, dst) in enumerate(((xea_h, xea), (xes_h, xes)))
    ]
    for load in loads:
        load.start()

    @pl.when(special)
    def _():
        for load in extra_loads:
            load.start()


    @pl.when(is_low | is_mid)
    def _():
        backr[:, 1] = jnp.zeros_like(backr[:, 1])

    def remote(src, dst, send, recv, x, y):
        return pltpu.make_async_remote_copy(
            src_ref=src, dst_ref=dst, send_sem=send, recv_sem=recv,
            device_id=(x, y), device_id_type=MESH,
        )

    def x_copy(p, peer, slot):
        return remote(
            sendx.at[p, peer], recvx.at[p, slot], sx_sem.at[p, peer], rx_sem.at[p, slot], peer, e
        )

    def start_x(p):
        over(GX, lambda k: x_copy(p, (d + k) & (GX - 1), d).start(), 1)
        recvx[p, d] = sendx[p, d]

    def wait_x(p):
        def go(k):
            peer = (d + GX - k) & (GX - 1)
            x_copy(p, peer, peer).wait_recv()

        over(GX, go, 1)

    def wait_x_sent(p):
        over(GX, lambda k: x_copy(p, (d + k) & (GX - 1), d).wait_send(), 1)

    def e_copy(f, j, slot):
        return remote(
            sende.at[f, j], recve.at[f, slot], se_sem.at[f, j], re_sem.at[f, slot], j * STRIDE, e
        )

    def start_e(f):
        def go(j):
            @pl.when(d != j * STRIDE)
            def _():
                e_copy(f, j, d).start()

        over(EXTRA, go)

        @pl.when(special)
        def _():
            recve[f, d] = sende[f, which]

    def wait_e_sent(f):
        def go(j):
            @pl.when(d != j * STRIDE)
            def _():
                e_copy(f, j, d).wait_send()

        over(EXTRA, go)

    def wait_e(f):
        def go(k):
            peer = (d + GX - k) & (GX - 1)
            remote(
                sende.at[f, 0], recve.at[f, peer], se_sem.at[f, 0], re_sem.at[f, peer], peer, e
            ).wait_recv()

        over(GX, go, 1)

    def r_copy(f, peer, j):
        return remote(
            sendr.at[f, peer], recvr.at[f, j], sr_sem.at[f, peer], rr_sem.at[f, j], peer, e
        )

    def start_r(f):
        over(GX, lambda k: r_copy(f, (d + k) & (GX - 1), which).start(), 1)
        recvr[f, which] = sendr[f, d]

    def wait_r(f):
        def go(j):
            @pl.when(d != j * STRIDE)
            def _():
                r_copy(f, 0, j).wait_recv()

        over(EXTRA, go)

    def wait_r_sent(f):
        @pl.when(special)
        def _():
            over(GX, lambda k: r_copy(f, (d + k) & (GX - 1), which).wait_send(), 1)

    def owner_of(part, m):
        if part == 0:
            x = jnp.where(is_a | is_mid, d, jnp.where(is_low, d + 16, mirror))
            slot = jnp.where(is_a, 3 * m, jnp.where(is_b, 1 + m, jnp.where(is_mid, m, 2 + m)))
        else:
            x = jnp.where(is_a, pair + (side + m) % 2, d)
            slot = jnp.where(is_a, m, 3 - m)
        return x, slot

    def each_y(f, act_on):
        def block(part, m, y, k):
            x, slot = owner_of(part, m)

            @pl.when((x != d) | (k != 0))
            def _():
                act_on(remote(
                    sendy.at[f, y, part, m], recvy.at[f, e, slot], sy_sem.at[f, 2 * part + m, y],
                    ry_sem.at[f, slot, e], x, y,
                ))

        def go(k):
            y = (e + k) & (GY - 1)
            for m in range(2):
                block(0, m, y, k)

            @pl.when(is_a | is_b)
            def _():
                for m in range(2):
                    block(1, m, y, k)

        over(GY, go)

    def each_ex(f, act_on):
        def go(k):
            y = (e + k) & (GY - 1)
            for part in range(2):
                slot = which if part == 0 else (4 - which) & 3

                def act_here():
                    act_on(remote(
                        exy.at[f, y, part], recvy.at[f, e, slot], sy_sem.at[f, 4 + part, y],
                        ry_sem.at[f, slot, e], part, y,
                    ))

                if part == 0:
                    pl.when((d != 0) | (k != 0))(act_here)
                else:
                    act_here()

        over(GY, go)

    def start_y(f):
        each_y(f, lambda copy: copy.start())
        for part in range(2):
            for m in range(2):
                x, slot = owner_of(part, m)

                @pl.when((x == d) & ((part == 0) | is_b))
                def _():
                    recvy[f, e, slot] = sendy[f, e, part, m]

    def start_ex(f):
        each_ex(f, lambda copy: copy.start())

        @pl.when(d == 0)
        def _():
            recvy[f, e, 0] = exy[f, e, 0]

    def wait_y(f):
        def go(k):
            y = (e + GY - k) & (GY - 1)
            for slot in range(4):
                own = jnp.where(
                    is_a, slot in (0, 3), jnp.where(is_b, slot >= 2, jnp.where(is_mid, slot < 2, slot == 0))
                ) & (d != 1)

                @pl.when((k != 0) | ~own)
                def _():
                    remote(
                        sendy.at[f, 0, 0, 0], recvy.at[f, y, slot], sy_sem.at[f, 0, 0],
                        ry_sem.at[f, slot, y], d, y,
                    ).wait_recv()

        over(GY, go)

    def maker_of(slot):
        if slot in (1, 2):
            x = mirror
            part, m = 0, slot - 1
        else:
            x = d
            part, m = 0, slot // 3
        if slot < 2:
            xb, mb = pair + (side + slot) % 2, slot
        else:
            xb, mb = d, 3 - slot
        xm, mm = (d, slot) if slot < 2 else (d - 16, slot - 2)
        x = jnp.where(is_b, xb, jnp.where(is_mid, xm, x))
        part = jnp.where(is_b, 1, part)
        m = jnp.where(is_b, mb, jnp.where(is_mid, mm, m))
        return x, part, m

    def each_b(f, act_on):
        def go(k):
            y = (e + k) & (GY - 1)

            @pl.when(d >= 2)
            def _():
                for slot in range(4):
                    x, part, m = maker_of(slot)

                    @pl.when((x != d) | (k != 0))
                    def _():
                        act_on(remote(
                            backs.at[f, y, slot], backr.at[f, part, m, e], sb_sem.at[f, slot, y],
                            rb_sem.at[f, 2 * part + m, e], x, y,
                        ))

            @pl.when(is_low)
            def _():
                for slot in range(4):
                    j = jnp.where(d == 0, slot, (4 - slot) & 3)

                    def act_here():
                        act_on(remote(
                            backs.at[f, y, slot], backx.at[f, side, e], sb_sem.at[f, slot, y],
                            rb_sem.at[f, 4 + side, e], j * STRIDE, y,
                        ))

                    if slot == 0:
                        pl.when((d != 0) | (k != 0))(act_here)
                    else:
                        act_here()

        over(GY, go)

    def start_b(f):
        each_b(f, lambda copy: copy.start())

        @pl.when(d >= 2)
        def _():
            for slot in range(4):
                x, part, m = maker_of(slot)

                @pl.when(x == d)
                def _():
                    backr[f, part, m, e] = backs[f, e, slot]

        @pl.when(d == 0)
        def _():
            backx[f, 0, e] = backs[f, e, 0]

    def wait_b(f):
        def go(k):
            y = (e + GY - k) & (GY - 1)

            def arrived(part, m):
                remote(
                    backs.at[f, 0, 0], backr.at[f, part, m, y], sb_sem.at[f, 0, 0],
                    rb_sem.at[f, 2 * part + m, y], d, y,
                ).wait_recv()

            for m in range(2):
                @pl.when((k != 0) | is_b | is_low)
                def _():
                    arrived(0, m)

                @pl.when(is_a | (is_b & (k != 0)))
                def _():
                    arrived(1, m)

        over(GY, go)

    def wait_sent(f):
        each_y(f, lambda copy: copy.wait_send())
        each_b(f, lambda copy: copy.wait_send())

        @pl.when(special)
        def _():
            each_ex(f, lambda copy: copy.wait_send())

    def wait_b_extra(f):
        def go(k):
            y = (e + GY - k) & (GY - 1)
            for part in range(2):
                def arrived():
                    remote(
                        backs.at[f, 0, 0], backx.at[f, part, y], sb_sem.at[f, 0, 0],
                        rb_sem.at[f, 4 + part, y], d, y,
                    ).wait_recv()

                if part == 0:
                    pl.when((d != 0) | (k != 0))(arrived)
                else:
                    arrived()

        over(GY, go)

    lane128 = lax.broadcasted_iota(jnp.int32, (1, 128), 1)

    def depth_analyse(p, f, get, terms):
        for t in range(XC + 1):
            total = None
            for tab, part in terms:
                if t < XC:
                    rows = get(t, part)[0:128]
                else:
                    rows = jnp.concatenate([get(x, part)[128:ROWS] for x in range(XC)], axis=0)
                term = dot(dtab[tab], rows, NTD)
                total = term if total is None else total + term
            sendx[p, :, t] = total[0:128].reshape(GX, 4, 128)
            sende[f, :, t] = total[128:136].reshape(EXTRA, 2, 128)

    def x_analyse(tiles, tables, out):
        left = tiles[XC]
        count = left.shape[0]
        per = 256 // count
        main, tail = None, None
        for b in range(XC // per):
            xs_here = range(b * per, (b + 1) * per)
            at = slice(b * 256, (b + 1) * 256)
            cols = split(jnp.concatenate([tiles[x] for x in xs_here], axis=0))
            term = dot3((tables[0, 0, :, at], tables[1, 0, :, at]), cols)
            main = term if main is None else main + term
            cols = split(jnp.concatenate(
                [left if x == 0 else pltpu.roll(left, 128 - 32 * x, 1) for x in xs_here], axis=0
            ))
            term = dot3((tables[0, 1, :, at], tables[1, 1, :, at]), cols)
            tail = term if tail is None else tail + term
        blocks = out.shape[:-2]
        size = tail.shape[0] // 4
        out[...] = main.reshape(blocks + (8, 128))
        tail = jnp.where(lane128 < 32, tail, 0.0)
        packed = tail[0:size]
        for g in range(1, 4):
            packed = packed + pltpu.roll(tail[size * g : size * g + size], 32 * g, 1)
        out[..., 6:8, :] = packed.reshape(blocks + (2, 128))

    def analyse_main(p, f):
        x_analyse([recvx[p, :, t].reshape(128, 128) for t in range(XC + 1)], xa, sendy.at[f])

    def analyse_extra(f):
        x_analyse(
            [recve[f, :, t].reshape(64, 128) for t in range(XC + 1)], xea, exy.at[f]
        )

    def y_cells(f):
        cols = split(jnp.concatenate([recvy[f, y].reshape(32, 128) for y in range(GY)], axis=1))
        merged = dot2(ut[...], cols)
        rows = []
        parts = [
            merged[16 * (g // GY) : 16 * (g // GY) + 16, 128 * (g % GY) : 128 * (g % GY) + 128]
            for g in range(16)
        ]
        rows += swap_groups(parts)
        parts = []
        for g in range(16):
            at = 32 + 16 * (g // GY)
            lanes = slice(128 * (g % GY), 128 * (g % GY) + 128)
            total = merged[at : at + 16, lanes]
            for n in range(1, 4):
                total = total + pltpu.roll(merged[at + 32 * n : at + 32 * n + 16, lanes], 128 - 32 * n, 1)
            parts.append(total)
        rows += swap_groups([jnp.where(lane128 < 32, part, 0.0) for part in parts])[: C - 16]
        return rows

    def y_synthesise(f, cols):
        main = swap_groups(cols[:16])
        tail = swap_groups(cols[16:] + [None] * (32 - C))
        stack = []
        for y in range(GY):
            rows = [main[y], main[GY + y]]
            for n in range(4):
                for g in (y, GY + y):
                    rows.append(tail[g] if n == 0 else pltpu.roll(tail[g], 32 * n, 1))
            stack.append(jnp.concatenate(rows, axis=0))
        out = dot2(u[...], split(jnp.concatenate(stack, axis=1)))
        for y in range(GY):
            backs[f, y] = out[:, 128 * y : 128 * y + 128].reshape(4, 8, 128)

    def x_synthesise(slots, tables, put):
        rows = slots[...]
        count = math.prod(rows.shape[:-2])
        main_cols = split(rows.reshape(count * 8, 128))
        tail = rows[..., 6:8, :].reshape(count * 2, 128)
        tail_cols = split(jnp.concatenate(
            [tail] + [pltpu.roll(tail, 128 - 32 * g, 1) for g in range(1, 4)], axis=0
        ))
        main = dot3((tables[0, 0], tables[1, 0]), main_cols)
        tail = dot3((tables[0, 1], tables[1, 1]), tail_cols)
        tail = jnp.where(lane128 < 32, tail, 0.0)
        per = main.shape[0] // XC
        left = None
        for x in range(XC):
            at = slice(per * x, per * x + per)
            put(x, main[at])
            part = tail[at]
            left = part if x == 0 else left + pltpu.roll(part, 32 * x, 1)
        put(XC, left)

    def synthesise_main(f, p):
        def put(t, rows):
            sendx[p, :, t] = rows.reshape(GX, 4, 128)

        x_synthesise(backr.at[f], xs, put)

    def synthesise_extra(f):
        def put(t, rows):
            sendr[f, :, t] = rows.reshape(GX, 2, 128)

        x_synthesise(backx.at[f], xes, put)

    def depth_rows(p, f, t):
        tile = recvx[p, :, t].reshape(128, 128)
        extra = recvr[f, :, t].reshape(8, 128)
        rest = jnp.zeros((120, 128), F32)
        low = jnp.concatenate([extra, rest], axis=0).T
        return jnp.concatenate([tile.T, low[:, 0:16]], axis=1)

    def depth_synthesise(p, f, x, left):
        cols = jnp.concatenate([depth_rows(p, f, x), left[32 * x : 32 * x + 32]], axis=0)
        return dot3(split(cols), (dtab[0], dtab[1])) * (1.0 / CELLS)

    def send_main_then_extra(p, f):
        @pl.when(special)
        def _():
            wait_e(f)
            analyse_extra(f)
            start_ex(f)

        wait_x(p)
        analyse_main(p, f)
        start_y(f)

    def cells_back(f, p):
        @pl.when(special)
        def _():
            wait_b_extra(f)
            synthesise_extra(f)
            start_r(f)

        wait_b(f)
        synthesise_main(f, p)
        start_x(p)

    loads[0].wait()
    for x in range(XC):
        vb[x] = hist[:, x].astype(F32).reshape(ROWS, 512).astype(BF16)
    loads[1].wait()
    depth_analyse(0, 0, lambda x, part: vb[x], ((0, 0), (1, 0)))

    pl.semaphore_wait(barrier, GX + GY - 2)
    start_e(0)
    start_x(0)

    for load in loads[2:]:
        load.wait()

    @pl.when(special)
    def _():
        for load in extra_loads:
            load.wait()

    wp[...] = jnp.zeros_like(wp)

    def pack(o):
        for r in range(2):
            for i in range(C):
                lanes = slice(32 * (i % 4), 32 * (i % 4) + MY)
                for k in range(KX):
                    wp[r, o, i // 4, 4 * k : 4 * k + 4, lanes] = w_v[r, o, i, k]

    over(C, pack)

    spread = (
        lax.broadcasted_iota(jnp.int32, (ROWS, C), 0) // YC
        == lax.broadcasted_iota(jnp.int32, (ROWS, C), 1)
    ).astype(F32)
    same_y = lax.rem(lax.broadcasted_iota(jnp.int32, (ROWS, ROWS), 0), YC) == lax.rem(
        lax.broadcasted_iota(jnp.int32, (ROWS, ROWS), 1), YC
    )
    wide = exact(exact(spread, wpt[...]), spread, NTD)
    point = split(jnp.where(same_y, wide, 0.0))
    wide_t = exact(exact(spread, wpt[...], ((1,), (1,))), spread, NTD)
    point_t = split(jnp.where(same_y, wide_t, 0.0))
    bias = jnp.sum(spread * off[...], axis=1, keepdims=True)
    for x in range(XC):
        base[x] = dot(point[0], vb[x], NN) + dot(point[1], vb[x], NN) + bias

    send_main_then_extra(0, 0)
    wait_y(0)
    cells = y_cells(0)
    cells = jnp.concatenate(
        [jnp.concatenate(cells[i : i + 4], axis=1) for i in range(0, C, 4)], axis=0
    )
    modes[...] = dot3(split(cells), (ya[0], ya[1]))

    def mix(o):
        real = jnp.zeros((16, 128), F32)
        imag = jnp.zeros((16, 128), F32)
        for i in range(C // 4):
            wr, wi = wp[0, o, i], wp[1, o, i]
            mr, mi = modes[16 * i : 16 * i + 16, 0:128], modes[16 * i : 16 * i + 16, 128:256]
            real += wr * mr - wi * mi
            imag += wr * mi + wi * mr
        at = pl.ds(pl.multiple_of(o * 16, 16), 16)
        mixed[at, 0:128] = real
        mixed[at, 128:256] = imag

    over(C, mix)
    cols = dot3(split(mixed[...]), (ysr[0], ysr[1]))
    y_synthesise(0, [cols[16 * c : 16 * c + 16] for c in range(C)])
    start_b(0)
    cells_back(0, 1)
    wait_x(1)
    wait_r(0)

    left = depth_rows(1, 0, XC)
    row_sum = jnp.zeros((ROWS, 1), F32)
    for x in range(XC):
        pre = depth_synthesise(1, 0, x, left) + base[x]
        inner = gelu_coef * (pre + gelu_cubic * pre * pre * pre)
        smooth = jnp.tanh(inner)
        slope = 0.5 * (1.0 + smooth) + 0.5 * pre * (1.0 - smooth * smooth) * gelu_coef * (
            1.0 + 3.0 * gelu_cubic * pre * pre
        )
        fields[0, :, x] = (0.5 * pre * (1.0 + smooth)).reshape(C, YC, 512).astype(BF16)
        grad = cot[:, x].astype(F32).reshape(ROWS, 512) * slope
        row_sum += jnp.sum(grad, axis=1, keepdims=True)
        hi, lo = split(grad)
        gpre[0, x] = hi
        gpre[1, x] = lo
    depth_analyse(2, 1, lambda x, part: gpre[part, x], ((0, 0), (0, 1), (1, 0)))
    start_e(1)
    start_x(2)
    wait_sent(0)
    wait_x_sent(0)
    wait_x_sent(1)

    cross = jnp.zeros((ROWS, ROWS), F32)
    for x in range(XC):
        g = (gpre[0, x], gpre[1, x])
        base[x] = dot3(point_t, g)
        cross += dot(g[0], vb[x], NTD) + dot(g[1], vb[x], NTD)
    row = lax.broadcasted_iota(jnp.int32, (40, ROWS), 0)
    gather = (
        lax.broadcasted_iota(jnp.int32, (40, ROWS), 1) // YC == 5 * lax.rem(row, 8) + row // 8
    ).astype(F32)
    place = (
        lax.broadcasted_iota(jnp.int32, (ROWS, 128), 0) // YC
        == lax.broadcasted_iota(jnp.int32, (ROWS, 128), 1)
    ).astype(F32)
    lane = lax.broadcasted_iota(jnp.int32, (ROWS, 128), 1)
    both = exact(jnp.where(same_y, cross, 0.0), place) + jnp.where(lane == C, row_sum, 0.0)
    parts = exact(gather, both)
    packed = parts[0:8]
    for m in range(1, 5):
        packed = packed + pltpu.roll(parts[8 * m : 8 * m + 8], 24 * m, 1)
    small[0] = packed

    def small_copy(s, k, peer, slot):
        return remote(small.at[s], smalls.at[s, slot], ss_sem.at[s, k], rs_sem.at[s, slot], *peer)

    xpos, zpos = d // ZPOS, lax.rem(d, ZPOS)
    steps = (
        (GY, e, lambda i: (d, i)),
        (XPOS, xpos, lambda i: (i * ZPOS + zpos, e)),
        (ZPOS, zpos, lambda i: (xpos * ZPOS + i, e)),
    )

    def start_small(s):
        count, me, peer_of = steps[s]
        for k in range(1, count):
            small_copy(s, k, peer_of(lax.rem(me + k, count)), me).start()
        smalls[s, me] = small[s]

    def finish_small(s):
        count, me, peer_of = steps[s]
        for k in range(1, count):
            other = lax.rem(me + count - k, count)
            copy = small_copy(s, k, peer_of(other), other)
            copy.wait_recv()
            copy.wait_send()
        total = smalls[s, 0]
        for k in range(1, count):
            total = total + smalls[s, k]
        return total

    start_small(0)
    send_main_then_extra(2, 1)
    small[1] = finish_small(0)
    start_small(1)
    wait_y(1)
    grads[...] = dot3(split(jnp.concatenate(y_cells(1), axis=0)), (yar[0], yar[1]))

    def mix_back(j):
        real = jnp.zeros((16, 128), F32)
        imag = jnp.zeros((16, 128), F32)
        for o in range(C):
            wr, wi = wp[0, o, j], wp[1, o, j]
            gr, gi = grads[16 * o : 16 * o + 16, 0:128], grads[16 * o : 16 * o + 16, 128:256]
            real += wr * gr + wi * gi
            imag += wr * gi - wi * gr
        at = pl.ds(pl.multiple_of(j * 16, 16), 16)
        mixed[at, 0:128] = real
        mixed[at, 128:256] = imag

    over(C // 4, mix_back)
    cols = dot3(split(mixed[0:80]), (ys[0], ys[1]))
    y_synthesise(1, [
        cols[16 * (c // 4) : 16 * (c // 4) + 16, 128 * (c % 4) : 128 * (c % 4) + 128] for c in range(C)
    ])
    start_b(1)
    small[2] = finish_small(1)
    start_small(2)
    cells_back(1, 3)

    total = finish_small(2)
    sums[400:408, 0:128] = total
    sums[400:408, 128:256] = jnp.zeros_like(total)

    wait_sent(1)
    wait_x_sent(2)
    wait_x(3)
    wait_r(1)
    left = depth_rows(3, 1, XC)
    for x in range(XC):
        total = depth_synthesise(3, 1, x, left) + base[x]
        fields[1, :, x] = total.reshape(C, YC, 512).astype(BF16)
    wait_x_sent(3)
    for f in range(2):
        wait_e_sent(f)
        wait_r_sent(f)


GROUPS = 5


def finish(fields, sums, act, ghist, gs, gpoint, goff, table, modes, gs_v, io_sem, gs_sem):
    grads = sums.at[80:400]
    copies = [
        pltpu.make_async_copy(fields.at[0], act, io_sem.at[0]),
        pltpu.make_async_copy(fields.at[1], ghist, io_sem.at[1]),
    ]
    for copy in copies:
        copy.start()
    for m in range(5):
        packed = sums[400:408, 0:128]
        packed = packed if m == 0 else pltpu.roll(packed, 128 - 24 * m, 1)
        for r in range(4):
            table[5 * r + m : 5 * r + m + 1, :] = packed[r : r + 1]
    gpoint[...] = table[0:C, 0:C]
    column = table[0:C, C : C + 1]
    diagonal = lax.broadcasted_iota(jnp.int32, (C, C), 0) == lax.broadcasted_iota(
        jnp.int32, (C, C), 1
    )
    goff[...] = jnp.sum(jnp.where(diagonal, column, 0.0), axis=0, keepdims=True)

    for j in range(C):
        for half in range(2):
            lanes = slice(128 * half, 128 * half + 128)
            tile = sums[16 * (j // 4) : 16 * (j // 4) + 16, lanes]
            modes[16 * j : 16 * j + 16, lanes] = tile if j % 4 == 0 else pltpu.roll(tile, 128 - 32 * (j % 4), 1)

    def row(o, carry):
        at = pl.ds(pl.multiple_of(o * 16, 16), 16)
        gr = grads[at, 0:128] * (1.0 / CELLS)
        gi = grads[at, 128:256] * (1.0 / CELLS)
        for j in range(C):
            mr, mi = modes[16 * j : 16 * j + 16, 0:128], modes[16 * j : 16 * j + 16, 128:256]
            real = gr * mr + gi * mi
            imag = gi * mr - gr * mi
            for k in range(KX):
                gs_v[0, o, j, k] = real[4 * k : 4 * k + 4, 0:MY]
                gs_v[1, o, j, k] = imag[4 * k : 4 * k + 4, 0:MY]
        return carry

    size = C // GROUPS
    for b in range(GROUPS):
        lax.fori_loop(b * size, (b + 1) * size, row, 0)
        for r in range(2):
            at = pl.ds(b * size, size)
            copy = pltpu.make_async_copy(gs_v.at[r, at], gs.at[r, at], gs_sem.at[r, b])
            copy.start()
            copies.append(copy)
    for copy in copies:
        copy.wait()


def per_device(history, w_point, offset, spectral_weight, cotangent):
    def two(table):
        return jnp.asarray(halves(table))

    xa, xs, xea, xes = x_tables()
    ya, yar = y_tables()
    slots = slot_table()
    weight = jnp.transpose(spectral_weight, (0, 1, 2, 4, 3, 5))
    vmem = pl.BlockSpec(memory_space=pltpu.VMEM)
    hbm = pl.BlockSpec(memory_space=pl.ANY)
    block = jax.ShapeDtypeStruct((C, XC, YC, NZ * NT), BF16)
    square = jax.ShapeDtypeStruct((C, C), F32)
    line = jax.ShapeDtypeStruct((1, C), F32)
    dma = pltpu.SemaphoreType.DMA
    fields, sums = pl.pallas_call(
        kernel,
        out_shape=(jax.ShapeDtypeStruct((2,) + block.shape, BF16), jax.ShapeDtypeStruct((408, 256), F32)),
        in_specs=[hbm] * 2 + [vmem] * 2 + [hbm] * 12,
        out_specs=(vmem,) * 2,
        scratch_shapes=[
            pltpu.VMEM(block.shape, BF16),
            pltpu.VMEM(block.shape, BF16),
            pltpu.VMEM((2, 144, 512), BF16),
            pltpu.VMEM((2, 2, 256, 512), BF16),
            pltpu.VMEM((2, 2, 512, 256), BF16),
            pltpu.VMEM((2, 2, 128, 256), BF16),
            pltpu.VMEM((2, 2, 256, 128), BF16),
            pltpu.VMEM((2, 512, 256), BF16),
            pltpu.VMEM((2, 128, 256), BF16),
            pltpu.VMEM((2, 256, 512), BF16),
            pltpu.VMEM((2, 256, 128), BF16),
            pltpu.VMEM((32, 160), BF16),
            pltpu.VMEM((160, 32), BF16),
            pltpu.VMEM((2, C, C, KX, Q, MY), F32),
            pltpu.VMEM((2, C, C // 4, 16, 128), F32),
            pltpu.VMEM((XC, ROWS, 512), BF16),
            pltpu.VMEM((XC, ROWS, 512), F32),
            pltpu.VMEM((2, XC, ROWS, 512), BF16),
            pltpu.VMEM((C * 16, 256), F32),
            pltpu.VMEM((4, GX, XC + 1, 4, 128), F32),
            pltpu.VMEM((4, GX, XC + 1, 4, 128), F32),
            pltpu.VMEM((2, EXTRA, XC + 1, 2, 128), F32),
            pltpu.VMEM((2, GX, XC + 1, 2, 128), F32),
            pltpu.VMEM((2, GX, XC + 1, 2, 128), F32),
            pltpu.VMEM((2, EXTRA, XC + 1, 2, 128), F32),
            pltpu.VMEM((2, GY, 2, 2, 8, 128), F32),
            pltpu.VMEM((2, GY, Q, 8, 128), F32),
            pltpu.VMEM((2, GY, Q, 8, 128), F32),
            pltpu.VMEM((2, 2, 2, GY, 8, 128), F32),
            pltpu.VMEM((2, GY, 2, 8, 128), F32),
            pltpu.VMEM((2, 2, GY, 8, 128), F32),
            pltpu.VMEM((3, 8, 128), F32),
            pltpu.VMEM((3, 8, 8, 128), F32),
            dma((14,)),
            dma((4, GX)),
            dma((4, GX)),
            dma((2, EXTRA)),
            dma((2, GX)),
            dma((2, GX)),
            dma((2, EXTRA)),
            dma((2, 6, GY)),
            dma((2, 4, GY)),
            dma((2, 4, GY)),
            dma((2, 6, GY)),
            dma((3, 8)),
            dma((3, 8)),
        ],
        compiler_params=pltpu.CompilerParams(
            collective_id=0, has_side_effects=True, vmem_limit_bytes=58 * 1024 * 1024
        ),
    )(
        history[0], cotangent[0], w_point, offset.reshape(1, C), weight,
        two(depth_table()), two(xa), two(xs), two(xea), two(xes), two(ya), two(yar), two(ya.T), two(yar.T),
        jnp.asarray(slots.astype(ml_dtypes.bfloat16)),
        jnp.asarray(slots.T.astype(ml_dtypes.bfloat16)),
    )
    act, ghist, gs, gpoint, goff = pl.pallas_call(
        finish,
        out_shape=(
            block, block, jax.ShapeDtypeStruct((2, C, C, KX, Q, MY), F32), square, line,
        ),
        in_specs=[vmem, vmem],
        out_specs=(hbm,) * 3 + (vmem,) * 2,
        scratch_shapes=[
            pltpu.VMEM((24, 128), F32), pltpu.VMEM((C * 16, 256), F32),
            pltpu.VMEM((2, C, C, KX, Q, MY), F32), dma((2,)), dma((2, GROUPS)),
        ],
        compiler_params=pltpu.CompilerParams(vmem_limit_bytes=60 * 1024 * 1024),
    )(fields, sums)
    grad_spectral = jnp.transpose(gs, (0, 1, 2, 4, 3, 5))
    return act[None], ghist[None], grad_spectral, gpoint, goff.reshape(C)


def solution(mesh):
    grid = P(None, None, "gx", "gy", None)
    modes = P(None, None, None, "gx", "gy", None)
    return jax.shard_map(
        per_device,
        mesh=mesh,
        in_specs=(grid, P(), P(), modes, grid),
        out_specs=(grid, grid, modes, P(), P()),
        check_vma=False,
    )
```
